256 devices in a mesh: row: 16 (over y, x_hi, core), col: 16 (over z, x_lo).
Axes of the slice: x: 4 (x_hi: 2, x_lo: 2; x = x_hi * 2 + x_lo), y: 4, z: 8, core: 2. Of those that a mesh axis runs over, the one named last changes fastest.
Arguments:
- pair: bfloat16 [1024, 4096, 128], P('row', 'col'), may hold values from -6 to 6
- single_q: bfloat16 [1024, 384], P('row'), may hold values from -6 to 6
- single_k: bfloat16 [4096, 384], P('col'), may hold values from -6 to 6
- w_query: bfloat16 [384, 192], replicated, may hold values from -0.3125 to 0.3125
- w_key: bfloat16 [384, 192], replicated, may hold values from -0.3125 to 0.3125
- w_value: bfloat16 [384, 192], replicated, may hold values from -0.3125 to 0.3125
- w_qpoint: bfloat16 [384, 288], replicated, may hold values from -0.3125 to 0.3125
- w_kpoint: bfloat16 [384, 288], replicated, may hold values from -0.3125 to 0.3125
- w_vpoint: bfloat16 [384, 288], replicated, may hold values from -0.3125 to 0.3125
- w_bias: bfloat16 [128, 12], replicated, may hold values from -0.5 to 0.5
- w_out: bfloat16 [2112, 384], replicated, may hold values from -0.125 to 0.125
- head_gamma: float32 [12], replicated, may hold values from 0.05 to 1
- chain_bias: float32 [12], replicated, may hold values from -1.5 to 1.5
- rot_q: float32 [9, 1024], P(None, 'row'), may hold values from -1 to 1, as said below
- trans_q: float32 [3, 1024], P(None, 'row'), may hold values from -6 to 26
- rot_k: float32 [9, 4096], P(None, 'col'), may hold values from -1 to 1, as said below
- trans_k: float32 [3, 4096], P(None, 'col'), may hold values from -6 to 6
- chain_q: int32 [1024], P('row'), may hold values from 0 to 4
- chain_k: int32 [4096], P('col'), may hold values from 0 to 4
- key_mask: int32 [4096], P('col'), may hold values 0 or 1
- cotangent: bfloat16 [1024, 384], P('row'), may hold values from -96 to 96
Outputs:
- pair_grad: bfloat16 [1024, 4096, 128], P('row', 'col')
- single_q_grad: bfloat16 [1024, 384], P('row')
- trans_q_grad: float32 [3, 1024], P(None, 'row')
- single_k_grad: bfloat16 [4096, 384], P('col')
- trans_k_grad: float32 [3, 4096], P(None, 'col')
The draws below stay inside these ranges and needn't reach their ends.
Inputs may be any that keep to these rules, and one draw needn't show every extreme that they name: `rot_q`: each column holds a rotation matrix. `rot_k`: each column holds a rotation matrix.
All inputs are finite; a program needn't handle non-finite values. No bound on the sum of `key_mask` on one device may be relied on, other than what follows from the above.
Results may differ from the reference program's by a relative error of at most 0.02.
The reference program's roundings to bfloat16 on the way (of `attn_b`, `d_cat` and `d_logit_b`) count: a program that leaves them out, or rounds other values in their place, can miss the bound.
Values sent between devices are 32-bit elements; how exact they have to be, the bound alone decides.
No kernel may reach another device: no remote copies, remote signals or barrier semaphores. Data moves between devices by JAX's collectives and lax.ppermute only.
A program may use at most 128 MiB of HBM per device.

```python
import math
import jax
import jax.numpy as jnp
from jax import lax

H = 12
C = 16
P_SIZE = 8
CS = 384
CZ = 128
QROW_DEV = 64
NQ = 1024
NK = 4096


def rotations(key, count):
    quat = jax.random.normal(key, (4, count), jnp.float32)
    quat = quat / jnp.sqrt(jnp.sum(quat * quat, axis=0) + 1e-06)
    real_part, first, second, third = (quat[0], quat[1], quat[2], quat[3])
    entries = [1.0 - 2.0 * (second * second + third * third), 2.0 * (first * second - real_part * third), 2.0 * (first * third + real_part * second), 2.0 * (first * second + real_part * third), 1.0 - 2.0 * (first * first + third * third), 2.0 * (second * third - real_part * first), 2.0 * (first * third - real_part * second), 2.0 * (second * third + real_part * first), 1.0 - 2.0 * (first * first + second * second)]
    return jnp.stack(entries)


def draw_rot_q(key, part):
    key = jax.random.fold_in(key, 21)
    return rotations(key, NQ)


def draw_rot_k(key, part):
    key = jax.random.fold_in(key, 22)
    return rotations(key, NK)


def draw_trans_q(key, part):
    key = jax.random.fold_in(key, 23)
    return jnp.clip(jax.random.normal(key, (3, NQ), jnp.float32), -6.0, 6.0)


def draw_trans_k(key, part):
    key = jax.random.fold_in(key, 25)
    return jnp.clip(jax.random.normal(key, (3, NK), jnp.float32), -6.0, 6.0)


def plant(drawn, stream_key, low, top_value):
    dims = drawn.shape
    place = [jax.random.randint(jax.random.fold_in(stream_key, axis), (), 0, dims[axis]) for axis in range(len(dims))]
    drawn = drawn.at[tuple(place)].set(low)
    longest = dims.index(max(dims))
    place[longest] = (place[longest] + 1) % dims[longest]
    return drawn.at[tuple(place)].set(top_value)


def steps_of(key, shape, split, smallest, top_value):
    factor_of, own = 1.0, jax.random.fold_in(key, 6)
    for position, parts in split:
        draws = jnp.exp(jax.random.uniform(jax.random.fold_in(own, position), (parts,), jnp.float32, smallest / len(split), top_value / len(split)))
        factor_of = factor_of * jnp.repeat(draws, shape[position] // parts).reshape([-1 if axis == position else 1 for axis in range(len(shape))])
    return factor_of


def centred(own_key, dims, deviation, reach, pieces=(), held_as=jnp.bfloat16):
    drawn = deviation * jax.random.normal(own_key, dims, jnp.float32)
    if pieces:
        drawn = drawn * steps_of(own_key, dims, pieces, -0.22, 0.18)
    return jnp.clip(drawn, -reach, reach).astype(held_as)


def setup_inputs(seed: int = 0) -> dict:
    key_list = jax.random.split(jax.random.key(seed), 22)
    return {
        "pair": centred(key_list[0], (NQ, NK, CZ), 1.0, 6.0, ((0, 16), (1, 16))),
        "single_q": centred(key_list[1], (NQ, CS), 1.0, 6.0, ((0, 16),)),
        "single_k": centred(key_list[2], (NK, CS), 1.0, 6.0, ((0, 16),)),
        "w_query": centred(key_list[3], (CS, H * C), CS ** -0.5, 0.3125),
        "w_key": centred(key_list[4], (CS, H * C), CS ** -0.5, 0.3125),
        "w_value": centred(key_list[5], (CS, H * C), CS ** -0.5, 0.3125),
        "w_qpoint": centred(key_list[6], (CS, 3 * H * P_SIZE), CS ** -0.5, 0.3125),
        "w_kpoint": centred(key_list[7], (CS, 3 * H * P_SIZE), CS ** -0.5, 0.3125),
        "w_vpoint": centred(key_list[8], (CS, 3 * H * P_SIZE), CS ** -0.5, 0.3125),
        "w_bias": centred(key_list[9], (CZ, H), CZ ** -0.5, 0.5),
        "w_out": centred(key_list[10], (H * C + H * CZ + 4 * H * P_SIZE, CS), (H * C + H * CZ + 4 * H * P_SIZE) ** -0.5, 0.125),
        "head_gamma": jnp.clip(jnp.exp(jax.random.uniform(key_list[11], (H,), jnp.float32, math.log(0.05), math.log(1.0))), 0.05, 1.0),
        "chain_bias": jnp.clip(jax.random.uniform(key_list[12], (H,), jnp.float32, -1.5, 1.5), -1.5, 1.5),
        "rot_q": draw_rot_q(jax.random.fold_in(key_list[21], 71), 0),
        "trans_q": draw_trans_q(jax.random.fold_in(key_list[21], 71), 0),
        "rot_k": draw_rot_k(jax.random.fold_in(key_list[21], 71), 0),
        "trans_k": draw_trans_k(jax.random.fold_in(key_list[21], 71), 0),
        "chain_q": plant(jax.random.randint(key_list[17], (NQ,), 0, 5), jax.random.fold_in(key_list[17], 1), 0, 4).astype(jnp.int32),
        "chain_k": plant(jax.random.randint(key_list[18], (NK,), 0, 5), jax.random.fold_in(key_list[18], 1), 0, 4).astype(jnp.int32),
        "key_mask": plant((jax.random.randint(key_list[19], (NK,), 0, 8) < 7).astype(jnp.int32), jax.random.fold_in(key_list[19], 1), 0, 1),
        "cotangent": centred(key_list[20], (NQ, CS), 16.0, 96.0, ((0, 16),)),
    }


HIGH = lax.Precision.HIGHEST

def points(single, weight, rotation, shift):
    count = single.shape[0]
    local = jnp.dot(single, weight, preferred_element_type=jnp.float32).reshape(count, 3, -1)
    rotm = rotation.reshape(3, 3, count)
    glob = jnp.einsum('abn,nbk->ank', rotm, local, precision=HIGH) + shift[:, :, None]
    return glob.reshape(3, count, H, P_SIZE)

def finish(pairs, pts, sums, coords, rotation, coef, wpoint):
    count = pts.shape[1]
    grad_pts = coef[None, None, :, None] * (pts - coords * sums.T[None, :, :, None])
    local = jnp.einsum('abn,anhp->nbhp', rotation.reshape(3, 3, count), grad_pts, precision=HIGH).reshape(count, -1)
    single = jnp.dot(local, wpoint.astype(jnp.float32).T, precision=HIGH)
    for grad, weight in pairs:
        single = single + jnp.dot(grad.reshape(count, -1), weight.astype(jnp.float32).T, precision=HIGH)
    return (single, lax.optimization_barrier(jnp.sum(grad_pts, axis=(2, 3))))

def value_part(vpts, rotation, wvpoint):
    count = vpts.shape[1]
    local = jnp.einsum('abn,anhp->nbhp', rotation.reshape(3, 3, count), vpts, precision=HIGH).reshape(count, -1)
    single = jnp.dot(local, wvpoint.astype(jnp.float32).T, precision=HIGH)
    return (single, lax.optimization_barrier(jnp.sum(vpts, axis=(2, 3))))

def point_back(opt, rotation, shift, d_ol, d_on):
    count = opt.shape[1]
    rotm = rotation.reshape(3, 3, count)
    oloc = jnp.einsum('abi,aihp->ibhp', rotm, opt - shift[:, :, None, None], precision=HIGH)
    onorm = jnp.sqrt(1.0 + lax.optimization_barrier(jnp.sum(oloc * oloc, axis=1)))
    d_loc = d_ol + (d_on / onorm)[:, None, :, :] * oloc
    return jnp.einsum('abi,ibhp->aihp', rotm, d_loc, precision=HIGH)

def reference(pair, single_q, single_k, w_query, w_key, w_value, w_qpoint, w_kpoint, w_vpoint, w_bias, w_out, head_gamma, chain_bias, rot_q, trans_q, rot_k, trans_k, chain_q, chain_k, key_mask, cotangent):
    w_logit = math.sqrt(1.0 / 3.0)
    w_point = math.sqrt(2.0 / (9.0 * P_SIZE))
    scale = w_logit / math.sqrt(C)
    query = jnp.dot(single_q, w_query, preferred_element_type=jnp.float32).astype(jnp.bfloat16).reshape(NQ, H, C).astype(jnp.float32)
    keyed = jnp.dot(single_k, w_key, preferred_element_type=jnp.float32).astype(jnp.bfloat16).reshape(NK, H, C).astype(jnp.float32)
    valued = jnp.dot(single_k, w_value, preferred_element_type=jnp.float32).astype(jnp.bfloat16).reshape(NK, H, C).astype(jnp.float32)
    gq = points(single_q, w_qpoint, rot_q, trans_q)
    gk = points(single_k, w_kpoint, rot_k, trans_k)
    gv = points(single_k, w_vpoint, rot_k, trans_k)
    coef = w_logit * w_point * head_gamma
    sq_k = lax.optimization_barrier(jnp.sum(gk * gk, axis=(0, 3)))
    d_cat = jnp.dot(cotangent, w_out.T, preferred_element_type=jnp.float32).astype(jnp.bfloat16).astype(jnp.float32)
    first = H * C + H * CZ
    d_os = d_cat[:, :H * C].reshape(NQ, H, C)
    d_oz = d_cat[:, H * C:first].reshape(NQ, H, CZ)
    d_ol = d_cat[:, first:first + 3 * H * P_SIZE].reshape(NQ, 3, H, P_SIZE)
    d_on = d_cat[:, first + 3 * H * P_SIZE:].reshape(NQ, H, P_SIZE)
    valid = (key_mask == 1)[None, None, :]
    bias_w = w_bias.astype(jnp.float32)

    def block(carry, inputs):
        acc_dk, acc_dv, acc_pts, acc_sums, acc_vpts = carry
        pair_b, query_b, gq_b, dos_b, doz_b, chain_b, dol_b, don_b, rot_b, shift_b = inputs
        pair_f = pair_b.astype(jnp.float32)
        sq_q = lax.optimization_barrier(jnp.sum(gq_b * gq_b, axis=(0, 3)))
        cross = jnp.einsum('cihp,cjhp->hij', gq_b, gk, precision=HIGH)
        dist = sq_q.T[:, :, None] + sq_k.T[:, None, :] - 2.0 * cross
        same = (chain_b[:, None] == chain_k[None, :]).astype(jnp.float32)
        logit = w_logit * (jnp.einsum('ihc,jhc->hij', query_b, keyed) / math.sqrt(C) + jnp.einsum('ijz,zh->hij', pair_f, bias_w) + chain_bias[:, None, None] * same[None]) - 0.5 * coef[:, None, None] * dist
        masked = jnp.where(valid, logit, -1e+30)
        top = lax.optimization_barrier(jnp.max(masked, axis=2, keepdims=True))
        expo = jnp.where(valid, jnp.exp(masked - top), 0.0)
        attn = expo / lax.optimization_barrier(jnp.sum(expo, axis=2, keepdims=True))
        attn_b = attn.astype(jnp.bfloat16).astype(jnp.float32)
        opt = jnp.einsum('hij,ajhp->aihp', attn_b, gv, precision=HIGH)
        d_glob = point_back(opt, rot_b, shift_b, dol_b, don_b)
        d_attn = jnp.einsum('ihc,jhc->hij', dos_b, valued) + jnp.einsum('ihz,ijz->hij', doz_b, pair_f) + jnp.einsum('aihp,ajhp->hij', d_glob, gv, precision=HIGH)
        delta = lax.optimization_barrier(jnp.sum(attn_b * d_attn, axis=2, keepdims=True))
        d_logit = attn * (d_attn - delta)
        d_logit_b = d_logit.astype(jnp.bfloat16).astype(jnp.float32)
        grad_pair = (w_logit * jnp.einsum('hij,zh->ijz', d_logit_b, bias_w) + jnp.einsum('hij,ihz->ijz', attn_b, doz_b)).astype(jnp.bfloat16)
        dq_b = scale * jnp.einsum('hij,jhc->ihc', d_logit_b, keyed)
        q_pts = jnp.einsum('hij,cjhp->cihp', d_logit, gk, precision=HIGH)
        q_sums = lax.optimization_barrier(jnp.sum(d_logit, axis=2))
        q_back = lax.optimization_barrier(jnp.sum(d_glob, axis=(2, 3)))
        acc_dk = acc_dk + scale * jnp.einsum('hij,ihc->jhc', d_logit_b, query_b)
        acc_dv = acc_dv + jnp.einsum('hij,ihc->jhc', attn_b, dos_b)
        acc_pts = acc_pts + jnp.einsum('hij,cihp->cjhp', d_logit, gq_b, precision=HIGH)
        acc_sums = acc_sums + lax.optimization_barrier(jnp.sum(d_logit, axis=1))
        acc_vpts = acc_vpts + jnp.einsum('hij,aihp->ajhp', attn, d_glob, precision=HIGH)
        return ((acc_dk, acc_dv, acc_pts, acc_sums, acc_vpts), (grad_pair, dq_b, q_pts, q_sums, q_back))
    blocks = NQ // QROW_DEV
    inputs = (pair.reshape(blocks, QROW_DEV, NK, CZ), query.reshape(blocks, QROW_DEV, H, C), jnp.moveaxis(gq.reshape(3, blocks, QROW_DEV, H, P_SIZE), 1, 0), d_os.reshape(blocks, QROW_DEV, H, C), d_oz.reshape(blocks, QROW_DEV, H, CZ), chain_q.reshape(blocks, QROW_DEV), d_ol.reshape(blocks, QROW_DEV, 3, H, P_SIZE), d_on.reshape(blocks, QROW_DEV, H, P_SIZE), jnp.moveaxis(rot_q.reshape(9, blocks, QROW_DEV), 1, 0), jnp.moveaxis(trans_q.reshape(3, blocks, QROW_DEV), 1, 0))
    start = (jnp.zeros((NK, H, C), jnp.float32), jnp.zeros((NK, H, C), jnp.float32), jnp.zeros((3, NK, H, P_SIZE), jnp.float32), jnp.zeros((H, NK), jnp.float32), jnp.zeros((3, NK, H, P_SIZE), jnp.float32))
    carry, outs = lax.scan(block, start, inputs)
    acc_dk, acc_dv, acc_pts, acc_sums, acc_vpts = carry
    grad_pair, dq_all, q_pts, q_sums, q_back = outs
    pair_grad = grad_pair.reshape(NQ, NK, CZ)
    dq_all = dq_all.reshape(NQ, H, C)
    q_pts = jnp.moveaxis(q_pts, 0, 1).reshape(3, NQ, H, P_SIZE)
    q_sums = jnp.moveaxis(q_sums, 0, 1).reshape(H, NQ)
    q_back = jnp.moveaxis(q_back, 0, 1).reshape(3, NQ)
    grad_q, shift_q = finish([(dq_all, w_query)], q_pts, q_sums, gq, rot_q, coef, w_qpoint)
    shift_q = shift_q - q_back
    grad_k, shift_k = finish([(acc_dk, w_key), (acc_dv, w_value)], acc_pts, acc_sums, gk, rot_k, coef, w_kpoint)
    more_k, more_shift = value_part(acc_vpts, rot_k, w_vpoint)
    grad_k = grad_k + more_k
    shift_k = shift_k + more_shift
    return (pair_grad, grad_q.astype(jnp.bfloat16), shift_q, grad_k.astype(jnp.bfloat16), shift_k)
```

```python
import functools
import math

import jax
import jax.numpy as jnp
from jax import lax
from jax.experimental import pallas as pl
from jax.experimental.pallas import tpu as pltpu
from jax.sharding import PartitionSpec as P

HIGH = lax.Precision.HIGHEST
F32 = jnp.float32
BF = jnp.bfloat16
HP = 16
LANE = 128
NEG = -1e30
LIMIT = 56 * 1024 * 1024


def nn(a, b, precision=None):
    return lax.dot_general(
        a, b, (((1,), (0,)), ((), ())), preferred_element_type=F32, precision=precision
    )


def nt(a, b, precision=None):
    return lax.dot_general(
        a, b, (((1,), (1,)), ((), ())), preferred_element_type=F32, precision=precision
    )


def tn(a, b, precision=None):
    return lax.dot_general(
        a, b, (((0,), (0,)), ((), ())), preferred_element_type=F32, precision=precision
    )


def split(x):
    hi = x.astype(BF)
    return hi, (x - hi.astype(F32)).astype(BF)


def iota(shape, axis):
    return lax.broadcasted_iota(jnp.int32, shape, axis)


def head_mask(heads, npoint, width):
    lane = iota((HP, width), 1) % LANE
    row = iota((HP, width), 0)
    return (lane // npoint == row) & (lane < heads * npoint)


def channel_mask(heads, channels):
    lane = iota((HP, heads * channels), 1)
    return lane // channels == iota((HP, heads * channels), 0)


def spread(x, mask):
    n, w = x.shape
    wide = jnp.broadcast_to(x[:, None, :], (n, HP, w))
    return jnp.where(mask[None], wide, jnp.zeros((), x.dtype)).reshape(n * HP, w)


def gather_heads(x, mask):
    w = x.shape[1]
    full = jnp.where(mask[None], x.reshape(-1, HP, w), 0.0)
    return jnp.sum(full, axis=1)


def to_lanes(col, offset=0):
    n = col.shape[0] // HP
    mask = iota((HP, LANE), 1) == iota((HP, LANE), 0) + offset
    wide = jnp.broadcast_to(col, (n * HP, LANE)).reshape(n, HP, LANE)
    return jnp.sum(jnp.where(mask[None], wide, 0.0), axis=1)


def to_col(x, offset=0):
    n = x.shape[0]
    mask = iota((HP, LANE), 1) == iota((HP, LANE), 0) + offset
    wide = jnp.broadcast_to(x[:, None, :], (n, HP, LANE))
    return jnp.sum(jnp.where(mask[None], wide, 0.0), axis=2, keepdims=True).reshape(n * HP, 1)


def pad_lanes(x, width=LANE):
    n, w = x.shape
    return jnp.concatenate([x, jnp.zeros((n, width - w), x.dtype)], axis=1)


def rotate_points(local, cols, hp):
    parts = [local[:, b * hp : (b + 1) * hp] for b in range(3)]
    out = []
    for a in range(3):
        g = cols[:, 9 + a : 10 + a]
        g = g + sum(cols[:, 3 * a + b : 3 * a + b + 1] * parts[b] for b in range(3))
        out.append(pad_lanes(g))
    return jnp.concatenate(out, axis=1)


def back_rotate(x, cols):
    parts = [x[:, a * LANE : (a + 1) * LANE] for a in range(3)]
    return [sum(cols[:, 3 * a + b : 3 * a + b + 1] * parts[a] for a in range(3)) for b in range(3)]


def logits_kernel(
    heads,
    channels,
    npoint,
    pair_hbm,
    sq_ref,
    sk_ref,
    wq_ref,
    wk_ref,
    wv_ref,
    wqp_ref,
    wkp_ref,
    wvp_ref,
    wb_ref,
    wout_ref,
    gamma_ref,
    chainb_ref,
    rotq_ref,
    trq_ref,
    rotk_ref,
    trk_ref,
    cq_ref,
    ck_ref,
    km_ref,
    cot_ref,
    masked_ref,
    base_ref,
    stats_ref,
    query_ref,
    key_ref,
    value_ref,
    gq_ref,
    gk_ref,
    gv_ref,
    dos_ref,
    dpt_ref,
    rhs_ref,
    qcol_ref,
    kcol_ref,
    pair_ref,
    lhs_ref,
    tq_ref,
    tk_ref,
    sems,
):
    rows, keys, depth = pair_hbm.shape
    hp = heads * npoint
    nchunk = sems.shape[0]
    step = rows // nchunk
    copies = [
        pltpu.make_async_copy(
            pair_hbm.at[pl.ds(c * step, step)], pair_ref.at[pl.ds(c * step, step)], sems.at[c]
        )
        for c in range(nchunk)
    ]
    for copy in copies:
        copy.start()

    w_logit = math.sqrt(1.0 / 3.0)
    w_point = math.sqrt(2.0 / (9.0 * npoint))
    tq_ref[...] = jnp.zeros_like(tq_ref)
    tq_ref[0:9, 0:rows] = rotq_ref[...]
    tq_ref[9:12, 0:rows] = trq_ref[...]
    tq_ref[12:13, 0:rows] = cq_ref[...].astype(F32)
    tq_ref[13:14, 0:heads] = gamma_ref[...]
    tq_ref[14:15, 0:heads] = chainb_ref[...]
    qcols_all = tq_ref[...].T
    qcols = qcols_all[:rows]
    head_cols = qcols_all[:HP]
    qcol_ref[...] = qcols_all
    tk_ref[...] = jnp.zeros_like(tk_ref)
    tk_ref[0:9, :] = rotk_ref[...]
    tk_ref[9:12, :] = trk_ref[...]
    kcols = tk_ref[...].T
    kcol_ref[...] = kcols

    sq = sq_ref[...]
    sk = sk_ref[...]
    cot = cot_ref[...]
    query = nt(sq, wq_ref[...]).astype(BF)
    key = nt(sk, wk_ref[...]).astype(BF)
    query_ref[...] = query
    key_ref[...] = key
    value_ref[...] = nt(sk, wv_ref[...]).astype(BF)
    gq = rotate_points(nt(sq, wqp_ref[...]), qcols, hp)
    gk = rotate_points(nt(sk, wkp_ref[...]), kcols, hp)
    gq_ref[...] = gq
    gk_ref[...] = gk
    gv_ref[...] = rotate_points(nt(sk, wvp_ref[...]), kcols, hp)

    nos = heads * channels
    first = nos + heads * depth
    dos_ref[...] = nt(cot, wout_ref[0:nos, :]).astype(BF)
    for b in range(4):
        d = nt(cot, wout_ref[first + b * hp : first + (b + 1) * hp, :]).astype(BF).astype(F32)
        dpt_ref[:, b * LANE : (b + 1) * LANE] = pad_lanes(d)
    doz = nt(cot, wout_ref[nos:first, :]).astype(BF).astype(F32)
    wbt = jnp.concatenate(
        [wb_ref[...].astype(F32), jnp.zeros((HP - heads, depth), F32)], axis=0
    )
    wb_wide = jnp.broadcast_to(wbt[None], (rows, HP, depth))
    lhs_ref[...] = jnp.zeros_like(lhs_ref)
    for h in range(heads):
        lhs_ref[pl.ds(HP + h, rows, stride=2 * HP), :] = doz[:, h * depth : (h + 1) * depth]
    lhs3 = lhs_ref[...].reshape(rows, 2 * HP, depth)
    doz_b = lhs3[:, HP:, :]
    whi, wlo = split(w_logit * wb_wide)
    rhs_ref[:, 0:HP, :] = whi
    rhs_ref[:, HP : 2 * HP, :] = wlo
    rhs_ref[:, 2 * HP : 3 * HP, :] = doz_b.astype(BF)
    lhs_ref[...] = jnp.concatenate([wb_wide, doz_b], axis=1).reshape(rows * 2 * HP, depth)

    for c in range(nchunk):
        copies[c].wait()

        def one(i, carry):
            r = pl.multiple_of(i * 2 * HP, 2 * HP)
            g = nt(lhs_ref[pl.ds(r, 2 * HP), :].astype(BF), pair_ref[i])
            r = pl.multiple_of(i * HP, HP)
            masked_ref[pl.ds(r, HP), :] = g[:HP]
            base_ref[pl.ds(r, HP), :] = g[HP:]
            return carry

        lax.fori_loop(c * step, (c + 1) * step, one, 0, unroll=8)

    pmask = head_mask(heads, npoint, 3 * LANE)
    cmask = channel_mask(heads, channels)
    gqm = spread(gq, pmask)
    cross = nt(gqm, gk, HIGH)
    sqq = jnp.sum(gqm * gqm, axis=1, keepdims=True)
    sqk = nt(pmask.astype(F32), gk * gk, HIGH)
    qk = nt(spread(query.astype(F32), cmask).astype(BF), key)
    coef = (w_logit * w_point) * head_cols[:, 13:14]
    same = (qcols[:, 12:13] == ck_ref[...].astype(F32)).astype(F32)
    shape = (rows, HP, keys)
    dist = (sqq.reshape(rows, HP, 1) + sqk[None]) - 2.0 * cross.reshape(shape)
    inner = (
        qk.reshape(shape) * (1.0 / math.sqrt(channels))
        + masked_ref[...].reshape(shape)
        + head_cols[:, 14:15][None] * jnp.broadcast_to(same[:, None, :], shape)
    )
    logit = w_logit * inner - (0.5 * coef)[None] * dist
    valid = (km_ref[...] == 1)[None]
    masked = jnp.where(valid, logit, NEG)
    top = jnp.max(masked, axis=2, keepdims=True)
    total = jnp.sum(jnp.where(valid, jnp.exp(masked - top), 0.0), axis=2, keepdims=True)
    masked_ref[...] = masked.reshape(rows * HP, keys)
    packed = to_lanes(top.reshape(rows * HP, 1)) + to_lanes(total.reshape(rows * HP, 1), HP)
    stats_ref[...] = packed.T[: 2 * HP]
    dosm = spread(dos_ref[...].astype(F32), cmask).astype(BF)
    base_ref[...] += nt(dosm, value_ref[...])


def attend_kernel(heads, npoint, masked_ref, base_ref, km_ref, stats_ref, gv_ref, attn_ref, out_ref):
    rows = stats_ref.shape[1]
    keys = masked_ref.shape[1]
    stats = jnp.concatenate(
        [stats_ref[...], jnp.zeros((LANE - stats_ref.shape[0], rows), F32)], axis=0
    ).T
    top = to_col(stats)
    total = to_col(stats, HP)
    valid = km_ref[...] == 1
    attn = jnp.where(valid, jnp.exp(masked_ref[...] - top), 0.0) / total
    attn_ref[...] = attn
    attn_b = attn.astype(BF)
    attn_f = attn_b.astype(F32)
    ghi, glo = split(gv_ref[...])
    opt = nn(attn_b, ghi) + nn(attn_b, glo)
    pmask = head_mask(heads, npoint, 3 * LANE)
    delta = jnp.sum(attn_f * base_ref[...], axis=1, keepdims=True)
    out_ref[...] = gather_heads(opt, pmask)
    out_ref[:, 0:LANE] += to_lanes(delta, heads * npoint)


def frames_of(heads, npoint, qcol_ref, rows):
    pmask = head_mask(heads, npoint, 3 * LANE)
    qall = qcol_ref[...]
    w_logit = math.sqrt(1.0 / 3.0)
    w_point = math.sqrt(2.0 / (9.0 * npoint))
    coef = (w_logit * w_point) * qall[:HP, 13:14]
    coef_lane = jnp.sum(jnp.where(pmask, coef, 0.0), axis=0, keepdims=True)
    return pmask, qall[:rows], coef_lane


def project(parts, width):
    single = jnp.zeros((parts[0][0].shape[0], width), F32)
    for part, weight in parts:
        phi, plo = split(part)
        single = single + (nn(phi, weight) + nn(plo, weight))
    return single


def component_sums(x):
    n = x.shape[0]
    cols = [jnp.sum(x[:, a * LANE : (a + 1) * LANE], axis=1, keepdims=True) for a in range(3)]
    return jnp.concatenate(cols + [jnp.zeros((n, LANE - 3), F32)], axis=1).T


def query_kernel(
    heads,
    channels,
    npoint,
    place_ref,
    attn_ref,
    base_ref,
    psum0_ref,
    psum1_ref,
    psum2_ref,
    psum3_ref,
    key_ref,
    gq_ref,
    gk_ref,
    gv_ref,
    dpt_ref,
    qcol_ref,
    wq_ref,
    wqp_ref,
    qout_ref,
    both_ref,
    dlo_ref,
    alo_ref,
    dglob_ref,
):
    rows, keys = gq_ref.shape[0], gk_ref.shape[0]
    hp = heads * npoint
    scale = math.sqrt(1.0 / 3.0) / math.sqrt(channels)
    cmask = channel_mask(heads, channels)
    pmask, qcols, coef_lane = frames_of(heads, npoint, qcol_ref, rows)
    inside = iota((1, LANE), 1) < hp

    psum = (psum0_ref[...] + psum1_ref[...]) + (psum2_ref[...] + psum3_ref[...])
    delta0 = to_col(psum[:, :LANE], hp)
    opt = [jnp.where(inside, psum[:, a * LANE : (a + 1) * LANE], 0.0) for a in range(3)]
    moved = [jnp.where(inside, opt[a] - qcols[:, 9 + a : 10 + a], 0.0) for a in range(3)]
    oloc = back_rotate(jnp.concatenate(moved, axis=1), qcols)
    onorm = jnp.sqrt(1.0 + (oloc[0] * oloc[0] + oloc[1] * oloc[1] + oloc[2] * oloc[2]))
    ratio = dpt_ref[:, 3 * LANE : 4 * LANE] / onorm
    dloc = [dpt_ref[:, b * LANE : (b + 1) * LANE] + ratio * oloc[b] for b in range(3)]
    dglob = jnp.concatenate(
        [
            sum(qcols[:, 3 * a + b : 3 * a + b + 1] * dloc[b] for b in range(3))
            for a in range(3)
        ],
        axis=1,
    )
    dglob_ref[...] = dglob
    dghi, dglo = split(spread(dglob, pmask))
    opt_row = jnp.concatenate(opt, axis=1)
    delta = delta0 + jnp.sum(spread(opt_row * dglob, pmask), axis=1, keepdims=True)
    gvhi, gvlo = split(gv_ref[...])
    dattn = base_ref[...] + nt(dghi, gvhi) + (nt(dghi, gvlo) + nt(dglo, gvhi))
    attn = attn_ref[...]
    dlogit = attn * (dattn - delta)
    dhi, dlo = split(dlogit)
    ahi, alo = split(attn)
    both_ref[:, 0:HP, :] = dhi.reshape(rows, HP, keys)
    both_ref[:, HP : 2 * HP, :] = ahi.reshape(rows, HP, keys)
    dlo_ref[...] = dlo
    alo_ref[...] = alo

    gkhi, gklo = split(gk_ref[...])
    dq = scale * gather_heads(nn(dhi, key_ref[...]), cmask)
    qpts = gather_heads(nn(dhi, gkhi) + (nn(dhi, gklo) + nn(dlo, gkhi)), pmask)
    qsum = jnp.sum(dlogit, axis=1, keepdims=True)
    qsum_lane = gather_heads(jnp.broadcast_to(qsum, (rows * HP, 3 * LANE)), pmask)
    dgq = coef_lane * (qpts - gq_ref[...] * qsum_lane)
    mq = back_rotate(dgq, qcols)
    width = qout_ref.shape[1]
    qout_ref[0:rows, :] = project(
        [(dq, wq_ref[...])]
        + [(mq[b][:, :hp], wqp_ref[b * hp : (b + 1) * hp, :]) for b in range(3)],
        width,
    )
    shift = jnp.where(place_ref[0] == 0, dgq - dglob, dgq)
    qout_ref[rows:, :] = jnp.zeros((qout_ref.shape[0] - rows, width), F32)
    qout_ref[rows : rows + 8, 0:rows] = component_sums(shift)[:8, :rows]


def key_kernel(
    heads,
    channels,
    npoint,
    place_ref,
    both_ref,
    dlo_ref,
    alo_ref,
    dglob_ref,
    query_ref,
    gq_ref,
    gk_ref,
    dos_ref,
    qcol_ref,
    kcol_ref,
    wk_ref,
    wv_ref,
    wkp_ref,
    wvp_ref,
    mine_ref,
    other_ref,
):
    rows, keys = gq_ref.shape[0], gk_ref.shape[0]
    hp = heads * npoint
    scale = math.sqrt(1.0 / 3.0) / math.sqrt(channels)
    cmask = channel_mask(heads, channels)
    pmask, qcols, coef_lane = frames_of(heads, npoint, qcol_ref, rows)
    kcols = kcol_ref[...]
    dhi = both_ref[:, 0:HP, :].reshape(rows * HP, keys)
    ahi = both_ref[:, HP : 2 * HP, :].reshape(rows * HP, keys)
    dlo, alo = dlo_ref[...], alo_ref[...]
    dghi, dglo = split(spread(dglob_ref[...], pmask))
    gqhi, gqlo = split(spread(gq_ref[...], pmask))
    ones = jnp.broadcast_to(pmask[None], (rows, HP, 3 * LANE)).astype(F32).reshape(
        rows * HP, 3 * LANE
    )
    ones = ones.astype(BF)
    qm = spread(query_ref[...].astype(F32), cmask).astype(BF)
    dosm = spread(dos_ref[...].astype(F32), cmask).astype(BF)
    dk = scale * tn(dhi, qm)
    dv = tn(ahi, dosm)
    kpts = tn(dhi, gqhi) + (tn(dhi, gqlo) + tn(dlo, gqhi))
    ksum = tn(dhi, ones) + tn(dlo, ones)
    vpts = tn(ahi, dghi) + (tn(ahi, dglo) + tn(alo, dghi))
    dgk = coef_lane * (kpts - gk_ref[...] * ksum)
    mk = back_rotate(dgk, kcols)
    mv = back_rotate(vpts, kcols)
    width = mine_ref.shape[1]
    single = project(
        [(dk, wk_ref[...]), (dv, wv_ref[...])]
        + [(mk[b][:, :hp], wkp_ref[b * hp : (b + 1) * hp, :]) for b in range(3)]
        + [(mv[b][:, :hp], wvp_ref[b * hp : (b + 1) * hp, :]) for b in range(3)],
        width,
    )
    cols = component_sums(dgk + vpts)
    piece = keys // 8
    core, quarter = place_ref[1], place_ref[2]

    def put(ref, half):
        for n in range(4):
            k = half * 4 + n
            r = pl.multiple_of((n ^ quarter) * (piece + 8), 8)
            ref[pl.ds(r, piece), :] = single[k * piece : (k + 1) * piece]
            r = pl.multiple_of((n ^ quarter) * (piece + 8) + piece, 8)
            ref[pl.ds(r, 8), :] = jnp.concatenate(
                [cols[:8, k * piece : (k + 1) * piece], jnp.zeros((8, width - piece), F32)], axis=1
            )

    @pl.when(core == 0)
    def _():
        put(mine_ref, 0)
        put(other_ref, 1)

    @pl.when(core != 0)
    def _():
        put(mine_ref, 1)
        put(other_ref, 0)


def finish_kernel(
    place_ref,
    q0_ref,
    q1_ref,
    q2_ref,
    q3_ref,
    mine_ref,
    other_ref,
    gradq_ref,
    shiftq_ref,
    gradk_ref,
    shiftk_ref,
    shift_ref,
):
    rows = gradq_ref.shape[0]
    keys = gradk_ref.shape[0]
    piece = keys // 8
    total = (q0_ref[...] + q1_ref[...]) + (q2_ref[...] + q3_ref[...])
    gradq_ref[...] = total[:rows].astype(BF)
    shiftq_ref[...] = total[rows : rows + 3, :rows]
    core, quarter = place_ref[1], place_ref[2]

    def put(ref, half):
        parts = []
        for n in range(4):
            k = half * 4 + n
            r = pl.multiple_of((n ^ quarter) * (piece + 8), 8)
            gradk_ref[k * piece : (k + 1) * piece, :] = ref[pl.ds(r, piece), :].astype(BF)
            r = pl.multiple_of((n ^ quarter) * (piece + 8) + piece, 8)
            parts.append(ref[pl.ds(r, 8), 0:piece])
        shift_ref[:, half * 4 * piece : (half + 1) * 4 * piece] = jnp.concatenate(parts, axis=1)

    @pl.when(core == 0)
    def _():
        put(mine_ref, 0)
        put(other_ref, 1)

    @pl.when(core != 0)
    def _():
        put(mine_ref, 1)
        put(other_ref, 0)

    shiftk_ref[...] = shift_ref[0:3, :]


def pair_kernel(both_ref, rhs_ref, out_ref):
    rows = both_ref.shape[0]

    def one(i, carry):
        both = both_ref[i]
        left = jnp.concatenate([both[:HP], both[:HP], both[HP:]], axis=0)
        out_ref[i] = tn(left, rhs_ref[i]).astype(BF)
        return carry

    lax.fori_loop(0, rows, one, 0, unroll=True)


def permuted(x, axis, flip):
    size = lax.axis_size(axis)
    return lax.ppermute(x, axis, [(i, i ^ flip) for i in range(size)])


def around(x, hops):
    size = lax.axis_size("col")
    ring = size // 2
    sign = -1 if hops == 2 else 1
    moves = []
    for i in range(size):
        z, low = i // 2, i % 2
        source = (z + (hops if z % 2 else -hops) * sign) % ring
        moves.append((source * 2 + low, i))
    return lax.ppermute(x, "col", moves)


def merged(parts):
    top = functools.reduce(jnp.maximum, [p[:HP] for p in parts])
    total = sum(p[HP:] * jnp.exp(p[:HP] - top) for p in parts)
    return jnp.concatenate([top, total], axis=0)


def body(
    pair,
    single_q,
    single_k,
    w_query,
    w_key,
    w_value,
    w_qpoint,
    w_kpoint,
    w_vpoint,
    w_bias,
    w_out,
    head_gamma,
    chain_bias,
    rot_q,
    trans_q,
    rot_k,
    trans_k,
    chain_q,
    chain_k,
    key_mask,
    cotangent,
):
    rows, keys, depth = pair.shape
    heads = w_bias.shape[1]
    channels = w_query.shape[1] // heads
    npoint = w_qpoint.shape[1] // (3 * heads)
    chans = single_q.shape[1]
    hc = heads * channels
    n = rows * HP
    sds = jax.ShapeDtypeStruct
    params = pltpu.CompilerParams(vmem_limit_bytes=LIMIT)
    vmem = pl.BlockSpec(memory_space=pltpu.VMEM)
    wide = 3 * LANE
    km = key_mask.reshape(1, keys)
    w_query, w_key, w_value = w_query.T, w_key.T, w_value.T
    w_qpoint, w_kpoint, w_vpoint = w_qpoint.T, w_kpoint.T, w_vpoint.T
    w_bias = w_bias.T
    (
        masked,
        base,
        stats,
        query,
        key,
        value,
        gq,
        gk,
        gv,
        d_os,
        d_pt,
        rhs,
        qcol,
        kcol,
    ) = pl.pallas_call(
        functools.partial(logits_kernel, heads, channels, npoint),
        out_shape=[
            sds((n, keys), F32),
            sds((n, keys), F32),
            sds((2 * HP, rows), F32),
            sds((rows, hc), BF),
            sds((keys, hc), BF),
            sds((keys, hc), BF),
            sds((rows, wide), F32),
            sds((keys, wide), F32),
            sds((keys, wide), F32),
            sds((rows, hc), BF),
            sds((rows, 4 * LANE), F32),
            sds((rows, 3 * HP, depth), BF),
            sds((LANE, LANE), F32),
            sds((keys, LANE), F32),
        ],
        in_specs=[pl.BlockSpec(memory_space=pl.ANY)] + [vmem] * 20,
        out_specs=[vmem] * 14,
        scratch_shapes=[
            pltpu.VMEM((rows, keys, depth), BF),
            pltpu.VMEM((rows * 2 * HP, depth), F32),
            pltpu.VMEM((LANE, LANE), F32),
            pltpu.VMEM((LANE, keys), F32),
            pltpu.SemaphoreType.DMA((4,)),
        ],
        compiler_params=params,
        name="logits",
    )(
        pair,
        single_q,
        single_k,
        w_query,
        w_key,
        w_value,
        w_qpoint,
        w_kpoint,
        w_vpoint,
        w_bias,
        w_out,
        head_gamma.reshape(1, heads),
        chain_bias.reshape(1, heads),
        rot_q,
        trans_q,
        rot_k,
        trans_k,
        chain_q.reshape(1, rows),
        chain_k.reshape(1, keys),
        km,
        cotangent,
    )

    parts = [stats] + [permuted(stats, "col", f) for f in (1, 2, 3)]
    stats = merged(parts)
    stats = merged([stats] + [around(stats, f) for f in (3, 2, 1)])

    attn, points = pl.pallas_call(
        functools.partial(attend_kernel, heads, npoint),
        out_shape=[sds((n, keys), F32), sds((rows, wide), F32)],
        in_specs=[vmem] * 5,
        out_specs=[vmem] * 2,
        compiler_params=params,
        name="attend",
    )(masked, base, km, stats, gv)
    points = points + sum(permuted(points, "col", f) for f in (1, 2, 3))
    parts = [points] + [around(points, f) for f in (3, 2, 1)]

    me = lax.axis_index("row")
    place = jnp.stack([lax.axis_index("col"), me % 2, me // 4]).astype(jnp.int32)
    smem = pl.BlockSpec(memory_space=pltpu.SMEM)
    qpart, both, dlo, alo, dglob = pl.pallas_call(
        functools.partial(query_kernel, heads, channels, npoint),
        out_shape=[
            sds((rows + 8, chans), F32),
            sds((rows, 2 * HP, keys), BF),
            sds((n, keys), BF),
            sds((n, keys), BF),
            sds((rows, wide), F32),
        ],
        in_specs=[smem] + [vmem] * 14,
        out_specs=[vmem] * 5,
        compiler_params=params,
        name="query_grads",
    )(place, attn, base, *parts, key, gq, gk, gv, d_pt, qcol, w_query, w_qpoint)

    first = [qpart] + [permuted(qpart, "col", f) for f in (1, 2, 3)]
    half = sds((keys // 2 + 32, chans), F32)
    mine, other = pl.pallas_call(
        functools.partial(key_kernel, heads, channels, npoint),
        out_shape=[half, half],
        in_specs=[smem] + [vmem] * 14,
        out_specs=[vmem] * 2,
        compiler_params=params,
        name="key_grads",
        cost_estimate=pl.CostEstimate(
            flops=2 * n * keys * 12 * wide, bytes_accessed=4 * n * keys, transcendentals=0
        ),
    )(
        place,
        both,
        dlo,
        alo,
        dglob,
        query,
        gq,
        gk,
        d_os,
        qcol,
        kcol,
        w_key,
        w_value,
        w_kpoint,
        w_vpoint,
    )
    first[0], mine, other = lax.optimization_barrier((first[0], mine, other))

    mine = mine + permuted(other, "row", 1)
    mine = mine.reshape(4, -1, chans)
    held = mine[0] + sum(permuted(mine[f], "row", 4 * f) for f in (1, 2, 3))

    pair_grad = pl.pallas_call(
        pair_kernel,
        out_shape=sds((rows, keys, depth), BF),
        in_specs=[vmem] * 2,
        out_specs=vmem,
        compiler_params=params,
        name="pair_grad",
        cost_estimate=pl.CostEstimate(
            flops=2 * rows * keys * depth * 3 * HP,
            bytes_accessed=2 * rows * keys * depth,
            transcendentals=0,
        ),
    )(both, rhs)
    held, pair_grad = lax.optimization_barrier((held, pair_grad))
    qpart = (first[0] + first[1]) + (first[2] + first[3])
    second = [qpart] + [around(qpart, f) for f in (3, 2, 1)]
    held = held + permuted(held, "row", 2)
    mine = jnp.concatenate([held] + [permuted(held, "row", 4 * f) for f in (1, 2, 3)], axis=0)
    other = permuted(mine, "row", 1)
    grad_q, shift_q, grad_k, shift_k = pl.pallas_call(
        finish_kernel,
        out_shape=[
            sds((rows, chans), BF),
            sds((3, rows), F32),
            sds((keys, chans), BF),
            sds((3, keys), F32),
        ],
        in_specs=[smem] + [vmem] * 6,
        out_specs=[vmem] * 4,
        scratch_shapes=[pltpu.VMEM((8, keys), F32)],
        compiler_params=params,
        name="finish",
    )(place, *second, mine, other)
    return pair_grad, grad_q, shift_q, grad_k, shift_k


def solution(mesh):
    placed = (
        P("row", "col", None),
        P("row", None),
        P("col", None),
        P(),
        P(),
        P(),
        P(),
        P(),
        P(),
        P(),
        P(),
        P(),
        P(),
        P(None, "row"),
        P(None, "row"),
        P(None, "col"),
        P(None, "col"),
        P("row"),
        P("col"),
        P("col"),
        P("row", None),
    )
    return jax.shard_map(
        body,
        mesh=mesh,
        in_specs=placed,
        out_specs=(
            P("row", "col", None),
            P("row", None),
            P(None, "row"),
            P("col", None),
            P(None, "col"),
        ),
        check_vma=False,
    )
```

```python
import functools
import math

import jax
import jax.numpy as jnp
from jax import lax
from jax.experimental import pallas as pl
from jax.experimental.pallas import tpu as pltpu
from jax.sharding import PartitionSpec as P

HIGH = lax.Precision.HIGHEST
F32 = jnp.float32
BF = jnp.bfloat16
HP = 16
LANE = 128
NEG = -1e30
LIMIT = 56 * 1024 * 1024


def nn(a, b, precision=None):
    return lax.dot_general(
        a, b, (((1,), (0,)), ((), ())), preferred_element_type=F32, precision=precision
    )


def nt(a, b, precision=None):
    return lax.dot_general(
        a, b, (((1,), (1,)), ((), ())), preferred_element_type=F32, precision=precision
    )


def tn(a, b, precision=None):
    return lax.dot_general(
        a, b, (((0,), (0,)), ((), ())), preferred_element_type=F32, precision=precision
    )


def split(x):
    hi = x.astype(BF)
    return hi, (x - hi.astype(F32)).astype(BF)


def iota(shape, axis):
    return lax.broadcasted_iota(jnp.int32, shape, axis)


def head_mask(heads, npoint, width):
    lane = iota((HP, width), 1) % LANE
    row = iota((HP, width), 0)
    return (lane // npoint == row) & (lane < heads * npoint)


def channel_mask(heads, channels):
    lane = iota((HP, heads * channels), 1)
    return lane // channels == iota((HP, heads * channels), 0)


def spread(x, mask):
    n, w = x.shape
    wide = jnp.broadcast_to(x[:, None, :], (n, HP, w))
    return jnp.where(mask[None], wide, jnp.zeros((), x.dtype)).reshape(n * HP, w)


def gather_heads(x, mask):
    w = x.shape[1]
    full = jnp.where(mask[None], x.reshape(-1, HP, w), 0.0)
    return jnp.sum(full, axis=1)


def to_lanes(col, offset=0):
    n = col.shape[0] // HP
    mask = iota((HP, LANE), 1) == iota((HP, LANE), 0) + offset
    wide = jnp.broadcast_to(col, (n * HP, LANE)).reshape(n, HP, LANE)
    return jnp.sum(jnp.where(mask[None], wide, 0.0), axis=1)


def to_col(x, offset=0):
    n = x.shape[0]
    mask = iota((HP, LANE), 1) == iota((HP, LANE), 0) + offset
    wide = jnp.broadcast_to(x[:, None, :], (n, HP, LANE))
    return jnp.sum(jnp.where(mask[None], wide, 0.0), axis=2, keepdims=True).reshape(n * HP, 1)


def pad_lanes(x, width=LANE):
    n, w = x.shape
    return jnp.concatenate([x, jnp.zeros((n, width - w), x.dtype)], axis=1)


def rotate_points(local, cols, hp):
    parts = [local[:, b * hp : (b + 1) * hp] for b in range(3)]
    out = []
    for a in range(3):
        g = cols[:, 9 + a : 10 + a]
        g = g + sum(cols[:, 3 * a + b : 3 * a + b + 1] * parts[b] for b in range(3))
        out.append(pad_lanes(g))
    return jnp.concatenate(out, axis=1)


def back_rotate(x, cols):
    parts = [x[:, a * LANE : (a + 1) * LANE] for a in range(3)]
    return [sum(cols[:, 3 * a + b : 3 * a + b + 1] * parts[a] for a in range(3)) for b in range(3)]


def logits_kernel(
    heads,
    channels,
    npoint,
    pair_hbm,
    sq_ref,
    sk_ref,
    wq_ref,
    wk_ref,
    wv_ref,
    wqp_ref,
    wkp_ref,
    wvp_ref,
    wb_ref,
    wout_ref,
    gamma_ref,
    chainb_ref,
    rotq_ref,
    trq_ref,
    rotk_ref,
    trk_ref,
    cq_ref,
    ck_ref,
    km_ref,
    cot_ref,
    masked_ref,
    base_ref,
    sums_ref,
    query_ref,
    key_ref,
    value_ref,
    gq_ref,
    gk_ref,
    gv_ref,
    dos_ref,
    dpt_ref,
    rhs_ref,
    qcol_ref,
    kcol_ref,
    pair_ref,
    lhs_ref,
    tq_ref,
    tk_ref,
    sems,
):
    rows, keys, depth = pair_hbm.shape
    hp = heads * npoint
    nchunk = sems.shape[0]
    step = rows // nchunk
    copies = [
        pltpu.make_async_copy(
            pair_hbm.at[pl.ds(c * step, step)], pair_ref.at[pl.ds(c * step, step)], sems.at[c]
        )
        for c in range(nchunk)
    ]
    for copy in copies:
        copy.start()

    w_logit = math.sqrt(1.0 / 3.0)
    w_point = math.sqrt(2.0 / (9.0 * npoint))
    tq_ref[...] = jnp.zeros_like(tq_ref)
    tq_ref[0:9, 0:rows] = rotq_ref[...]
    tq_ref[9:12, 0:rows] = trq_ref[...]
    tq_ref[12:13, 0:rows] = cq_ref[...].astype(F32)
    tq_ref[13:14, 0:heads] = gamma_ref[...]
    tq_ref[14:15, 0:heads] = chainb_ref[...]
    qcols_all = tq_ref[...].T
    qcols = qcols_all[:rows]
    head_cols = qcols_all[:HP]
    qcol_ref[...] = qcols_all
    tk_ref[...] = jnp.zeros_like(tk_ref)
    tk_ref[0:9, :] = rotk_ref[...]
    tk_ref[9:12, :] = trk_ref[...]
    kcols = tk_ref[...].T
    kcol_ref[...] = kcols

    sq = sq_ref[...]
    sk = sk_ref[...]
    cot = cot_ref[...]
    query = nt(sq, wq_ref[...]).astype(BF)
    key = nt(sk, wk_ref[...]).astype(BF)
    query_ref[...] = query
    key_ref[...] = key
    value_ref[...] = nt(sk, wv_ref[...]).astype(BF)
    gq = rotate_points(nt(sq, wqp_ref[...]), qcols, hp)
    gk = rotate_points(nt(sk, wkp_ref[...]), kcols, hp)
    gq_ref[...] = gq
    gk_ref[...] = gk
    gv_ref[...] = rotate_points(nt(sk, wvp_ref[...]), kcols, hp)

    nos = heads * channels
    first = nos + heads * depth
    dos_ref[...] = nt(cot, wout_ref[0:nos, :]).astype(BF)
    for b in range(4):
        d = nt(cot, wout_ref[first + b * hp : first + (b + 1) * hp, :]).astype(BF).astype(F32)
        dpt_ref[:, b * LANE : (b + 1) * LANE] = pad_lanes(d)
    doz = nt(cot, wout_ref[nos:first, :]).astype(BF).astype(F32)
    wbt = jnp.concatenate(
        [wb_ref[...].astype(F32), jnp.zeros((HP - heads, depth), F32)], axis=0
    )
    wb_wide = jnp.broadcast_to(wbt[None], (rows, HP, depth))
    lhs_ref[...] = jnp.zeros_like(lhs_ref)
    for h in range(heads):
        lhs_ref[pl.ds(HP + h, rows, stride=2 * HP), :] = doz[:, h * depth : (h + 1) * depth]
    lhs3 = lhs_ref[...].reshape(rows, 2 * HP, depth)
    doz_b = lhs3[:, HP:, :]
    whi, wlo = split(w_logit * wb_wide)
    rhs_ref[:, 0:HP, :] = whi
    rhs_ref[:, HP : 2 * HP, :] = wlo
    rhs_ref[:, 2 * HP : 3 * HP, :] = doz_b.astype(BF)
    lhs_ref[...] = jnp.concatenate([wb_wide, doz_b], axis=1).reshape(rows * 2 * HP, depth)

    for c in range(nchunk):
        copies[c].wait()

        def one(i, carry):
            r = pl.multiple_of(i * 2 * HP, 2 * HP)
            g = nt(lhs_ref[pl.ds(r, 2 * HP), :].astype(BF), pair_ref[i])
            r = pl.multiple_of(i * HP, HP)
            masked_ref[pl.ds(r, HP), :] = g[:HP]
            base_ref[pl.ds(r, HP), :] = g[HP:]
            return carry

        lax.fori_loop(c * step, (c + 1) * step, one, 0, unroll=8)

    pmask = head_mask(heads, npoint, 3 * LANE)
    cmask = channel_mask(heads, channels)
    gqm = spread(gq, pmask)
    cross = nt(gqm, gk, HIGH)
    sqq = jnp.sum(gqm * gqm, axis=1, keepdims=True)
    sqk = nt(pmask.astype(F32), gk * gk, HIGH)
    qk = nt(spread(query.astype(F32), cmask).astype(BF), key)
    coef = (w_logit * w_point) * head_cols[:, 13:14]
    same = (qcols[:, 12:13] == ck_ref[...].astype(F32)).astype(F32)
    shape = (rows, HP, keys)
    dist = (sqq.reshape(rows, HP, 1) + sqk[None]) - 2.0 * cross.reshape(shape)
    inner = (
        qk.reshape(shape) * (1.0 / math.sqrt(channels))
        + masked_ref[...].reshape(shape)
        + head_cols[:, 14:15][None] * jnp.broadcast_to(same[:, None, :], shape)
    )
    logit = w_logit * inner - (0.5 * coef)[None] * dist
    valid = (km_ref[...] == 1)[None]
    masked = jnp.where(valid, logit, NEG)
    top = jnp.max(masked, axis=2, keepdims=True)
    expo = jnp.where(valid, jnp.exp(masked - top), 0.0)
    total = jnp.sum(expo, axis=2, keepdims=True).reshape(rows * HP, 1)
    expo = expo.reshape(rows * HP, keys)
    masked_ref[...] = expo
    dosm = spread(dos_ref[...].astype(F32), cmask).astype(BF)
    base = base_ref[...] + nt(dosm, value_ref[...])
    base_ref[...] = base
    ehi, elo = split(expo)
    ghi, glo = split(gv_ref[...])
    points = nn(ehi, ghi) + (nn(ehi, glo) + nn(elo, ghi))
    sums_ref[...] = gather_heads(points, pmask)
    sums_ref[:, 0:LANE] += to_lanes(jnp.sum(expo * base, axis=1, keepdims=True), hp)
    sums_ref[:, LANE : 2 * LANE] += to_lanes(top.reshape(rows * HP, 1), hp)
    sums_ref[:, 2 * LANE : 3 * LANE] += to_lanes(total, hp)


def stat_lanes(heads, npoint):
    lane = iota((1, LANE), 1) - heads * npoint
    return (lane >= 0) & (lane < heads)


def over_lanes(x, heads, npoint):
    hp = heads * npoint
    row = iota((LANE, 3 * LANE), 0)
    full = iota((LANE, 3 * LANE), 1)
    lane = full % LANE
    hit = ((lane < hp) & (lane // npoint == row - hp)) | ((lane == row) & (full // LANE != 1))
    hit = hit & (row >= hp) & (row < hp + heads)
    x = jnp.where(stat_lanes(heads, npoint), x, 0.0)
    return nn(x, hit.astype(F32), HIGH)


def combined(parts, heads, npoint):
    tops = [p[:, LANE : 2 * LANE] for p in parts]
    top = functools.reduce(jnp.maximum, tops)
    total = sum(
        p * over_lanes(jnp.exp(t - top), heads, npoint) for p, t in zip(parts, tops)
    )
    top = jnp.where(stat_lanes(heads, npoint), top, 0.0)
    zero = jnp.zeros_like(top)
    return total + jnp.concatenate([zero, top, zero], axis=1)


def combine_kernel(heads, npoint, p0_ref, p1_ref, p2_ref, p3_ref, out_ref):
    out_ref[...] = combined(
        [p0_ref[...], p1_ref[...], p2_ref[...], p3_ref[...]], heads, npoint
    )


def frames_of(heads, npoint, qcol_ref, rows):
    pmask = head_mask(heads, npoint, 3 * LANE)
    qall = qcol_ref[...]
    w_logit = math.sqrt(1.0 / 3.0)
    w_point = math.sqrt(2.0 / (9.0 * npoint))
    coef = (w_logit * w_point) * qall[:HP, 13:14]
    coef_lane = jnp.sum(jnp.where(pmask, coef, 0.0), axis=0, keepdims=True)
    return pmask, qall[:rows], coef_lane


def project(parts, width):
    single = jnp.zeros((parts[0][0].shape[0], width), F32)
    for part, weight in parts:
        phi, plo = split(part)
        single = single + (nn(phi, weight) + nn(plo, weight))
    return single


def component_sums(x):
    n = x.shape[0]
    cols = [jnp.sum(x[:, a * LANE : (a + 1) * LANE], axis=1, keepdims=True) for a in range(3)]
    return jnp.concatenate(cols + [jnp.zeros((n, LANE - 3), F32)], axis=1).T


def query_kernel(
    heads,
    channels,
    npoint,
    place_ref,
    expo_ref,
    base_ref,
    own_ref,
    psum0_ref,
    psum1_ref,
    psum2_ref,
    psum3_ref,
    key_ref,
    gq_ref,
    gk_ref,
    gv_ref,
    dpt_ref,
    qcol_ref,
    wq_ref,
    wqp_ref,
    qout_ref,
    both_ref,
    dlo_ref,
    alo_ref,
    dglob_ref,
):
    rows, keys = gq_ref.shape[0], gk_ref.shape[0]
    hp = heads * npoint
    scale = math.sqrt(1.0 / 3.0) / math.sqrt(channels)
    cmask = channel_mask(heads, channels)
    pmask, qcols, coef_lane = frames_of(heads, npoint, qcol_ref, rows)
    inside = iota((1, LANE), 1) < hp

    psum = combined(
        [psum0_ref[...], psum1_ref[...], psum2_ref[...], psum3_ref[...]], heads, npoint
    )
    stat = stat_lanes(heads, npoint)
    inv = jnp.where(stat, 1.0 / psum[:, 2 * LANE :], 0.0)
    own = jnp.where(stat, own_ref[:, LANE : 2 * LANE] - psum[:, LANE : 2 * LANE], 0.0)
    attn = expo_ref[...] * to_col(jnp.exp(own) * inv, hp)
    psum = psum * over_lanes(inv, heads, npoint)
    delta0 = to_col(psum[:, :LANE], hp)
    opt = [jnp.where(inside, psum[:, a * LANE : (a + 1) * LANE], 0.0) for a in range(3)]
    moved = [jnp.where(inside, opt[a] - qcols[:, 9 + a : 10 + a], 0.0) for a in range(3)]
    oloc = back_rotate(jnp.concatenate(moved, axis=1), qcols)
    onorm = jnp.sqrt(1.0 + (oloc[0] * oloc[0] + oloc[1] * oloc[1] + oloc[2] * oloc[2]))
    ratio = dpt_ref[:, 3 * LANE : 4 * LANE] / onorm
    dloc = [dpt_ref[:, b * LANE : (b + 1) * LANE] + ratio * oloc[b] for b in range(3)]
    dglob = jnp.concatenate(
        [
            sum(qcols[:, 3 * a + b : 3 * a + b + 1] * dloc[b] for b in range(3))
            for a in range(3)
        ],
        axis=1,
    )
    dglob_ref[...] = dglob
    dghi, dglo = split(spread(dglob, pmask))
    opt_row = jnp.concatenate(opt, axis=1)
    delta = delta0 + jnp.sum(spread(opt_row * dglob, pmask), axis=1, keepdims=True)
    gvhi, gvlo = split(gv_ref[...])
    dattn = base_ref[...] + nt(dghi, gvhi) + (nt(dghi, gvlo) + nt(dglo, gvhi))
    dlogit = attn * (dattn - delta)
    dhi, dlo = split(dlogit)
    ahi, alo = split(attn)
    both_ref[:, 0:HP, :] = dhi.reshape(rows, HP, keys)
    both_ref[:, HP : 2 * HP, :] = ahi.reshape(rows, HP, keys)
    dlo_ref[...] = dlo
    alo_ref[...] = alo

    gkhi, gklo = split(gk_ref[...])
    dq = scale * gather_heads(nn(dhi, key_ref[...]), cmask)
    qpts = gather_heads(nn(dhi, gkhi) + (nn(dhi, gklo) + nn(dlo, gkhi)), pmask)
    qsum = jnp.sum(dlogit + (attn - ahi.astype(F32)) * dattn, axis=1, keepdims=True)
    qsum_lane = gather_heads(jnp.broadcast_to(qsum, (rows * HP, 3 * LANE)), pmask)
    dgq = coef_lane * (qpts - gq_ref[...] * qsum_lane)
    mq = back_rotate(dgq, qcols)
    width = qout_ref.shape[1]
    qout_ref[0:rows, :] = project(
        [(dq, wq_ref[...])]
        + [(mq[b][:, :hp], wqp_ref[b * hp : (b + 1) * hp, :]) for b in range(3)],
        width,
    )
    shift = jnp.where(place_ref[0] == 0, dgq - dglob, dgq)
    qout_ref[rows:, :] = jnp.zeros((qout_ref.shape[0] - rows, width), F32)
    qout_ref[rows : rows + 8, 0:rows] = component_sums(shift)[:8, :rows]


def key_kernel(
    heads,
    channels,
    npoint,
    place_ref,
    both_ref,
    dlo_ref,
    alo_ref,
    dglob_ref,
    query_ref,
    gq_ref,
    gk_ref,
    dos_ref,
    qcol_ref,
    kcol_ref,
    wk_ref,
    wv_ref,
    wkp_ref,
    wvp_ref,
    mine_ref,
    other_ref,
):
    rows, keys = gq_ref.shape[0], gk_ref.shape[0]
    hp = heads * npoint
    scale = math.sqrt(1.0 / 3.0) / math.sqrt(channels)
    cmask = channel_mask(heads, channels)
    pmask, qcols, coef_lane = frames_of(heads, npoint, qcol_ref, rows)
    kcols = kcol_ref[...]
    dhi = both_ref[:, 0:HP, :].reshape(rows * HP, keys)
    ahi = both_ref[:, HP : 2 * HP, :].reshape(rows * HP, keys)
    dlo, alo = dlo_ref[...], alo_ref[...]
    dghi, dglo = split(spread(dglob_ref[...], pmask))
    gqhi, gqlo = split(spread(gq_ref[...], pmask))
    ones = jnp.broadcast_to(pmask[None], (rows, HP, 3 * LANE)).astype(F32).reshape(
        rows * HP, 3 * LANE
    )
    ones = ones.astype(BF)
    qm = spread(query_ref[...].astype(F32), cmask).astype(BF)
    dosm = spread(dos_ref[...].astype(F32), cmask).astype(BF)
    dk = scale * tn(dhi, qm)
    dv = tn(ahi, dosm)
    kpts = tn(dhi, gqhi) + (tn(dhi, gqlo) + tn(dlo, gqhi))
    ksum = tn(dhi, ones) + tn(dlo, ones)
    vpts = tn(ahi, dghi) + (tn(ahi, dglo) + tn(alo, dghi))
    dgk = coef_lane * (kpts - gk_ref[...] * ksum)
    mk = back_rotate(dgk, kcols)
    mv = back_rotate(vpts, kcols)
    width = mine_ref.shape[1]
    single = project(
        [(dk, wk_ref[...]), (dv, wv_ref[...])]
        + [(mk[b][:, :hp], wkp_ref[b * hp : (b + 1) * hp, :]) for b in range(3)]
        + [(mv[b][:, :hp], wvp_ref[b * hp : (b + 1) * hp, :]) for b in range(3)],
        width,
    )
    cols = component_sums(dgk + vpts)
    piece = keys // 8
    core, quarter = place_ref[1], place_ref[2]

    def put(ref, half):
        for n in range(4):
            k = half * 4 + n
            r = pl.multiple_of((n ^ quarter) * (piece + 8), 8)
            ref[pl.ds(r, piece), :] = single[k * piece : (k + 1) * piece]
            r = pl.multiple_of((n ^ quarter) * (piece + 8) + piece, 8)
            ref[pl.ds(r, 8), :] = jnp.concatenate(
                [cols[:8, k * piece : (k + 1) * piece], jnp.zeros((8, width - piece), F32)], axis=1
            )

    @pl.when(core == 0)
    def _():
        put(mine_ref, 0)
        put(other_ref, 1)

    @pl.when(core != 0)
    def _():
        put(mine_ref, 1)
        put(other_ref, 0)


def finish_kernel(
    place_ref,
    q0_ref,
    q1_ref,
    q2_ref,
    q3_ref,
    mine_ref,
    other_ref,
    gradq_ref,
    shiftq_ref,
    gradk_ref,
    shiftk_ref,
    shift_ref,
):
    rows = gradq_ref.shape[0]
    keys = gradk_ref.shape[0]
    piece = keys // 8
    total = (q0_ref[...] + q1_ref[...]) + (q2_ref[...] + q3_ref[...])
    gradq_ref[...] = total[:rows].astype(BF)
    shiftq_ref[...] = total[rows : rows + 3, :rows]
    core, quarter = place_ref[1], place_ref[2]

    def put(ref, half):
        parts = []
        for n in range(4):
            k = half * 4 + n
            r = pl.multiple_of((n ^ quarter) * (piece + 8), 8)
            gradk_ref[k * piece : (k + 1) * piece, :] = ref[pl.ds(r, piece), :].astype(BF)
            r = pl.multiple_of((n ^ quarter) * (piece + 8) + piece, 8)
            parts.append(ref[pl.ds(r, 8), 0:piece])
        shift_ref[:, half * 4 * piece : (half + 1) * 4 * piece] = jnp.concatenate(parts, axis=1)

    @pl.when(core == 0)
    def _():
        put(mine_ref, 0)
        put(other_ref, 1)

    @pl.when(core != 0)
    def _():
        put(mine_ref, 1)
        put(other_ref, 0)

    shiftk_ref[...] = shift_ref[0:3, :]


def pair_kernel(both_ref, rhs_ref, out_ref):
    rows = both_ref.shape[0]

    def one(i, carry):
        both = both_ref[i]
        left = jnp.concatenate([both[:HP], both[:HP], both[HP:]], axis=0)
        out_ref[i] = tn(left, rhs_ref[i]).astype(BF)
        return carry

    lax.fori_loop(0, rows, one, 0, unroll=True)


def permuted(x, axis, flip):
    size = lax.axis_size(axis)
    return lax.ppermute(x, axis, [(i, i ^ flip) for i in range(size)])


def around(x, hops):
    size = lax.axis_size("col")
    ring = size // 2
    sign = -1 if hops == 2 else 1
    moves = []
    for i in range(size):
        z, low = i // 2, i % 2
        source = (z + (hops if z % 2 else -hops) * sign) % ring
        moves.append((source * 2 + low, i))
    return lax.ppermute(x, "col", moves)


def body(
    pair,
    single_q,
    single_k,
    w_query,
    w_key,
    w_value,
    w_qpoint,
    w_kpoint,
    w_vpoint,
    w_bias,
    w_out,
    head_gamma,
    chain_bias,
    rot_q,
    trans_q,
    rot_k,
    trans_k,
    chain_q,
    chain_k,
    key_mask,
    cotangent,
):
    rows, keys, depth = pair.shape
    heads = w_bias.shape[1]
    channels = w_query.shape[1] // heads
    npoint = w_qpoint.shape[1] // (3 * heads)
    chans = single_q.shape[1]
    hc = heads * channels
    n = rows * HP
    sds = jax.ShapeDtypeStruct
    params = pltpu.CompilerParams(vmem_limit_bytes=LIMIT)
    vmem = pl.BlockSpec(memory_space=pltpu.VMEM)
    wide = 3 * LANE
    km = key_mask.reshape(1, keys)
    w_query, w_key, w_value = w_query.T, w_key.T, w_value.T
    w_qpoint, w_kpoint, w_vpoint = w_qpoint.T, w_kpoint.T, w_vpoint.T
    w_bias = w_bias.T
    (
        expo,
        base,
        sums,
        query,
        key,
        value,
        gq,
        gk,
        gv,
        d_os,
        d_pt,
        rhs,
        qcol,
        kcol,
    ) = pl.pallas_call(
        functools.partial(logits_kernel, heads, channels, npoint),
        out_shape=[
            sds((n, keys), F32),
            sds((n, keys), F32),
            sds((rows, wide), F32),
            sds((rows, hc), BF),
            sds((keys, hc), BF),
            sds((keys, hc), BF),
            sds((rows, wide), F32),
            sds((keys, wide), F32),
            sds((keys, wide), F32),
            sds((rows, hc), BF),
            sds((rows, 4 * LANE), F32),
            sds((rows, 3 * HP, depth), BF),
            sds((LANE, LANE), F32),
            sds((keys, LANE), F32),
        ],
        in_specs=[pl.BlockSpec(memory_space=pl.ANY)] + [vmem] * 20,
        out_specs=[vmem] * 14,
        scratch_shapes=[
            pltpu.VMEM((rows, keys, depth), BF),
            pltpu.VMEM((rows * 2 * HP, depth), F32),
            pltpu.VMEM((LANE, LANE), F32),
            pltpu.VMEM((LANE, keys), F32),
            pltpu.SemaphoreType.DMA((4,)),
        ],
        compiler_params=params,
        name="logits",
    )(
        pair,
        single_q,
        single_k,
        w_query,
        w_key,
        w_value,
        w_qpoint,
        w_kpoint,
        w_vpoint,
        w_bias,
        w_out,
        head_gamma.reshape(1, heads),
        chain_bias.reshape(1, heads),
        rot_q,
        trans_q,
        rot_k,
        trans_k,
        chain_q.reshape(1, rows),
        chain_k.reshape(1, keys),
        km,
        cotangent,
    )

    parts = [sums] + [permuted(sums, "col", f) for f in (1, 2, 3)]
    merged = pl.pallas_call(
        functools.partial(combine_kernel, heads, npoint),
        out_shape=sds((rows, wide), F32),
        in_specs=[vmem] * 4,
        out_specs=vmem,
        compiler_params=params,
        name="combine",
    )(*parts)
    parts = [merged] + [around(merged, f) for f in (3, 2, 1)]

    me = lax.axis_index("row")
    place = jnp.stack([lax.axis_index("col"), me % 2, me // 4]).astype(jnp.int32)
    smem = pl.BlockSpec(memory_space=pltpu.SMEM)
    qpart, both, dlo, alo, dglob = pl.pallas_call(
        functools.partial(query_kernel, heads, channels, npoint),
        out_shape=[
            sds((rows + 8, chans), F32),
            sds((rows, 2 * HP, keys), BF),
            sds((n, keys), BF),
            sds((n, keys), BF),
            sds((rows, wide), F32),
        ],
        in_specs=[smem] + [vmem] * 15,
        out_specs=[vmem] * 5,
        compiler_params=params,
        name="query_grads",
    )(place, expo, base, sums, *parts, key, gq, gk, gv, d_pt, qcol, w_query, w_qpoint)

    first = [qpart] + [permuted(qpart, "col", f) for f in (1, 2, 3)]
    half = sds((keys // 2 + 32, chans), F32)
    mine, other = pl.pallas_call(
        functools.partial(key_kernel, heads, channels, npoint),
        out_shape=[half, half],
        in_specs=[smem] + [vmem] * 14,
        out_specs=[vmem] * 2,
        compiler_params=params,
        name="key_grads",
        cost_estimate=pl.CostEstimate(
            flops=2 * n * keys * 12 * wide, bytes_accessed=4 * n * keys, transcendentals=0
        ),
    )(
        place,
        both,
        dlo,
        alo,
        dglob,
        query,
        gq,
        gk,
        d_os,
        qcol,
        kcol,
        w_key,
        w_value,
        w_kpoint,
        w_vpoint,
    )
    *first, mine, other = lax.optimization_barrier((*first, mine, other))

    mine = mine + permuted(other, "row", 1)
    mine = mine.reshape(4, -1, chans)
    held = mine[0] + sum(permuted(mine[f], "row", 4 * f) for f in (1, 2, 3))

    pair_grad = pl.pallas_call(
        pair_kernel,
        out_shape=sds((rows, keys, depth), BF),
        in_specs=[vmem] * 2,
        out_specs=vmem,
        compiler_params=params,
        name="pair_grad",
        cost_estimate=pl.CostEstimate(
            flops=2 * rows * keys * depth * 3 * HP,
            bytes_accessed=2 * rows * keys * depth,
            transcendentals=0,
        ),
    )(both, rhs)
    held, pair_grad = lax.optimization_barrier((held, pair_grad))
    qpart = (first[0] + first[1]) + (first[2] + first[3])
    second = [qpart] + [around(qpart, f) for f in (3, 2, 1)]
    held = held + permuted(held, "row", 2)
    held, *second = lax.optimization_barrier((held, *second))
    mine = jnp.concatenate([held] + [permuted(held, "row", 4 * f) for f in (1, 2, 3)], axis=0)
    other = permuted(mine, "row", 1)
    grad_q, shift_q, grad_k, shift_k = pl.pallas_call(
        finish_kernel,
        out_shape=[
            sds((rows, chans), BF),
            sds((3, rows), F32),
            sds((keys, chans), BF),
            sds((3, keys), F32),
        ],
        in_specs=[smem] + [vmem] * 6,
        out_specs=[vmem] * 4,
        scratch_shapes=[pltpu.VMEM((8, keys), F32)],
        compiler_params=params,
        name="finish",
    )(place, *second, mine, other)
    return pair_grad, grad_q, shift_q, grad_k, shift_k


def solution(mesh):
    placed = (
        P("row", "col", None),
        P("row", None),
        P("col", None),
        P(),
        P(),
        P(),
        P(),
        P(),
        P(),
        P(),
        P(),
        P(),
        P(),
        P(None, "row"),
        P(None, "row"),
        P(None, "col"),
        P(None, "col"),
        P("row"),
        P("col"),
        P("col"),
        P("row", None),
    )
    return jax.shard_map(
        body,
        mesh=mesh,
        in_specs=placed,
        out_specs=(
            P("row", "col", None),
            P("row", None),
            P(None, "row"),
            P("col", None),
            P(None, "col"),
        ),
        check_vma=False,
    )
```

```python
import functools
import math

import jax
import jax.numpy as jnp
from jax import lax
from jax.experimental import pallas as pl
from jax.experimental.pallas import tpu as pltpu
from jax.sharding import PartitionSpec as P

HIGH = lax.Precision.HIGHEST
F32 = jnp.float32
BF = jnp.bfloat16
HP = 16
LANE = 128
NEG = -1e30
LIMIT = 24 * 1024 * 1024


def nn(a, b, precision=None):
    return lax.dot_general(
        a, b, (((1,), (0,)), ((), ())), preferred_element_type=F32, precision=precision
    )


def nt(a, b, precision=None):
    return lax.dot_general(
        a, b, (((1,), (1,)), ((), ())), preferred_element_type=F32, precision=precision
    )


def tn(a, b, precision=None):
    return lax.dot_general(
        a, b, (((0,), (0,)), ((), ())), preferred_element_type=F32, precision=precision
    )


def split(x):
    hi = x.astype(BF)
    return hi, (x - hi.astype(F32)).astype(BF)


def iota(shape, axis):
    return lax.broadcasted_iota(jnp.int32, shape, axis)


def head_mask(heads, npoint, width):
    lane = iota((HP, width), 1) % LANE
    row = iota((HP, width), 0)
    return (lane // npoint == row) & (lane < heads * npoint)


def channel_mask(heads, channels):
    lane = iota((HP, heads * channels), 1)
    return lane // channels == iota((HP, heads * channels), 0)


def spread(x, mask):
    n, w = x.shape
    wide = jnp.broadcast_to(x[:, None, :], (n, HP, w))
    return jnp.where(mask[None], wide, jnp.zeros((), x.dtype)).reshape(n * HP, w)


def gather_heads(x, mask):
    w = x.shape[1]
    full = jnp.where(mask[None], x.reshape(-1, HP, w), 0.0)
    return jnp.sum(full, axis=1)


def to_lanes(col, offset=0):
    n = col.shape[0] // HP
    mask = iota((HP, LANE), 1) == iota((HP, LANE), 0) + offset
    wide = jnp.broadcast_to(col, (n * HP, LANE)).reshape(n, HP, LANE)
    return jnp.sum(jnp.where(mask[None], wide, 0.0), axis=1)


def to_col(x, offset=0):
    n = x.shape[0]
    mask = iota((HP, LANE), 1) == iota((HP, LANE), 0) + offset
    wide = jnp.broadcast_to(x[:, None, :], (n, HP, LANE))
    return jnp.sum(jnp.where(mask[None], wide, 0.0), axis=2, keepdims=True).reshape(n * HP, 1)


def pad_lanes(x, width=LANE):
    n, w = x.shape
    return jnp.concatenate([x, jnp.zeros((n, width - w), x.dtype)], axis=1)


def rotate_points(local, cols, hp):
    parts = [local[:, b * hp : (b + 1) * hp] for b in range(3)]
    out = []
    for a in range(3):
        g = cols[:, 9 + a : 10 + a]
        g = g + sum(cols[:, 3 * a + b : 3 * a + b + 1] * parts[b] for b in range(3))
        out.append(pad_lanes(g))
    return jnp.concatenate(out, axis=1)


def back_rotate(x, cols):
    parts = [x[:, a * LANE : (a + 1) * LANE] for a in range(3)]
    return [sum(cols[:, 3 * a + b : 3 * a + b + 1] * parts[a] for a in range(3)) for b in range(3)]


def load_pair(pair_hbm, pair_ref, sems):
    nchunk = sems.shape[0]
    step = pair_hbm.shape[0] // nchunk
    copies = [
        pltpu.make_async_copy(
            pair_hbm.at[pl.ds(c * step, step)], pair_ref.at[pl.ds(c * step, step)], sems.at[c]
        )
        for c in range(nchunk)
    ]
    for copy in copies:
        copy.start()
    return copies, step


def padded_bias(wb_ref):
    heads, depth = wb_ref.shape
    return jnp.concatenate([wb_ref[...].astype(F32), jnp.zeros((HP - heads, depth), F32)], axis=0)


def logits_kernel(
    heads,
    channels,
    npoint,
    pair_hbm,
    sq_ref,
    sk_ref,
    wq_ref,
    wk_ref,
    wqp_ref,
    wkp_ref,
    wb_ref,
    gamma_ref,
    chainb_ref,
    rotq_ref,
    trq_ref,
    rotk_ref,
    trk_ref,
    cq_ref,
    ck_ref,
    km_ref,
    masked_ref,
    stats_ref,
    query_ref,
    key_ref,
    gq_ref,
    gk_ref,
    qcol_ref,
    kcol_ref,
    pair_ref,
    tq_ref,
    tk_ref,
    sems,
):
    rows, keys, depth = pair_hbm.shape
    hp = heads * npoint
    copies, step = load_pair(pair_hbm, pair_ref, sems)
    w_logit = math.sqrt(1.0 / 3.0)
    w_point = math.sqrt(2.0 / (9.0 * npoint))
    tq_ref[...] = jnp.zeros_like(tq_ref)
    tq_ref[0:9, 0:rows] = rotq_ref[...]
    tq_ref[9:12, 0:rows] = trq_ref[...]
    tq_ref[12:13, 0:rows] = cq_ref[...].astype(F32)
    tq_ref[13:14, 0:heads] = gamma_ref[...]
    tq_ref[14:15, 0:heads] = chainb_ref[...]
    qcols_all = tq_ref[...].T
    qcols = qcols_all[:rows]
    head_cols = qcols_all[:HP]
    qcol_ref[...] = qcols_all
    tk_ref[...] = jnp.zeros_like(tk_ref)
    tk_ref[0:9, :] = rotk_ref[...]
    tk_ref[9:12, :] = trk_ref[...]
    kcols = tk_ref[...].T
    kcol_ref[...] = kcols

    sq = sq_ref[...]
    sk = sk_ref[...]
    query = nt(sq, wq_ref[...]).astype(BF)
    key = nt(sk, wk_ref[...]).astype(BF)
    query_ref[...] = query
    key_ref[...] = key
    gq = rotate_points(nt(sq, wqp_ref[...]), qcols, hp)
    gk = rotate_points(nt(sk, wkp_ref[...]), kcols, hp)
    gq_ref[...] = gq
    gk_ref[...] = gk

    wbt = padded_bias(wb_ref).astype(BF)
    for c, copy in enumerate(copies):
        copy.wait()

        def one(i, carry):
            r = pl.multiple_of(i * HP, HP)
            masked_ref[pl.ds(r, HP), :] = nt(wbt, pair_ref[i])
            return carry

        lax.fori_loop(c * step, (c + 1) * step, one, 0, unroll=8)

    pmask = head_mask(heads, npoint, 3 * LANE)
    cmask = channel_mask(heads, channels)
    gqm = spread(gq, pmask)
    cross = nt(gqm, gk, HIGH)
    sqq = jnp.sum(gqm * gqm, axis=1, keepdims=True)
    sqk = nt(pmask.astype(F32), gk * gk, HIGH)
    qk = nt(spread(query.astype(F32), cmask).astype(BF), key)
    coef = (w_logit * w_point) * head_cols[:, 13:14]
    same = (qcols[:, 12:13] == ck_ref[...].astype(F32)).astype(F32)
    shape = (rows, HP, keys)
    dist = (sqq.reshape(rows, HP, 1) + sqk[None]) - 2.0 * cross.reshape(shape)
    inner = (
        qk.reshape(shape) * (1.0 / math.sqrt(channels))
        + masked_ref[...].reshape(shape)
        + head_cols[:, 14:15][None] * jnp.broadcast_to(same[:, None, :], shape)
    )
    logit = w_logit * inner - (0.5 * coef)[None] * dist
    valid = (km_ref[...] == 1)[None]
    masked = jnp.where(valid, logit, NEG)
    top = jnp.max(masked, axis=2, keepdims=True)
    total = jnp.sum(jnp.where(valid, jnp.exp(masked - top), 0.0), axis=2, keepdims=True)
    masked_ref[...] = masked.reshape(rows * HP, keys)
    packed = to_lanes(top.reshape(rows * HP, 1)) + to_lanes(total.reshape(rows * HP, 1), HP)
    stats_ref[...] = packed.T[: 2 * HP]


def base_kernel(
    heads,
    channels,
    npoint,
    pair_hbm,
    sk_ref,
    cot_ref,
    wv_ref,
    wvp_ref,
    wout_ref,
    kcol_ref,
    base_ref,
    gv_ref,
    dos_ref,
    dpt_ref,
    doz_ref,
    pair_ref,
    lhs_ref,
    sems,
):
    rows, keys, depth = pair_hbm.shape
    hp = heads * npoint
    copies, step = load_pair(pair_hbm, pair_ref, sems)
    sk = sk_ref[...]
    cot = cot_ref[...]
    value = nt(sk, wv_ref[...]).astype(BF)
    gv_ref[...] = rotate_points(nt(sk, wvp_ref[...]), kcol_ref[...], hp)
    nos = heads * channels
    first = nos + heads * depth
    dos = nt(cot, wout_ref[0:nos, :]).astype(BF)
    dos_ref[...] = dos
    for b in range(4):
        d = nt(cot, wout_ref[first + b * hp : first + (b + 1) * hp, :]).astype(BF).astype(F32)
        dpt_ref[:, b * LANE : (b + 1) * LANE] = pad_lanes(d)
    doz = nt(cot, wout_ref[nos:first, :]).astype(BF).astype(F32)
    lhs_ref[...] = jnp.zeros_like(lhs_ref)
    for h in range(heads):
        lhs_ref[pl.ds(h, rows, stride=HP), :] = doz[:, h * depth : (h + 1) * depth]
    doz_ref[...] = lhs_ref[...].astype(BF)
    dosm = spread(dos.astype(F32), channel_mask(heads, channels)).astype(BF)
    base_ref[...] = nt(dosm, value)
    for c, copy in enumerate(copies):
        copy.wait()

        def one(i, carry):
            r = pl.multiple_of(i * HP, HP)
            base_ref[pl.ds(r, HP), :] += nt(doz_ref[pl.ds(r, HP), :], pair_ref[i])
            return carry

        lax.fori_loop(c * step, (c + 1) * step, one, 0, unroll=8)


def attend_kernel(heads, npoint, masked_ref, base_ref, km_ref, stats_ref, gv_ref, attn_ref, out_ref):
    rows = stats_ref.shape[1]
    keys = masked_ref.shape[1]
    stats = jnp.concatenate(
        [stats_ref[...], jnp.zeros((LANE - stats_ref.shape[0], rows), F32)], axis=0
    ).T
    top = to_col(stats)
    total = to_col(stats, HP)
    valid = km_ref[...] == 1
    attn = jnp.where(valid, jnp.exp(masked_ref[...] - top), 0.0) / total
    attn_ref[...] = attn
    attn_b = attn.astype(BF)
    attn_f = attn_b.astype(F32)
    ghi, glo = split(gv_ref[...])
    opt = nn(attn_b, ghi) + nn(attn_b, glo)
    pmask = head_mask(heads, npoint, 3 * LANE)
    delta = jnp.sum(attn_f * base_ref[...], axis=1, keepdims=True)
    out_ref[...] = gather_heads(opt, pmask)
    out_ref[:, 0:LANE] += to_lanes(delta, heads * npoint)


def frames_of(heads, npoint, qcol_ref, rows):
    pmask = head_mask(heads, npoint, 3 * LANE)
    qall = qcol_ref[...]
    w_logit = math.sqrt(1.0 / 3.0)
    w_point = math.sqrt(2.0 / (9.0 * npoint))
    coef = (w_logit * w_point) * qall[:HP, 13:14]
    coef_lane = jnp.sum(jnp.where(pmask, coef, 0.0), axis=0, keepdims=True)
    return pmask, qall[:rows], coef_lane


def project(parts, width):
    single = jnp.zeros((parts[0][0].shape[0], width), F32)
    for part, weight in parts:
        phi, plo = split(part)
        single = single + (nn(phi, weight) + nn(plo, weight))
    return single


def component_sums(x):
    n = x.shape[0]
    cols = [jnp.sum(x[:, a * LANE : (a + 1) * LANE], axis=1, keepdims=True) for a in range(3)]
    return jnp.concatenate(cols + [jnp.zeros((n, LANE - 3), F32)], axis=1).T


def query_kernel(
    heads,
    channels,
    npoint,
    place_ref,
    attn_ref,
    base_ref,
    psum0_ref,
    psum1_ref,
    psum2_ref,
    psum3_ref,
    key_ref,
    gq_ref,
    gk_ref,
    gv_ref,
    dpt_ref,
    qcol_ref,
    wq_ref,
    wqp_ref,
    qout_ref,
    both_ref,
    dlo_ref,
    alo_ref,
    dglob_ref,
):
    rows, keys = gq_ref.shape[0], gk_ref.shape[0]
    hp = heads * npoint
    scale = math.sqrt(1.0 / 3.0) / math.sqrt(channels)
    cmask = channel_mask(heads, channels)
    pmask, qcols, coef_lane = frames_of(heads, npoint, qcol_ref, rows)
    inside = iota((1, LANE), 1) < hp

    psum = (psum0_ref[...] + psum1_ref[...]) + (psum2_ref[...] + psum3_ref[...])
    delta0 = to_col(psum[:, :LANE], hp)
    opt = [jnp.where(inside, psum[:, a * LANE : (a + 1) * LANE], 0.0) for a in range(3)]
    moved = [jnp.where(inside, opt[a] - qcols[:, 9 + a : 10 + a], 0.0) for a in range(3)]
    oloc = back_rotate(jnp.concatenate(moved, axis=1), qcols)
    onorm = jnp.sqrt(1.0 + (oloc[0] * oloc[0] + oloc[1] * oloc[1] + oloc[2] * oloc[2]))
    ratio = dpt_ref[:, 3 * LANE : 4 * LANE] / onorm
    dloc = [dpt_ref[:, b * LANE : (b + 1) * LANE] + ratio * oloc[b] for b in range(3)]
    dglob = jnp.concatenate(
        [
            sum(qcols[:, 3 * a + b : 3 * a + b + 1] * dloc[b] for b in range(3))
            for a in range(3)
        ],
        axis=1,
    )
    dglob_ref[...] = dglob
    dghi, dglo = split(spread(dglob, pmask))
    opt_row = jnp.concatenate(opt, axis=1)
    delta = delta0 + jnp.sum(spread(opt_row * dglob, pmask), axis=1, keepdims=True)
    gvhi, gvlo = split(gv_ref[...])
    dattn = base_ref[...] + nt(dghi, gvhi) + (nt(dghi, gvlo) + nt(dglo, gvhi))
    attn = attn_ref[...]
    dlogit = attn * (dattn - delta)
    dhi, dlo = split(dlogit)
    ahi, alo = split(attn)
    both_ref[:, 0:HP, :] = dhi.reshape(rows, HP, keys)
    both_ref[:, HP : 2 * HP, :] = ahi.reshape(rows, HP, keys)
    dlo_ref[...] = dlo
    alo_ref[...] = alo

    gkhi, gklo = split(gk_ref[...])
    dq = scale * gather_heads(nn(dhi, key_ref[...]), cmask)
    qpts = gather_heads(nn(dhi, gkhi) + (nn(dhi, gklo) + nn(dlo, gkhi)), pmask)
    qsum = jnp.sum(dlogit, axis=1, keepdims=True)
    qsum_lane = gather_heads(jnp.broadcast_to(qsum, (rows * HP, 3 * LANE)), pmask)
    dgq = coef_lane * (qpts - gq_ref[...] * qsum_lane)
    mq = back_rotate(dgq, qcols)
    width = qout_ref.shape[1]
    qout_ref[0:rows, :] = project(
        [(dq, wq_ref[...])]
        + [(mq[b][:, :hp], wqp_ref[b * hp : (b + 1) * hp, :]) for b in range(3)],
        width,
    )
    shift = jnp.where(place_ref[0] == 0, dgq - dglob, dgq)
    qout_ref[rows:, :] = jnp.zeros((qout_ref.shape[0] - rows, width), F32)
    qout_ref[rows : rows + 8, 0:rows] = component_sums(shift)[:8, :rows]


def key_kernel(
    heads,
    channels,
    npoint,
    place_ref,
    both_ref,
    dlo_ref,
    alo_ref,
    dglob_ref,
    query_ref,
    gq_ref,
    gk_ref,
    dos_ref,
    qcol_ref,
    kcol_ref,
    wk_ref,
    wv_ref,
    wkp_ref,
    wvp_ref,
    mine_ref,
    other_ref,
):
    rows, keys = gq_ref.shape[0], gk_ref.shape[0]
    hp = heads * npoint
    scale = math.sqrt(1.0 / 3.0) / math.sqrt(channels)
    cmask = channel_mask(heads, channels)
    pmask, qcols, coef_lane = frames_of(heads, npoint, qcol_ref, rows)
    kcols = kcol_ref[...]
    dhi = both_ref[:, 0:HP, :].reshape(rows * HP, keys)
    ahi = both_ref[:, HP : 2 * HP, :].reshape(rows * HP, keys)
    dlo, alo = dlo_ref[...], alo_ref[...]
    dghi, dglo = split(spread(dglob_ref[...], pmask))
    gqhi, gqlo = split(spread(gq_ref[...], pmask))
    ones = jnp.broadcast_to(pmask[None], (rows, HP, 3 * LANE)).astype(F32).reshape(
        rows * HP, 3 * LANE
    )
    ones = ones.astype(BF)
    qm = spread(query_ref[...].astype(F32), cmask).astype(BF)
    dosm = spread(dos_ref[...].astype(F32), cmask).astype(BF)
    dk = scale * tn(dhi, qm)
    dv = tn(ahi, dosm)
    kpts = tn(dhi, gqhi) + (tn(dhi, gqlo) + tn(dlo, gqhi))
    ksum = tn(dhi, ones) + tn(dlo, ones)
    vpts = tn(ahi, dghi) + (tn(ahi, dglo) + tn(alo, dghi))
    dgk = coef_lane * (kpts - gk_ref[...] * ksum)
    mk = back_rotate(dgk, kcols)
    mv = back_rotate(vpts, kcols)
    width = mine_ref.shape[1]
    single = project(
        [(dk, wk_ref[...]), (dv, wv_ref[...])]
        + [(mk[b][:, :hp], wkp_ref[b * hp : (b + 1) * hp, :]) for b in range(3)]
        + [(mv[b][:, :hp], wvp_ref[b * hp : (b + 1) * hp, :]) for b in range(3)],
        width,
    )
    cols = component_sums(dgk + vpts)
    piece = keys // 8
    core, quarter = place_ref[1], place_ref[2]

    def put(ref, half):
        for n in range(4):
            k = half * 4 + n
            r = pl.multiple_of((n ^ quarter) * (piece + 8), 8)
            ref[pl.ds(r, piece), :] = single[k * piece : (k + 1) * piece]
            r = pl.multiple_of((n ^ quarter) * (piece + 8) + piece, 8)
            ref[pl.ds(r, 8), :] = jnp.concatenate(
                [cols[:8, k * piece : (k + 1) * piece], jnp.zeros((8, width - piece), F32)], axis=1
            )

    @pl.when(core == 0)
    def _():
        put(mine_ref, 0)
        put(other_ref, 1)

    @pl.when(core != 0)
    def _():
        put(mine_ref, 1)
        put(other_ref, 0)


def finish_kernel(
    place_ref,
    q0_ref,
    q1_ref,
    q2_ref,
    q3_ref,
    mine_ref,
    other_ref,
    gradq_ref,
    shiftq_ref,
    gradk_ref,
    shiftk_ref,
    shift_ref,
):
    rows = gradq_ref.shape[0]
    keys = gradk_ref.shape[0]
    piece = keys // 8
    total = (q0_ref[...] + q1_ref[...]) + (q2_ref[...] + q3_ref[...])
    gradq_ref[...] = total[:rows].astype(BF)
    shiftq_ref[...] = total[rows : rows + 3, :rows]
    core, quarter = place_ref[1], place_ref[2]

    def put(ref, half):
        parts = []
        for n in range(4):
            k = half * 4 + n
            r = pl.multiple_of((n ^ quarter) * (piece + 8), 8)
            gradk_ref[k * piece : (k + 1) * piece, :] = ref[pl.ds(r, piece), :].astype(BF)
            r = pl.multiple_of((n ^ quarter) * (piece + 8) + piece, 8)
            parts.append(ref[pl.ds(r, 8), 0:piece])
        shift_ref[:, half * 4 * piece : (half + 1) * 4 * piece] = jnp.concatenate(parts, axis=1)

    @pl.when(core == 0)
    def _():
        put(mine_ref, 0)
        put(other_ref, 1)

    @pl.when(core != 0)
    def _():
        put(mine_ref, 1)
        put(other_ref, 0)

    shiftk_ref[...] = shift_ref[0:3, :]


def pair_kernel(both_ref, doz_ref, wb_ref, *refs):
    out_ref = refs[-1]
    rows = both_ref.shape[0]
    whi, wlo = split(math.sqrt(1.0 / 3.0) * padded_bias(wb_ref))

    def one(i, carry):
        both = both_ref[i]
        left = jnp.concatenate([both[:HP], both], axis=0)
        doz = doz_ref[pl.ds(pl.multiple_of(i * HP, HP), HP), :]
        right = jnp.concatenate([wlo, whi, doz], axis=0)
        out_ref[i] = tn(left, right).astype(BF)
        return carry

    lax.fori_loop(0, rows, one, 0, unroll=True)


def pair_part(part, parts, both, doz, w_bias, before, params):
    rows, _, keys = both.shape
    depth = doz.shape[1]
    step = rows // parts
    specs = [
        pl.BlockSpec((step, 2 * HP, keys), lambda g: (part, 0, 0)),
        pl.BlockSpec((step * HP, depth), lambda g: (part, 0)),
        pl.BlockSpec(w_bias.shape, lambda g: (0, 0)),
    ]
    operands = [both, doz, w_bias]
    if before is not None:
        specs.append(pl.BlockSpec(memory_space=pl.ANY))
        operands.append(before)
    return pl.pallas_call(
        pair_kernel,
        grid=(1,),
        out_shape=jax.ShapeDtypeStruct((rows, keys, depth), BF),
        in_specs=specs,
        out_specs=pl.BlockSpec((step, keys, depth), lambda g: (part, 0, 0)),
        input_output_aliases={} if before is None else {3: 0},
        compiler_params=params,
        name="pair_grad",
        cost_estimate=pl.CostEstimate(
            flops=2 * step * keys * depth * 3 * HP,
            bytes_accessed=2 * step * keys * depth,
            transcendentals=0,
        ),
    )(*operands)


def permuted(x, axis, flip):
    size = lax.axis_size(axis)
    return lax.ppermute(x, axis, [(i, i ^ flip) for i in range(size)])


def around(x, hops):
    size = lax.axis_size("col")
    ring = size // 2
    sign = -1 if hops == 2 else 1
    moves = []
    for i in range(size):
        z, low = i // 2, i % 2
        source = (z + (hops if z % 2 else -hops) * sign) % ring
        moves.append((source * 2 + low, i))
    return lax.ppermute(x, "col", moves)


def merged(parts):
    top = functools.reduce(jnp.maximum, [p[:HP] for p in parts])
    total = sum(p[HP:] * jnp.exp(p[:HP] - top) for p in parts)
    return jnp.concatenate([top, total], axis=0)


def body(
    pair,
    single_q,
    single_k,
    w_query,
    w_key,
    w_value,
    w_qpoint,
    w_kpoint,
    w_vpoint,
    w_bias,
    w_out,
    head_gamma,
    chain_bias,
    rot_q,
    trans_q,
    rot_k,
    trans_k,
    chain_q,
    chain_k,
    key_mask,
    cotangent,
):
    rows, keys, depth = pair.shape
    heads = w_bias.shape[1]
    channels = w_query.shape[1] // heads
    npoint = w_qpoint.shape[1] // (3 * heads)
    chans = single_q.shape[1]
    hc = heads * channels
    n = rows * HP
    sds = jax.ShapeDtypeStruct
    params = pltpu.CompilerParams(vmem_limit_bytes=LIMIT)
    vmem = pl.BlockSpec(memory_space=pltpu.VMEM)
    wide = 3 * LANE
    km = key_mask.reshape(1, keys)
    w_query, w_key, w_value = w_query.T, w_key.T, w_value.T
    w_qpoint, w_kpoint, w_vpoint = w_qpoint.T, w_kpoint.T, w_vpoint.T
    w_bias = w_bias.T
    masked, stats, query, key, gq, gk, qcol, kcol = pl.pallas_call(
        functools.partial(logits_kernel, heads, channels, npoint),
        out_shape=[
            sds((n, keys), F32),
            sds((2 * HP, rows), F32),
            sds((rows, hc), BF),
            sds((keys, hc), BF),
            sds((rows, wide), F32),
            sds((keys, wide), F32),
            sds((LANE, LANE), F32),
            sds((keys, LANE), F32),
        ],
        in_specs=[pl.BlockSpec(memory_space=pl.ANY)] + [vmem] * 16,
        out_specs=[vmem] * 8,
        scratch_shapes=[
            pltpu.VMEM((rows, keys, depth), BF),
            pltpu.VMEM((LANE, LANE), F32),
            pltpu.VMEM((LANE, keys), F32),
            pltpu.SemaphoreType.DMA((4,)),
        ],
        compiler_params=params,
        name="logits",
    )(
        pair,
        single_q,
        single_k,
        w_query,
        w_key,
        w_qpoint,
        w_kpoint,
        w_bias,
        head_gamma.reshape(1, heads),
        chain_bias.reshape(1, heads),
        rot_q,
        trans_q,
        rot_k,
        trans_k,
        chain_q.reshape(1, rows),
        chain_k.reshape(1, keys),
        km,
    )

    first = [stats] + [permuted(stats, "col", f) for f in (1, 2, 3)]
    base, gv, d_os, d_pt, doz = pl.pallas_call(
        functools.partial(base_kernel, heads, channels, npoint),
        out_shape=[
            sds((n, keys), F32),
            sds((keys, wide), F32),
            sds((rows, hc), BF),
            sds((rows, 4 * LANE), F32),
            sds((n, depth), BF),
        ],
        in_specs=[pl.BlockSpec(memory_space=pl.ANY)] + [vmem] * 6,
        out_specs=[vmem] * 5,
        scratch_shapes=[
            pltpu.VMEM((rows, keys, depth), BF),
            pltpu.VMEM((n, depth), F32),
            pltpu.SemaphoreType.DMA((4,)),
        ],
        compiler_params=params,
        name="base",
        cost_estimate=pl.CostEstimate(
            flops=8 * n * keys * wide, bytes_accessed=4 * rows * keys * depth, transcendentals=0
        ),
    )(pair, single_k, cotangent, w_value, w_vpoint, w_out, kcol)
    stats = merged(first)
    stats = merged([stats] + [around(stats, f) for f in (3, 2, 1)])

    attn, points = pl.pallas_call(
        functools.partial(attend_kernel, heads, npoint),
        out_shape=[sds((n, keys), F32), sds((rows, wide), F32)],
        in_specs=[vmem] * 5,
        out_specs=[vmem] * 2,
        compiler_params=params,
        name="attend",
    )(masked, base, km, stats, gv)
    points = points + sum(permuted(points, "col", f) for f in (1, 2, 3))
    parts = [points] + [around(points, f) for f in (1, 2, 3)]

    me = lax.axis_index("row")
    place = jnp.stack([lax.axis_index("col"), me % 2, me // 4]).astype(jnp.int32)
    smem = pl.BlockSpec(memory_space=pltpu.SMEM)
    qpart, both, dlo, alo, dglob = pl.pallas_call(
        functools.partial(query_kernel, heads, channels, npoint),
        out_shape=[
            sds((rows + 8, chans), F32),
            sds((rows, 2 * HP, keys), BF),
            sds((n, keys), BF),
            sds((n, keys), BF),
            sds((rows, wide), F32),
        ],
        in_specs=[smem] + [vmem] * 14,
        out_specs=[vmem] * 5,
        compiler_params=params,
        name="query_grads",
    )(place, attn, base, *parts, key, gq, gk, gv, d_pt, qcol, w_query, w_qpoint)

    first = [qpart] + [permuted(qpart, "col", f) for f in (1, 2, 3)]
    half = sds((keys // 2 + 32, chans), F32)
    mine, other = pl.pallas_call(
        functools.partial(key_kernel, heads, channels, npoint),
        out_shape=[half, half],
        in_specs=[smem] + [vmem] * 14,
        out_specs=[vmem] * 2,
        compiler_params=params,
        name="key_grads",
        cost_estimate=pl.CostEstimate(
            flops=2 * n * keys * 12 * wide, bytes_accessed=4 * n * keys, transcendentals=0
        ),
    )(
        place,
        both,
        dlo,
        alo,
        dglob,
        query,
        gq,
        gk,
        d_os,
        qcol,
        kcol,
        w_key,
        w_value,
        w_kpoint,
        w_vpoint,
    )
    *first, mine, other = lax.optimization_barrier((*first, mine, other))

    mine = mine + permuted(other, "row", 1)
    mine, both = lax.optimization_barrier((mine, both))
    mine = mine.reshape(4, -1, chans)
    held = mine[0] + sum(permuted(mine[f], "row", 4 * f) for f in (1, 2, 3))
    pair_grad = pair_part(0, 2, both, doz, w_bias, None, params)
    held, both, pair_grad = lax.optimization_barrier((held, both, pair_grad))
    qpart = (first[0] + first[1]) + (first[2] + first[3])
    second = [qpart] + [around(qpart, f) for f in (1, 2, 3)]
    held = held + permuted(held, "row", 2)
    pair_grad = pair_part(1, 2, both, doz, w_bias, pair_grad, params)
    held, pair_grad, *second = lax.optimization_barrier((held, pair_grad, *second))
    mine = jnp.concatenate([held] + [permuted(held, "row", 4 * f) for f in (1, 2, 3)], axis=0)
    other = permuted(mine, "row", 1)
    grad_q, shift_q, grad_k, shift_k = pl.pallas_call(
        finish_kernel,
        out_shape=[
            sds((rows, chans), BF),
            sds((3, rows), F32),
            sds((keys, chans), BF),
            sds((3, keys), F32),
        ],
        in_specs=[smem] + [vmem] * 6,
        out_specs=[vmem] * 4,
        scratch_shapes=[pltpu.VMEM((8, keys), F32)],
        compiler_params=params,
        name="finish",
    )(place, *second, mine, other)
    return pair_grad, grad_q, shift_q, grad_k, shift_k


def solution(mesh):
    placed = (
        P("row", "col", None),
        P("row", None),
        P("col", None),
        P(),
        P(),
        P(),
        P(),
        P(),
        P(),
        P(),
        P(),
        P(),
        P(),
        P(None, "row"),
        P(None, "row"),
        P(None, "col"),
        P(None, "col"),
        P("row"),
        P("col"),
        P("col"),
        P("row", None),
    )
    return jax.shard_map(
        body,
        mesh=mesh,
        in_specs=placed,
        out_specs=(
            P("row", "col", None),
            P("row", None),
            P(None, "row"),
            P("col", None),
            P(None, "col"),
        ),
        check_vma=False,
    )
```

```python
import functools
import math

import jax
import jax.numpy as jnp
from jax import lax
from jax.experimental import pallas as pl
from jax.experimental.pallas import tpu as pltpu
from jax.sharding import PartitionSpec as P

HIGH = lax.Precision.HIGHEST
F32 = jnp.float32
BF = jnp.bfloat16
HP = 16
LANE = 128
NEG = -1e30
LIMIT = 24 * 1024 * 1024
ALONE = 56 * 1024 * 1024


VMEM = pl.BlockSpec(memory_space=pltpu.VMEM)
SMEM = pl.BlockSpec(memory_space=pltpu.SMEM)
ANY = pl.BlockSpec(memory_space=pl.ANY)


def call(kernel, name, outs, smem, hbm, vmem, scratch=(), cost=None, limit=LIMIT):
    return pl.pallas_call(
        kernel,
        out_shape=outs,
        in_specs=[SMEM] * len(smem) + [ANY] * len(hbm) + [VMEM] * len(vmem),
        out_specs=[VMEM] * len(outs),
        scratch_shapes=list(scratch),
        compiler_params=pltpu.CompilerParams(vmem_limit_bytes=limit),
        name=name,
        cost_estimate=cost,
    )(*smem, *hbm, *vmem)


def nn(a, b, precision=None):
    return lax.dot_general(
        a, b, (((1,), (0,)), ((), ())), preferred_element_type=F32, precision=precision
    )


def nt(a, b, precision=None):
    return lax.dot_general(
        a, b, (((1,), (1,)), ((), ())), preferred_element_type=F32, precision=precision
    )


def tn(a, b, precision=None):
    return lax.dot_general(
        a, b, (((0,), (0,)), ((), ())), preferred_element_type=F32, precision=precision
    )


def split(x):
    hi = x.astype(BF)
    return hi, (x - hi.astype(F32)).astype(BF)


def iota(shape, axis):
    return lax.broadcasted_iota(jnp.int32, shape, axis)


def head_mask(heads, npoint, width):
    lane = iota((HP, width), 1) % LANE
    row = iota((HP, width), 0)
    return (lane // npoint == row) & (lane < heads * npoint)


def channel_mask(heads, channels):
    lane = iota((HP, heads * channels), 1)
    return lane // channels == iota((HP, heads * channels), 0)


def spread(x, mask):
    n, w = x.shape
    wide = jnp.broadcast_to(x[:, None, :], (n, HP, w))
    return jnp.where(mask[None], wide, jnp.zeros((), x.dtype)).reshape(n * HP, w)


def gather_heads(x, mask):
    w = x.shape[1]
    full = jnp.where(mask[None], x.reshape(-1, HP, w), 0.0)
    return jnp.sum(full, axis=1)


def to_lanes(col, offset=0):
    n = col.shape[0] // HP
    mask = iota((HP, LANE), 1) == iota((HP, LANE), 0) + offset
    wide = jnp.broadcast_to(col, (n * HP, LANE)).reshape(n, HP, LANE)
    return jnp.sum(jnp.where(mask[None], wide, 0.0), axis=1)


def to_col(x, offset=0):
    n = x.shape[0]
    mask = iota((HP, LANE), 1) == iota((HP, LANE), 0) + offset
    wide = jnp.broadcast_to(x[:, None, :], (n, HP, LANE))
    return jnp.sum(jnp.where(mask[None], wide, 0.0), axis=2, keepdims=True).reshape(n * HP, 1)


def pad_lanes(x, width=LANE):
    n, w = x.shape
    return jnp.concatenate([x, jnp.zeros((n, width - w), x.dtype)], axis=1)


def rotate_points(local, cols, hp):
    parts = [local[:, b * hp : (b + 1) * hp] for b in range(3)]
    out = []
    for a in range(3):
        g = cols[:, 9 + a : 10 + a]
        g = g + sum(cols[:, 3 * a + b : 3 * a + b + 1] * parts[b] for b in range(3))
        out.append(pad_lanes(g))
    return jnp.concatenate(out, axis=1)


def back_rotate(x, cols):
    parts = [x[:, a * LANE : (a + 1) * LANE] for a in range(3)]
    return [sum(cols[:, 3 * a + b : 3 * a + b + 1] * parts[a] for a in range(3)) for b in range(3)]


def load_pair(pair_hbm, pair_ref, sems):
    nchunk = sems.shape[0]
    step = pair_hbm.shape[0] // nchunk
    copies = [
        pltpu.make_async_copy(
            pair_hbm.at[pl.ds(c * step, step)], pair_ref.at[pl.ds(c * step, step)], sems.at[c]
        )
        for c in range(nchunk)
    ]
    for copy in copies:
        copy.start()
    return copies, step


def padded_bias(wb_ref):
    heads, depth = wb_ref.shape
    return jnp.concatenate([wb_ref[...].astype(F32), jnp.zeros((HP - heads, depth), F32)], axis=0)


def logits_kernel(
    heads,
    channels,
    npoint,
    pair_hbm,
    sq_ref,
    sk_ref,
    wq_ref,
    wk_ref,
    wqp_ref,
    wkp_ref,
    wb_ref,
    gamma_ref,
    chainb_ref,
    rotq_ref,
    trq_ref,
    rotk_ref,
    trk_ref,
    cq_ref,
    ck_ref,
    km_ref,
    masked_ref,
    stats_ref,
    query_ref,
    key_ref,
    gq_ref,
    gk_ref,
    qcol_ref,
    kcol_ref,
    pair_ref,
    tq_ref,
    tk_ref,
    sems,
):
    rows, keys, depth = pair_hbm.shape
    hp = heads * npoint
    copies, step = load_pair(pair_hbm, pair_ref, sems)
    w_logit = math.sqrt(1.0 / 3.0)
    w_point = math.sqrt(2.0 / (9.0 * npoint))
    tq_ref[...] = jnp.zeros_like(tq_ref)
    tq_ref[0:9, 0:rows] = rotq_ref[...]
    tq_ref[9:12, 0:rows] = trq_ref[...]
    tq_ref[12:13, 0:rows] = cq_ref[...].astype(F32)
    tq_ref[13:14, 0:heads] = gamma_ref[...]
    tq_ref[14:15, 0:heads] = chainb_ref[...]
    qcols_all = tq_ref[...].T
    qcols = qcols_all[:rows]
    head_cols = qcols_all[:HP]
    qcol_ref[...] = qcols_all
    tk_ref[...] = jnp.zeros_like(tk_ref)
    tk_ref[0:9, :] = rotk_ref[...]
    tk_ref[9:12, :] = trk_ref[...]
    kcols = tk_ref[...].T
    kcol_ref[...] = kcols

    sq = sq_ref[...]
    sk = sk_ref[...]
    query = nt(sq, wq_ref[...]).astype(BF)
    key = nt(sk, wk_ref[...]).astype(BF)
    query_ref[...] = query
    key_ref[...] = key
    gq = rotate_points(nt(sq, wqp_ref[...]), qcols, hp)
    gk = rotate_points(nt(sk, wkp_ref[...]), kcols, hp)
    gq_ref[...] = gq
    gk_ref[...] = gk

    wbt = padded_bias(wb_ref).astype(BF)
    for c, copy in enumerate(copies):
        copy.wait()

        def one(i, carry):
            r = pl.multiple_of(i * HP, HP)
            masked_ref[pl.ds(r, HP), :] = nt(wbt, pair_ref[i])
            return carry

        lax.fori_loop(c * step, (c + 1) * step, one, 0, unroll=8)

    pmask = head_mask(heads, npoint, 3 * LANE)
    cmask = channel_mask(heads, channels)
    gqm = spread(gq, pmask)
    cross = nt(gqm, gk, HIGH)
    sqq = jnp.sum(gqm * gqm, axis=1, keepdims=True)
    sqk = nt(pmask.astype(F32), gk * gk, HIGH)
    qk = nt(spread(query.astype(F32), cmask).astype(BF), key)
    coef = (w_logit * w_point) * head_cols[:, 13:14]
    same = (qcols[:, 12:13] == ck_ref[...].astype(F32)).astype(F32)
    shape = (rows, HP, keys)
    dist = (sqq.reshape(rows, HP, 1) + sqk[None]) - 2.0 * cross.reshape(shape)
    inner = (
        qk.reshape(shape) * (1.0 / math.sqrt(channels))
        + masked_ref[...].reshape(shape)
        + head_cols[:, 14:15][None] * jnp.broadcast_to(same[:, None, :], shape)
    )
    logit = w_logit * inner - (0.5 * coef)[None] * dist
    valid = (km_ref[...] == 1)[None]
    masked = jnp.where(valid, logit, NEG)
    top = jnp.max(masked, axis=2, keepdims=True)
    total = jnp.sum(jnp.where(valid, jnp.exp(masked - top), 0.0), axis=2, keepdims=True)
    masked_ref[...] = masked.reshape(rows * HP, keys)
    packed = to_lanes(top.reshape(rows * HP, 1)) + to_lanes(total.reshape(rows * HP, 1), HP)
    stats_ref[...] = packed.T[: 2 * HP]


def base_kernel(
    heads,
    channels,
    npoint,
    pair_hbm,
    kcol_ref,
    sk_ref,
    cot_ref,
    wv_ref,
    wvp_ref,
    wout_ref,
    base_ref,
    gv_ref,
    dos_ref,
    dpt_ref,
    doz_ref,
    pair_ref,
    lhs_ref,
    sems,
):
    rows, keys, depth = pair_hbm.shape
    hp = heads * npoint
    copies, step = load_pair(pair_hbm, pair_ref, sems)
    sk = sk_ref[...]
    cot = cot_ref[...]
    value = nt(sk, wv_ref[...]).astype(BF)
    gv_ref[...] = rotate_points(nt(sk, wvp_ref[...]), kcol_ref[...], hp)
    nos = heads * channels
    first = nos + heads * depth
    dos = nt(cot, wout_ref[0:nos, :]).astype(BF)
    dos_ref[...] = dos
    for b in range(4):
        d = nt(cot, wout_ref[first + b * hp : first + (b + 1) * hp, :]).astype(BF).astype(F32)
        dpt_ref[:, b * LANE : (b + 1) * LANE] = pad_lanes(d)
    doz = nt(cot, wout_ref[nos:first, :]).astype(BF).astype(F32)
    lhs_ref[...] = jnp.zeros_like(lhs_ref)
    for h in range(heads):
        lhs_ref[pl.ds(h, rows, stride=HP), :] = doz[:, h * depth : (h + 1) * depth]
    doz_ref[...] = lhs_ref[...].astype(BF)
    dosm = spread(dos.astype(F32), channel_mask(heads, channels)).astype(BF)
    base_ref[...] = nt(dosm, value)
    for c, copy in enumerate(copies):
        copy.wait()

        def one(i, carry):
            r = pl.multiple_of(i * HP, HP)
            base_ref[pl.ds(r, HP), :] += nt(doz_ref[pl.ds(r, HP), :], pair_ref[i])
            return carry

        lax.fori_loop(c * step, (c + 1) * step, one, 0, unroll=8)


def attend_kernel(
    heads,
    npoint,
    masked_ref,
    base_ref,
    gv_ref,
    km_ref,
    stats_ref,
    attn_ref,
    out_ref,
):
    rows = stats_ref.shape[1]
    stats = jnp.concatenate(
        [stats_ref[...], jnp.zeros((LANE - stats_ref.shape[0], rows), F32)], axis=0
    ).T
    top = to_col(stats)
    total = to_col(stats, HP)
    valid = km_ref[...] == 1
    attn = jnp.where(valid, jnp.exp(masked_ref[...] - top), 0.0) / total
    attn_ref[...] = attn
    attn_b = attn.astype(BF)
    attn_f = attn_b.astype(F32)
    ghi, glo = split(gv_ref[...])
    opt = nn(attn_b, ghi) + nn(attn_b, glo)
    pmask = head_mask(heads, npoint, 3 * LANE)
    delta = jnp.sum(attn_f * base_ref[...], axis=1, keepdims=True)
    out_ref[...] = gather_heads(opt, pmask)
    out_ref[:, 0:LANE] += to_lanes(delta, heads * npoint)


def frames_of(heads, npoint, qcol_ref, rows):
    pmask = head_mask(heads, npoint, 3 * LANE)
    qall = qcol_ref[...]
    w_logit = math.sqrt(1.0 / 3.0)
    w_point = math.sqrt(2.0 / (9.0 * npoint))
    coef = (w_logit * w_point) * qall[:HP, 13:14]
    coef_lane = jnp.sum(jnp.where(pmask, coef, 0.0), axis=0, keepdims=True)
    return pmask, qall[:rows], coef_lane


def project(parts, width):
    single = jnp.zeros((parts[0][0].shape[0], width), F32)
    for part, weight in parts:
        phi, plo = split(part)
        single = single + (nn(phi, weight) + nn(plo, weight))
    return single


def component_sums(x):
    n = x.shape[0]
    cols = [jnp.sum(x[:, a * LANE : (a + 1) * LANE], axis=1, keepdims=True) for a in range(3)]
    return jnp.concatenate(cols + [jnp.zeros((n, LANE - 3), F32)], axis=1).T


def query_kernel(
    heads,
    channels,
    npoint,
    place_ref,
    attn_ref,
    base_ref,
    key_ref,
    gq_ref,
    gk_ref,
    gv_ref,
    dpt_ref,
    qcol_ref,
    psum_ref,
    wq_ref,
    wqp_ref,
    qout_ref,
    both_ref,
    dlo_ref,
    alo_ref,
    dglob_ref,
):
    rows, keys = gq_ref.shape[0], gk_ref.shape[0]
    hp = heads * npoint
    scale = math.sqrt(1.0 / 3.0) / math.sqrt(channels)
    cmask = channel_mask(heads, channels)
    pmask, qcols, coef_lane = frames_of(heads, npoint, qcol_ref, rows)
    inside = iota((1, LANE), 1) < hp

    psum = psum_ref[...]
    delta0 = to_col(psum[:, :LANE], hp)
    opt = [jnp.where(inside, psum[:, a * LANE : (a + 1) * LANE], 0.0) for a in range(3)]
    moved = [jnp.where(inside, opt[a] - qcols[:, 9 + a : 10 + a], 0.0) for a in range(3)]
    oloc = back_rotate(jnp.concatenate(moved, axis=1), qcols)
    onorm = jnp.sqrt(1.0 + (oloc[0] * oloc[0] + oloc[1] * oloc[1] + oloc[2] * oloc[2]))
    ratio = dpt_ref[:, 3 * LANE : 4 * LANE] / onorm
    dloc = [dpt_ref[:, b * LANE : (b + 1) * LANE] + ratio * oloc[b] for b in range(3)]
    dglob = jnp.concatenate(
        [
            sum(qcols[:, 3 * a + b : 3 * a + b + 1] * dloc[b] for b in range(3))
            for a in range(3)
        ],
        axis=1,
    )
    dglob_ref[...] = dglob
    dghi, dglo = split(spread(dglob, pmask))
    opt_row = jnp.concatenate(opt, axis=1)
    delta = delta0 + jnp.sum(spread(opt_row * dglob, pmask), axis=1, keepdims=True)
    gvhi, gvlo = split(gv_ref[...])
    dattn = base_ref[...] + nt(dghi, gvhi) + (nt(dghi, gvlo) + nt(dglo, gvhi))
    attn = attn_ref[...]
    dlogit = attn * (dattn - delta)
    dhi, dlo = split(dlogit)
    ahi, alo = split(attn)
    both_ref[:, 0:HP, :] = dhi.reshape(rows, HP, keys)
    both_ref[:, HP : 2 * HP, :] = ahi.reshape(rows, HP, keys)
    dlo_ref[...] = dlo
    alo_ref[...] = alo

    gkhi, gklo = split(gk_ref[...])
    dq = scale * gather_heads(nn(dhi, key_ref[...]), cmask)
    qpts = gather_heads(nn(dhi, gkhi) + (nn(dhi, gklo) + nn(dlo, gkhi)), pmask)
    qsum = jnp.sum(dlogit, axis=1, keepdims=True)
    qsum_lane = gather_heads(jnp.broadcast_to(qsum, (rows * HP, 3 * LANE)), pmask)
    dgq = coef_lane * (qpts - gq_ref[...] * qsum_lane)
    mq = back_rotate(dgq, qcols)
    width = qout_ref.shape[1]
    qout_ref[0:rows, :] = project(
        [(dq, wq_ref[...])]
        + [(mq[b][:, :hp], wqp_ref[b * hp : (b + 1) * hp, :]) for b in range(3)],
        width,
    )
    shift = jnp.where(place_ref[0] == 0, dgq - dglob, dgq)
    qout_ref[rows:, :] = jnp.zeros((qout_ref.shape[0] - rows, width), F32)
    qout_ref[rows : rows + 8, 0:rows] = component_sums(shift)[:8, :rows]


def key_kernel(
    heads,
    channels,
    npoint,
    place_ref,
    both_ref,
    dlo_ref,
    alo_ref,
    dglob_ref,
    query_ref,
    gq_ref,
    gk_ref,
    dos_ref,
    qcol_ref,
    kcol_ref,
    wk_ref,
    wv_ref,
    wkp_ref,
    wvp_ref,
    mine_ref,
    other_ref,
):
    rows, keys = gq_ref.shape[0], gk_ref.shape[0]
    hp = heads * npoint
    scale = math.sqrt(1.0 / 3.0) / math.sqrt(channels)
    cmask = channel_mask(heads, channels)
    pmask, qcols, coef_lane = frames_of(heads, npoint, qcol_ref, rows)
    kcols = kcol_ref[...]
    dhi = both_ref[:, 0:HP, :].reshape(rows * HP, keys)
    ahi = both_ref[:, HP : 2 * HP, :].reshape(rows * HP, keys)
    dlo, alo = dlo_ref[...], alo_ref[...]
    dghi, dglo = split(spread(dglob_ref[...], pmask))
    gqhi, gqlo = split(spread(gq_ref[...], pmask))
    ones = jnp.broadcast_to(pmask[None], (rows, HP, 3 * LANE)).astype(F32).reshape(
        rows * HP, 3 * LANE
    )
    ones = ones.astype(BF)
    qm = spread(query_ref[...].astype(F32), cmask).astype(BF)
    dosm = spread(dos_ref[...].astype(F32), cmask).astype(BF)
    dk = scale * tn(dhi, qm)
    dv = tn(ahi, dosm)
    kpts = tn(dhi, gqhi) + (tn(dhi, gqlo) + tn(dlo, gqhi))
    ksum = tn(dhi, ones) + tn(dlo, ones)
    vpts = tn(ahi, dghi) + (tn(ahi, dglo) + tn(alo, dghi))
    dgk = coef_lane * (kpts - gk_ref[...] * ksum)
    mk = back_rotate(dgk, kcols)
    mv = back_rotate(vpts, kcols)
    width = mine_ref.shape[1]
    single = project(
        [(dk, wk_ref[...]), (dv, wv_ref[...])]
        + [(mk[b][:, :hp], wkp_ref[b * hp : (b + 1) * hp, :]) for b in range(3)]
        + [(mv[b][:, :hp], wvp_ref[b * hp : (b + 1) * hp, :]) for b in range(3)],
        width,
    )
    cols = component_sums(dgk + vpts)
    piece = keys // 8
    core, quarter = place_ref[1], place_ref[2]

    def put(ref, half):
        for n in range(4):
            k = half * 4 + n
            r = pl.multiple_of((n ^ quarter) * (piece + 8), 8)
            ref[pl.ds(r, piece), :] = single[k * piece : (k + 1) * piece]
            r = pl.multiple_of((n ^ quarter) * (piece + 8) + piece, 8)
            ref[pl.ds(r, 8), :] = jnp.concatenate(
                [cols[:8, k * piece : (k + 1) * piece], jnp.zeros((8, width - piece), F32)], axis=1
            )

    @pl.when(core == 0)
    def _():
        put(mine_ref, 0)
        put(other_ref, 1)

    @pl.when(core != 0)
    def _():
        put(mine_ref, 1)
        put(other_ref, 0)


def finish_kernel(
    place_ref,
    q0_ref,
    q1_ref,
    mine_ref,
    other_ref,
    gradq_ref,
    shiftq_ref,
    gradk_ref,
    shiftk_ref,
    shift_ref,
):
    rows = gradq_ref.shape[0]
    keys = gradk_ref.shape[0]
    piece = keys // 8
    total = q0_ref[...] + q1_ref[...]
    gradq_ref[...] = total[:rows].astype(BF)
    shiftq_ref[...] = total[rows : rows + 3, :rows]
    core, quarter = place_ref[1], place_ref[2]

    def put(ref, half):
        parts = []
        for n in range(4):
            k = half * 4 + n
            r = pl.multiple_of((n ^ quarter) * (piece + 8), 8)
            gradk_ref[k * piece : (k + 1) * piece, :] = ref[pl.ds(r, piece), :].astype(BF)
            r = pl.multiple_of((n ^ quarter) * (piece + 8) + piece, 8)
            parts.append(ref[pl.ds(r, 8), 0:piece])
        shift_ref[:, half * 4 * piece : (half + 1) * 4 * piece] = jnp.concatenate(parts, axis=1)

    @pl.when(core == 0)
    def _():
        put(mine_ref, 0)
        put(other_ref, 1)

    @pl.when(core != 0)
    def _():
        put(mine_ref, 1)
        put(other_ref, 0)

    shiftk_ref[...] = shift_ref[0:3, :]


def pair_kernel(both_ref, doz_ref, wb_ref, *refs):
    out_ref = refs[-1]
    rows = both_ref.shape[0]
    whi, wlo = split(math.sqrt(1.0 / 3.0) * padded_bias(wb_ref))

    def one(i, carry):
        both = both_ref[i]
        left = jnp.concatenate([both[:HP], both], axis=0)
        doz = doz_ref[pl.ds(pl.multiple_of(i * HP, HP), HP), :]
        right = jnp.concatenate([wlo, whi, doz], axis=0)
        out_ref[i] = tn(left, right).astype(BF)
        return carry

    lax.fori_loop(0, rows, one, 0, unroll=True)


def pair_part(part, parts, both, doz, w_bias, before, params):
    rows, _, keys = both.shape
    depth = doz.shape[1]
    step = rows // parts
    specs = [
        pl.BlockSpec((step, 2 * HP, keys), lambda g: (part, 0, 0)),
        pl.BlockSpec((step * HP, depth), lambda g: (part, 0)),
        pl.BlockSpec(w_bias.shape, lambda g: (0, 0)),
    ]
    operands = [both, doz, w_bias]
    if before is not None:
        specs.append(pl.BlockSpec(memory_space=pl.ANY))
        operands.append(before)
    return pl.pallas_call(
        pair_kernel,
        grid=(1,),
        out_shape=jax.ShapeDtypeStruct((rows, keys, depth), BF),
        in_specs=specs,
        out_specs=pl.BlockSpec((step, keys, depth), lambda g: (part, 0, 0)),
        input_output_aliases={} if before is None else {3: 0},
        compiler_params=params,
        name="pair_grad",
        cost_estimate=pl.CostEstimate(
            flops=2 * step * keys * depth * 3 * HP,
            bytes_accessed=2 * step * keys * depth,
            transcendentals=0,
        ),
    )(*operands)


def permuted(x, axis, flip):
    size = lax.axis_size(axis)
    return lax.ppermute(x, axis, [(i, i ^ flip) for i in range(size)])


def around(x, hops):
    size = lax.axis_size("col")
    ring = size // 2
    moves = []
    for i in range(size):
        z, low = i // 2, i % 2
        source = (z + (hops if z % 2 else -hops)) % ring
        moves.append((source * 2 + low, i))
    return lax.ppermute(x, "col", moves)


def merged(parts):
    top = functools.reduce(jnp.maximum, [p[:HP] for p in parts])
    total = sum(p[HP:] * jnp.exp(p[:HP] - top) for p in parts)
    return jnp.concatenate([top, total], axis=0)


def body(
    pair,
    single_q,
    single_k,
    w_query,
    w_key,
    w_value,
    w_qpoint,
    w_kpoint,
    w_vpoint,
    w_bias,
    w_out,
    head_gamma,
    chain_bias,
    rot_q,
    trans_q,
    rot_k,
    trans_k,
    chain_q,
    chain_k,
    key_mask,
    cotangent,
):
    rows, keys, depth = pair.shape
    heads = w_bias.shape[1]
    channels = w_query.shape[1] // heads
    npoint = w_qpoint.shape[1] // (3 * heads)
    chans = single_q.shape[1]
    hc = heads * channels
    n = rows * HP
    sds = jax.ShapeDtypeStruct
    params = pltpu.CompilerParams(vmem_limit_bytes=LIMIT)
    wide = 3 * LANE
    km = key_mask.reshape(1, keys)
    w_query, w_key, w_value = w_query.T, w_key.T, w_value.T
    w_qpoint, w_kpoint, w_vpoint = w_qpoint.T, w_kpoint.T, w_vpoint.T
    w_bias = w_bias.T
    frames = [head_gamma.reshape(1, heads), chain_bias.reshape(1, heads)]
    frames += [rot_q, trans_q, rot_k, trans_k, chain_q.reshape(1, rows), chain_k.reshape(1, keys)]
    masked, stats, query, key, gq, gk, qcol, kcol = call(
        functools.partial(logits_kernel, heads, channels, npoint),
        "logits",
        [
            sds((n, keys), F32),
            sds((2 * HP, rows), F32),
            sds((rows, hc), BF),
            sds((keys, hc), BF),
            sds((rows, wide), F32),
            sds((keys, wide), F32),
            sds((LANE, LANE), F32),
            sds((keys, LANE), F32),
        ],
        [],
        [pair],
        [single_q, single_k, w_query, w_key, w_qpoint, w_kpoint, w_bias, *frames, km],
        [
            pltpu.VMEM((rows, keys, depth), BF),
            pltpu.VMEM((LANE, LANE), F32),
            pltpu.VMEM((LANE, keys), F32),
            pltpu.SemaphoreType.DMA((4,)),
        ],
        limit=ALONE,
    )

    first = [stats] + [permuted(stats, "col", f) for f in (1, 2, 3)]
    base, gv, d_os, d_pt, doz = call(
        functools.partial(base_kernel, heads, channels, npoint),
        "base",
        [
            sds((n, keys), F32),
            sds((keys, wide), F32),
            sds((rows, hc), BF),
            sds((rows, 4 * LANE), F32),
            sds((n, depth), BF),
        ],
        [],
        [pair],
        [kcol, single_k, cotangent, w_value, w_vpoint, w_out],
        [
            pltpu.VMEM((rows, keys, depth), BF),
            pltpu.VMEM((n, depth), F32),
            pltpu.SemaphoreType.DMA((4,)),
        ],
        pl.CostEstimate(
            flops=8 * n * keys * wide, bytes_accessed=4 * rows * keys * depth, transcendentals=0
        ),
    )
    stats = merged(first)
    stats = merged([stats] + [around(stats, f) for f in (3, -2, 1)])

    attn, points = call(
        functools.partial(attend_kernel, heads, npoint),
        "attend",
        [sds((n, keys), F32), sds((rows, wide), F32)],
        [],
        [],
        [masked, base, gv, km, stats],
    )
    points = points + sum(permuted(points, "col", f) for f in (1, 2, 3))
    points = points + sum(around(points, f) for f in (1, -2, 3))

    me = lax.axis_index("row")
    place = jnp.stack([lax.axis_index("col"), me % 2, me // 4]).astype(jnp.int32)
    qpart, both, dlo, alo, dglob = call(
        functools.partial(query_kernel, heads, channels, npoint),
        "query_grads",
        [
            sds((rows + 8, chans), F32),
            sds((rows, 2 * HP, keys), BF),
            sds((n, keys), BF),
            sds((n, keys), BF),
            sds((rows, wide), F32),
        ],
        [place],
        [],
        [attn, base, key, gq, gk, gv, d_pt, qcol, points, w_query, w_qpoint],
    )

    moved = permuted(qpart, "col", 1)
    half = sds((keys // 2 + 32, chans), F32)
    mine, other = call(
        functools.partial(key_kernel, heads, channels, npoint),
        "key_grads",
        [half, half],
        [place],
        [],
        [both, dlo, alo, dglob, query, gq, gk, d_os, qcol, kcol, w_key, w_value, w_kpoint, w_vpoint],
        [],
        pl.CostEstimate(
            flops=2 * n * keys * 12 * wide, bytes_accessed=4 * n * keys, transcendentals=0
        ),
    )
    moved, mine, other = lax.optimization_barrier((moved, mine, other))

    qpart = qpart + moved
    mine = mine + permuted(other, "row", 1)
    mine, both = lax.optimization_barrier((mine, both))
    mine = mine.reshape(4, -1, chans)
    held = mine[0] + sum(permuted(mine[f], "row", 4 * f) for f in (1, 2, 3))
    moved = permuted(qpart, "col", 2)
    pair_grad = pair_part(0, 2, both, doz, w_bias, None, params)
    held, both, pair_grad, moved = lax.optimization_barrier((held, both, pair_grad, moved))
    qpart = qpart + moved
    received = permuted(held, "row", 2)
    moved = around(qpart, 1)
    pair_grad = pair_part(1, 2, both, doz, w_bias, pair_grad, params)
    received, moved, pair_grad = lax.optimization_barrier((received, moved, pair_grad))
    held = held + received
    qpart = qpart + moved
    mine = jnp.concatenate([held] + [permuted(held, "row", 4 * f) for f in (1, 2, 3)], axis=0)
    moved = around(qpart, -3)
    mine, moved = lax.optimization_barrier((mine, moved))
    other = permuted(mine, "row", 1)
    grad_q, shift_q, grad_k, shift_k = call(
        finish_kernel,
        "finish",
        [
            sds((rows, chans), BF),
            sds((3, rows), F32),
            sds((keys, chans), BF),
            sds((3, keys), F32),
        ],
        [place],
        [],
        [qpart, moved, mine, other],
        [pltpu.VMEM((8, keys), F32)],
    )
    return pair_grad, grad_q, shift_q, grad_k, shift_k


def solution(mesh):
    placed = (
        P("row", "col", None),
        P("row", None),
        P("col", None),
        P(),
        P(),
        P(),
        P(),
        P(),
        P(),
        P(),
        P(),
        P(),
        P(),
        P(None, "row"),
        P(None, "row"),
        P(None, "col"),
        P(None, "col"),
        P("row"),
        P("col"),
        P("col"),
        P("row", None),
    )
    return jax.shard_map(
        body,
        mesh=mesh,
        in_specs=placed,
        out_specs=(
            P("row", "col", None),
            P("row", None),
            P(None, "row"),
            P("col", None),
            P(None, "col"),
        ),
        check_vma=False,
    )
```

```python
import functools
import math

import jax
import jax.numpy as jnp
from jax import lax
from jax.experimental import pallas as pl
from jax.experimental.pallas import tpu as pltpu
from jax.sharding import PartitionSpec as P

HIGH = lax.Precision.HIGHEST
F32 = jnp.float32
BF = jnp.bfloat16
HP = 16
LANE = 128
NEG = -1e30
LIMIT = 24 * 1024 * 1024
ALONE = 56 * 1024 * 1024


VMEM = pl.BlockSpec(memory_space=pltpu.VMEM)
SMEM = pl.BlockSpec(memory_space=pltpu.SMEM)
ANY = pl.BlockSpec(memory_space=pl.ANY)


def call(kernel, name, outs, smem, hbm, vmem, scratch=(), cost=None, limit=LIMIT):
    return pl.pallas_call(
        kernel,
        out_shape=outs,
        in_specs=[SMEM] * len(smem) + [ANY] * len(hbm) + [VMEM] * len(vmem),
        out_specs=[VMEM] * len(outs),
        scratch_shapes=list(scratch),
        compiler_params=pltpu.CompilerParams(vmem_limit_bytes=limit),
        name=name,
        cost_estimate=cost,
    )(*smem, *hbm, *vmem)


def nn(a, b, precision=None):
    return lax.dot_general(
        a, b, (((1,), (0,)), ((), ())), preferred_element_type=F32, precision=precision
    )


def nt(a, b, precision=None):
    return lax.dot_general(
        a, b, (((1,), (1,)), ((), ())), preferred_element_type=F32, precision=precision
    )


def tn(a, b, precision=None):
    return lax.dot_general(
        a, b, (((0,), (0,)), ((), ())), preferred_element_type=F32, precision=precision
    )


def split(x):
    hi = x.astype(BF)
    return hi, (x - hi.astype(F32)).astype(BF)


def iota(shape, axis):
    return lax.broadcasted_iota(jnp.int32, shape, axis)


def head_mask(heads, npoint, width):
    lane = iota((HP, width), 1) % LANE
    row = iota((HP, width), 0)
    return (lane // npoint == row) & (lane < heads * npoint)


def channel_mask(heads, channels):
    lane = iota((HP, heads * channels), 1)
    return lane // channels == iota((HP, heads * channels), 0)


def spread(x, mask):
    n, w = x.shape
    wide = jnp.broadcast_to(x[:, None, :], (n, HP, w))
    return jnp.where(mask[None], wide, jnp.zeros((), x.dtype)).reshape(n * HP, w)


def gather_heads(x, mask):
    w = x.shape[1]
    full = jnp.where(mask[None], x.reshape(-1, HP, w), 0.0)
    return jnp.sum(full, axis=1)


def to_lanes(col, offset=0):
    n = col.shape[0] // HP
    mask = iota((HP, LANE), 1) == iota((HP, LANE), 0) + offset
    wide = jnp.broadcast_to(col, (n * HP, LANE)).reshape(n, HP, LANE)
    return jnp.sum(jnp.where(mask[None], wide, 0.0), axis=1)


def to_col(x, offset=0):
    n = x.shape[0]
    mask = iota((HP, LANE), 1) == iota((HP, LANE), 0) + offset
    wide = jnp.broadcast_to(x[:, None, :], (n, HP, LANE))
    return jnp.sum(jnp.where(mask[None], wide, 0.0), axis=2, keepdims=True).reshape(n * HP, 1)


def pad_lanes(x, width=LANE):
    n, w = x.shape
    return jnp.concatenate([x, jnp.zeros((n, width - w), x.dtype)], axis=1)


def rotate_points(local, cols, hp):
    parts = [local[:, b * hp : (b + 1) * hp] for b in range(3)]
    out = []
    for a in range(3):
        g = cols[:, 9 + a : 10 + a]
        g = g + sum(cols[:, 3 * a + b : 3 * a + b + 1] * parts[b] for b in range(3))
        out.append(pad_lanes(g))
    return jnp.concatenate(out, axis=1)


def back_rotate(x, cols):
    parts = [x[:, a * LANE : (a + 1) * LANE] for a in range(3)]
    return [sum(cols[:, 3 * a + b : 3 * a + b + 1] * parts[a] for a in range(3)) for b in range(3)]


def load_pair(pair_hbm, pair_ref, sems):
    nchunk = sems.shape[0]
    step = pair_hbm.shape[0] // nchunk
    copies = [
        pltpu.make_async_copy(
            pair_hbm.at[pl.ds(c * step, step)], pair_ref.at[pl.ds(c * step, step)], sems.at[c]
        )
        for c in range(nchunk)
    ]
    for copy in copies:
        copy.start()
    return copies, step


def padded_bias(wb_ref):
    heads, depth = wb_ref.shape
    return jnp.concatenate([wb_ref[...].astype(F32), jnp.zeros((HP - heads, depth), F32)], axis=0)


class packing:
    def __init__(self, rows, keys, hc):
        first = keys + rows
        second = first + LANE
        self.shape = (second + keys, 3 * LANE)
        self.gk = (slice(0, keys), slice(0, 3 * LANE))
        self.gq = (slice(keys, first), slice(0, 3 * LANE))
        self.qcol = (slice(first, second), slice(0, LANE))
        self.query = (slice(first, first + rows), slice(LANE, LANE + hc))
        self.key = (slice(second, second + keys), slice(0, hc))
        self.kcol = (slice(second, second + keys), slice(2 * LANE, 3 * LANE))


class value_packing:
    def __init__(self, rows, keys, hc):
        first = keys + rows
        self.shape = (first + rows, 3 * LANE)
        self.gv = (slice(0, keys), slice(0, 3 * LANE))
        self.dol = [(slice(keys, first), slice(b * LANE, (b + 1) * LANE)) for b in range(3)]
        self.don = (slice(first, first + rows), slice(0, LANE))
        self.dos = (slice(first, first + rows), slice(LANE, LANE + hc))


def logits_kernel(
    heads,
    channels,
    npoint,
    pair_hbm,
    sq_ref,
    sk_ref,
    wq_ref,
    wk_ref,
    wqp_ref,
    wkp_ref,
    wb_ref,
    gamma_ref,
    chainb_ref,
    rotq_ref,
    trq_ref,
    rotk_ref,
    trk_ref,
    cq_ref,
    ck_ref,
    km_ref,
    masked_ref,
    stats_ref,
    pack_ref,
    pair_ref,
    tq_ref,
    tk_ref,
    sems,
):
    rows, keys, depth = pair_hbm.shape
    hp = heads * npoint
    copies, step = load_pair(pair_hbm, pair_ref, sems)
    place = packing(rows, keys, channels * heads)
    w_logit = math.sqrt(1.0 / 3.0)
    w_point = math.sqrt(2.0 / (9.0 * npoint))
    tq_ref[...] = jnp.zeros_like(tq_ref)
    tq_ref[0:9, 0:rows] = rotq_ref[...]
    tq_ref[9:12, 0:rows] = trq_ref[...]
    tq_ref[12:13, 0:rows] = cq_ref[...].astype(F32)
    tq_ref[13:14, 0:heads] = gamma_ref[...]
    tq_ref[14:15, 0:heads] = chainb_ref[...]
    qcols_all = tq_ref[...].T
    qcols = qcols_all[:rows]
    head_cols = qcols_all[:HP]
    pack_ref[place.qcol] = qcols_all
    tk_ref[...] = jnp.zeros_like(tk_ref)
    tk_ref[0:9, :] = rotk_ref[...]
    tk_ref[9:12, :] = trk_ref[...]
    kcols = tk_ref[...].T
    pack_ref[place.kcol] = kcols

    sq = sq_ref[...]
    sk = sk_ref[...]
    query = nt(sq, wq_ref[...]).astype(BF)
    key = nt(sk, wk_ref[...]).astype(BF)
    pack_ref[place.query] = query.astype(F32)
    pack_ref[place.key] = key.astype(F32)
    gq = rotate_points(nt(sq, wqp_ref[...]), qcols, hp)
    gk = rotate_points(nt(sk, wkp_ref[...]), kcols, hp)
    pack_ref[place.gq] = gq
    pack_ref[place.gk] = gk

    pmask = head_mask(heads, npoint, 3 * LANE)
    cmask = channel_mask(heads, channels)
    gqm = spread(gq, pmask)
    cross = nt(gqm, gk, HIGH)
    sqq = jnp.sum(gqm * gqm, axis=1, keepdims=True)
    sqk = nt(pmask.astype(F32), gk * gk, HIGH)
    qk = nt(spread(query.astype(F32), cmask).astype(BF), key)
    coef = (w_logit * w_point) * head_cols[:, 13:14]
    same = (qcols[:, 12:13] == ck_ref[...].astype(F32)).astype(F32)
    shape = (rows, HP, keys)
    dist = (sqq.reshape(rows, HP, 1) + sqk[None]) - 2.0 * cross.reshape(shape)
    inner = qk.reshape(shape) * (1.0 / math.sqrt(channels)) + head_cols[:, 14:15][
        None
    ] * jnp.broadcast_to(same[:, None, :], shape)
    logit = w_logit * inner - (0.5 * coef)[None] * dist
    masked_ref[...] = logit.reshape(rows * HP, keys)

    wbt = padded_bias(wb_ref).astype(BF)
    for c, copy in enumerate(copies):
        copy.wait()

        def one(i, carry):
            r = pl.multiple_of(i * HP, HP)
            masked_ref[pl.ds(r, HP), :] += w_logit * nt(wbt, pair_ref[i])
            return carry

        lax.fori_loop(c * step, (c + 1) * step, one, 0, unroll=16)

    valid = (km_ref[...] == 1)[None]
    masked = jnp.where(valid, masked_ref[...].reshape(shape), NEG)
    top = jnp.max(masked, axis=2, keepdims=True)
    total = jnp.sum(jnp.where(valid, jnp.exp(masked - top), 0.0), axis=2, keepdims=True)
    masked_ref[...] = masked.reshape(rows * HP, keys)
    packed = to_lanes(top.reshape(rows * HP, 1)) + to_lanes(total.reshape(rows * HP, 1), HP)
    stats_ref[...] = packed.T[: 2 * HP]


def base_kernel(
    heads,
    channels,
    npoint,
    pair_hbm,
    pack_ref,
    sk_ref,
    cot_ref,
    wv_ref,
    wvp_ref,
    wout_ref,
    base_ref,
    vals_ref,
    doz_ref,
    pair_ref,
    lhs_ref,
    sems,
):
    rows, keys, depth = pair_hbm.shape
    hp = heads * npoint
    copies, step = load_pair(pair_hbm, pair_ref, sems)
    sk = sk_ref[...]
    cot = cot_ref[...]
    value = nt(sk, wv_ref[...]).astype(BF)
    nos = heads * channels
    place = value_packing(rows, keys, nos)
    kcols = pack_ref[packing(rows, keys, nos).kcol]
    vals_ref[place.gv] = rotate_points(nt(sk, wvp_ref[...]), kcols, hp)
    first = nos + heads * depth
    dos = nt(cot, wout_ref[0:nos, :]).astype(BF)
    vals_ref[place.dos] = dos.astype(F32)
    for b in range(4):
        d = nt(cot, wout_ref[first + b * hp : first + (b + 1) * hp, :]).astype(BF).astype(F32)
        vals_ref[(place.dol + [place.don])[b]] = pad_lanes(d)
    doz = nt(cot, wout_ref[nos:first, :]).astype(BF).astype(F32)
    lhs_ref[...] = jnp.zeros_like(lhs_ref)
    for h in range(heads):
        lhs_ref[pl.ds(h, rows, stride=HP), :] = doz[:, h * depth : (h + 1) * depth]
    doz_ref[...] = lhs_ref[...].astype(BF)
    dosm = spread(dos.astype(F32), channel_mask(heads, channels)).astype(BF)
    base_ref[...] = nt(dosm, value)
    for c, copy in enumerate(copies):
        copy.wait()

        def one(i, carry):
            r = pl.multiple_of(i * HP, HP)
            base_ref[pl.ds(r, HP), :] += nt(doz_ref[pl.ds(r, HP), :], pair_ref[i])
            return carry

        lax.fori_loop(c * step, (c + 1) * step, one, 0, unroll=16)


def attend_kernel(
    heads,
    npoint,
    masked_ref,
    base_ref,
    vals_ref,
    km_ref,
    stats_ref,
    attn_ref,
    out_ref,
):
    rows = stats_ref.shape[1]
    stats = jnp.concatenate(
        [stats_ref[...], jnp.zeros((LANE - stats_ref.shape[0], rows), F32)], axis=0
    ).T
    top = to_col(stats)
    total = to_col(stats, HP)
    valid = km_ref[...] == 1
    attn = jnp.where(valid, jnp.exp(masked_ref[...] - top), 0.0) / total
    attn_ref[...] = attn
    attn_b = attn.astype(BF)
    attn_f = attn_b.astype(F32)
    ghi, glo = split(vals_ref[0 : masked_ref.shape[1], :])
    opt = nn(attn_b, ghi) + nn(attn_b, glo)
    pmask = head_mask(heads, npoint, 3 * LANE)
    delta = jnp.sum(attn_f * base_ref[...], axis=1, keepdims=True)
    out_ref[...] = gather_heads(opt, pmask)
    out_ref[:, 0:LANE] += to_lanes(delta, heads * npoint)


def frames_of(heads, npoint, qall, rows):
    pmask = head_mask(heads, npoint, 3 * LANE)
    w_logit = math.sqrt(1.0 / 3.0)
    w_point = math.sqrt(2.0 / (9.0 * npoint))
    coef = (w_logit * w_point) * qall[:HP, 13:14]
    coef_lane = jnp.sum(jnp.where(pmask, coef, 0.0), axis=0, keepdims=True)
    return pmask, qall[:rows], coef_lane


def project(parts, width):
    single = jnp.zeros((parts[0][0].shape[0], width), F32)
    for part, weight in parts:
        phi, plo = split(part)
        single = single + (nn(phi, weight) + nn(plo, weight))
    return single


def component_sums(x):
    n = x.shape[0]
    cols = [jnp.sum(x[:, a * LANE : (a + 1) * LANE], axis=1, keepdims=True) for a in range(3)]
    return jnp.concatenate(cols + [jnp.zeros((n, LANE - 3), F32)], axis=1).T


def query_kernel(
    heads,
    channels,
    npoint,
    place_ref,
    attn_ref,
    base_ref,
    pack_ref,
    vals_ref,
    psum_ref,
    wq_ref,
    wqp_ref,
    qout_ref,
    both_ref,
    dlo_ref,
    alo_ref,
    dglob_ref,
):
    rows, keys = psum_ref.shape[0], base_ref.shape[1]
    place = packing(rows, keys, heads * channels)
    vplace = value_packing(rows, keys, heads * channels)
    hp = heads * npoint
    scale = math.sqrt(1.0 / 3.0) / math.sqrt(channels)
    cmask = channel_mask(heads, channels)
    pmask, qcols, coef_lane = frames_of(heads, npoint, pack_ref[place.qcol], rows)
    inside = iota((1, LANE), 1) < hp

    psum = psum_ref[...]
    delta0 = to_col(psum[:, :LANE], hp)
    opt = [jnp.where(inside, psum[:, a * LANE : (a + 1) * LANE], 0.0) for a in range(3)]
    moved = [jnp.where(inside, opt[a] - qcols[:, 9 + a : 10 + a], 0.0) for a in range(3)]
    oloc = back_rotate(jnp.concatenate(moved, axis=1), qcols)
    onorm = jnp.sqrt(1.0 + (oloc[0] * oloc[0] + oloc[1] * oloc[1] + oloc[2] * oloc[2]))
    ratio = vals_ref[vplace.don] / onorm
    dloc = [vals_ref[vplace.dol[b]] + ratio * oloc[b] for b in range(3)]
    dglob = jnp.concatenate(
        [
            sum(qcols[:, 3 * a + b : 3 * a + b + 1] * dloc[b] for b in range(3))
            for a in range(3)
        ],
        axis=1,
    )
    dglob_ref[...] = dglob
    dghi, dglo = split(spread(dglob, pmask))
    opt_row = jnp.concatenate(opt, axis=1)
    delta = delta0 + jnp.sum(spread(opt_row * dglob, pmask), axis=1, keepdims=True)
    gvhi, gvlo = split(vals_ref[vplace.gv])
    dattn = base_ref[...] + nt(dghi, gvhi) + (nt(dghi, gvlo) + nt(dglo, gvhi))
    attn = attn_ref[...]
    dlogit = attn * (dattn - delta)
    dhi, dlo = split(dlogit)
    ahi, alo = split(attn)
    both_ref[:, 0:HP, :] = dhi.reshape(rows, HP, keys)
    both_ref[:, HP : 2 * HP, :] = ahi.reshape(rows, HP, keys)
    dlo_ref[...] = dlo
    alo_ref[...] = alo

    gkhi, gklo = split(pack_ref[place.gk])
    dq = scale * gather_heads(nn(dhi, pack_ref[place.key].astype(BF)), cmask)
    qpts = gather_heads(nn(dhi, gkhi) + (nn(dhi, gklo) + nn(dlo, gkhi)), pmask)
    qsum = jnp.sum(dlogit, axis=1, keepdims=True)
    qsum_lane = gather_heads(jnp.broadcast_to(qsum, (rows * HP, 3 * LANE)), pmask)
    dgq = coef_lane * (qpts - pack_ref[place.gq] * qsum_lane)
    mq = back_rotate(dgq, qcols)
    width = qout_ref.shape[1]
    qout_ref[0:rows, :] = project(
        [(dq, wq_ref[...])]
        + [(mq[b][:, :hp], wqp_ref[b * hp : (b + 1) * hp, :]) for b in range(3)],
        width,
    )
    shift = jnp.where(place_ref[0] == 0, dgq - dglob, dgq)
    qout_ref[rows:, :] = jnp.zeros((qout_ref.shape[0] - rows, width), F32)
    qout_ref[rows : rows + 8, 0:rows] = component_sums(shift)[:8, :rows]


def key_kernel(
    heads,
    channels,
    npoint,
    place_ref,
    both_ref,
    dlo_ref,
    alo_ref,
    dglob_ref,
    pack_ref,
    vals_ref,
    wk_ref,
    wv_ref,
    wkp_ref,
    wvp_ref,
    mine_ref,
    other_ref,
):
    rows, keys = dglob_ref.shape[0], dlo_ref.shape[1]
    place = packing(rows, keys, heads * channels)
    vplace = value_packing(rows, keys, heads * channels)
    hp = heads * npoint
    scale = math.sqrt(1.0 / 3.0) / math.sqrt(channels)
    cmask = channel_mask(heads, channels)
    pmask, qcols, coef_lane = frames_of(heads, npoint, pack_ref[place.qcol], rows)
    kcols = pack_ref[place.kcol]
    dhi = both_ref[:, 0:HP, :].reshape(rows * HP, keys)
    ahi = both_ref[:, HP : 2 * HP, :].reshape(rows * HP, keys)
    dlo, alo = dlo_ref[...], alo_ref[...]
    dghi, dglo = split(spread(dglob_ref[...], pmask))
    gqhi, gqlo = split(spread(pack_ref[place.gq], pmask))
    ones = jnp.broadcast_to(pmask[None], (rows, HP, 3 * LANE)).astype(F32).reshape(
        rows * HP, 3 * LANE
    )
    ones = ones.astype(BF)
    qm = spread(pack_ref[place.query], cmask).astype(BF)
    dosm = spread(vals_ref[vplace.dos], cmask).astype(BF)
    dk = scale * tn(dhi, qm)
    dv = tn(ahi, dosm)
    kpts = tn(dhi, gqhi) + (tn(dhi, gqlo) + tn(dlo, gqhi))
    ksum = tn(dhi, ones) + tn(dlo, ones)
    vpts = tn(ahi, dghi) + (tn(ahi, dglo) + tn(alo, dghi))
    dgk = coef_lane * (kpts - pack_ref[place.gk] * ksum)
    mk = back_rotate(dgk, kcols)
    mv = back_rotate(vpts, kcols)
    width = mine_ref.shape[1]
    single = project(
        [(dk, wk_ref[...]), (dv, wv_ref[...])]
        + [(mk[b][:, :hp], wkp_ref[b * hp : (b + 1) * hp, :]) for b in range(3)]
        + [(mv[b][:, :hp], wvp_ref[b * hp : (b + 1) * hp, :]) for b in range(3)],
        width,
    )
    cols = component_sums(dgk + vpts)
    piece = keys // 8
    core, quarter = place_ref[1], place_ref[2]

    def put(ref, half):
        for n in range(4):
            k = half * 4 + n
            r = pl.multiple_of((n ^ quarter) * (piece + 8), 8)
            ref[pl.ds(r, piece), :] = single[k * piece : (k + 1) * piece]
            r = pl.multiple_of((n ^ quarter) * (piece + 8) + piece, 8)
            ref[pl.ds(r, 8), :] = jnp.concatenate(
                [cols[:8, k * piece : (k + 1) * piece], jnp.zeros((8, width - piece), F32)], axis=1
            )

    @pl.when(core == 0)
    def _():
        put(mine_ref, 0)
        put(other_ref, 1)

    @pl.when(core != 0)
    def _():
        put(mine_ref, 1)
        put(other_ref, 0)


def finish_kernel(
    place_ref,
    q0_ref,
    q1_ref,
    mine_ref,
    other_ref,
    gradq_ref,
    shiftq_ref,
    gradk_ref,
    shiftk_ref,
    shift_ref,
):
    rows = gradq_ref.shape[0]
    keys = gradk_ref.shape[0]
    piece = keys // 8
    total = q0_ref[...] + q1_ref[...]
    gradq_ref[...] = total[:rows].astype(BF)
    shiftq_ref[...] = total[rows : rows + 3, :rows]
    core, quarter = place_ref[1], place_ref[2]

    def put(ref, half):
        parts = []
        for n in range(4):
            k = half * 4 + n
            r = pl.multiple_of((n ^ quarter) * (piece + 8), 8)
            gradk_ref[k * piece : (k + 1) * piece, :] = ref[pl.ds(r, piece), :].astype(BF)
            r = pl.multiple_of((n ^ quarter) * (piece + 8) + piece, 8)
            parts.append(ref[pl.ds(r, 8), 0:piece])
        shift_ref[:, half * 4 * piece : (half + 1) * 4 * piece] = jnp.concatenate(parts, axis=1)

    @pl.when(core == 0)
    def _():
        put(mine_ref, 0)
        put(other_ref, 1)

    @pl.when(core != 0)
    def _():
        put(mine_ref, 1)
        put(other_ref, 0)

    shiftk_ref[...] = shift_ref[0:3, :]


def pair_kernel(both_ref, doz_ref, wb_ref, *refs):
    out_ref = refs[-1]
    rows = both_ref.shape[0]
    whi, wlo = split(math.sqrt(1.0 / 3.0) * padded_bias(wb_ref))

    def one(i, carry):
        both = both_ref[i]
        left = jnp.concatenate([both[:HP], both], axis=0)
        doz = doz_ref[pl.ds(pl.multiple_of(i * HP, HP), HP), :]
        right = jnp.concatenate([wlo, whi, doz], axis=0)
        out_ref[i] = tn(left, right).astype(BF)
        return carry

    lax.fori_loop(0, rows, one, 0, unroll=True)


def pair_part(part, parts, both, doz, w_bias, before, params):
    rows, _, keys = both.shape
    depth = doz.shape[1]
    step = rows // parts
    specs = [
        pl.BlockSpec((step, 2 * HP, keys), lambda g: (part, 0, 0)),
        pl.BlockSpec((step * HP, depth), lambda g: (part, 0)),
        pl.BlockSpec(w_bias.shape, lambda g: (0, 0)),
    ]
    operands = [both, doz, w_bias]
    if before is not None:
        specs.append(pl.BlockSpec(memory_space=pl.ANY))
        operands.append(before)
    return pl.pallas_call(
        pair_kernel,
        grid=(1,),
        out_shape=jax.ShapeDtypeStruct((rows, keys, depth), BF),
        in_specs=specs,
        out_specs=pl.BlockSpec((step, keys, depth), lambda g: (part, 0, 0)),
        input_output_aliases={} if before is None else {3: 0},
        compiler_params=params,
        name="pair_grad",
        cost_estimate=pl.CostEstimate(
            flops=2 * step * keys * depth * 3 * HP,
            bytes_accessed=2 * step * keys * depth,
            transcendentals=0,
        ),
    )(*operands)


def permuted(x, axis, flip):
    size = lax.axis_size(axis)
    return lax.ppermute(x, axis, [(i, i ^ flip) for i in range(size)])


def around(x, hops):
    size = lax.axis_size("col")
    ring = size // 2
    moves = []
    for i in range(size):
        z, low = i // 2, i % 2
        source = (z + (hops if z % 2 else -hops)) % ring
        moves.append((source * 2 + low, i))
    return lax.ppermute(x, "col", moves)


def merged(parts):
    top = functools.reduce(jnp.maximum, [p[:HP] for p in parts])
    total = sum(p[HP:] * jnp.exp(p[:HP] - top) for p in parts)
    return jnp.concatenate([top, total], axis=0)


def body(
    pair,
    single_q,
    single_k,
    w_query,
    w_key,
    w_value,
    w_qpoint,
    w_kpoint,
    w_vpoint,
    w_bias,
    w_out,
    head_gamma,
    chain_bias,
    rot_q,
    trans_q,
    rot_k,
    trans_k,
    chain_q,
    chain_k,
    key_mask,
    cotangent,
):
    rows, keys, depth = pair.shape
    heads = w_bias.shape[1]
    channels = w_query.shape[1] // heads
    npoint = w_qpoint.shape[1] // (3 * heads)
    chans = single_q.shape[1]
    hc = heads * channels
    n = rows * HP
    sds = jax.ShapeDtypeStruct
    params = pltpu.CompilerParams(vmem_limit_bytes=LIMIT)
    wide = 3 * LANE
    km = key_mask.reshape(1, keys)
    w_query, w_key, w_value = w_query.T, w_key.T, w_value.T
    w_qpoint, w_kpoint, w_vpoint = w_qpoint.T, w_kpoint.T, w_vpoint.T
    w_bias = w_bias.T
    frames = [head_gamma.reshape(1, heads), chain_bias.reshape(1, heads)]
    frames += [rot_q, trans_q, rot_k, trans_k, chain_q.reshape(1, rows), chain_k.reshape(1, keys)]
    inputs = [single_q, single_k, w_query, w_key, w_qpoint, w_kpoint, w_bias, *frames, km]
    masked, stats, pack = call(
        functools.partial(logits_kernel, heads, channels, npoint),
        "logits",
        [
            sds((n, keys), F32),
            sds((2 * HP, rows), F32),
            sds(packing(rows, keys, hc).shape, F32),
        ],
        [],
        [pair],
        inputs,
        [
            pltpu.VMEM((rows, keys, depth), BF),
            pltpu.VMEM((LANE, LANE), F32),
            pltpu.VMEM((LANE, keys), F32),
            pltpu.SemaphoreType.DMA((1,)),
        ],
        limit=ALONE,
    )

    first = [stats] + [permuted(stats, "col", f) for f in (1, 2, 3)]
    base, vals, doz = call(
        functools.partial(base_kernel, heads, channels, npoint),
        "base",
        [
            sds((n, keys), F32),
            sds(value_packing(rows, keys, hc).shape, F32),
            sds((n, depth), BF),
        ],
        [],
        [pair],
        [pack, single_k, cotangent, w_value, w_vpoint, w_out],
        [
            pltpu.VMEM((rows, keys, depth), BF),
            pltpu.VMEM((n, depth), F32),
            pltpu.SemaphoreType.DMA((1,)),
        ],
        pl.CostEstimate(
            flops=8 * n * keys * wide, bytes_accessed=4 * rows * keys * depth, transcendentals=0
        ),
    )
    stats = merged(first)
    stats = merged([stats] + [around(stats, f) for f in (3, -2, 1)])

    attn, points = call(
        functools.partial(attend_kernel, heads, npoint),
        "attend",
        [sds((n, keys), F32), sds((rows, wide), F32)],
        [],
        [],
        [masked, base, vals, km, stats],
    )
    points = points + sum(permuted(points, "col", f) for f in (1, 2, 3))
    points = points + sum(around(points, f) for f in (1, -2, 3))

    me = lax.axis_index("row")
    place = jnp.stack([lax.axis_index("col"), me % 2, me // 4]).astype(jnp.int32)
    qpart, both, dlo, alo, dglob = call(
        functools.partial(query_kernel, heads, channels, npoint),
        "query_grads",
        [
            sds((rows + 8, chans), F32),
            sds((rows, 2 * HP, keys), BF),
            sds((n, keys), BF),
            sds((n, keys), BF),
            sds((rows, wide), F32),
        ],
        [place],
        [],
        [attn, base, pack, vals, points, w_query, w_qpoint],
    )

    moved = permuted(qpart, "col", 1)
    half = sds((keys // 2 + 32, chans), F32)
    mine, other = call(
        functools.partial(key_kernel, heads, channels, npoint),
        "key_grads",
        [half, half],
        [place],
        [],
        [both, dlo, alo, dglob, pack, vals, w_key, w_value, w_kpoint, w_vpoint],
        [],
        pl.CostEstimate(
            flops=2 * n * keys * 12 * wide, bytes_accessed=4 * n * keys, transcendentals=0
        ),
    )
    moved, mine, other = lax.optimization_barrier((moved, mine, other))

    qpart = qpart + moved
    mine = mine + permuted(other, "row", 1)
    mine, both = lax.optimization_barrier((mine, both))
    mine = mine.reshape(4, -1, chans)
    held = mine[0] + sum(permuted(mine[f], "row", 4 * f) for f in (1, 2, 3))
    moved = permuted(qpart, "col", 2)
    pair_grad = pair_part(0, 2, both, doz, w_bias, None, params)
    held, both, pair_grad, moved = lax.optimization_barrier((held, both, pair_grad, moved))
    qpart = qpart + moved
    received = permuted(held, "row", 2)
    moved = around(qpart, 1)
    pair_grad = pair_part(1, 2, both, doz, w_bias, pair_grad, params)
    received, moved, pair_grad = lax.optimization_barrier((received, moved, pair_grad))
    held = held + received
    qpart = qpart + moved
    mine = jnp.concatenate([held] + [permuted(held, "row", 4 * f) for f in (1, 2, 3)], axis=0)
    moved = around(qpart, -3)
    mine, moved = lax.optimization_barrier((mine, moved))
    other = permuted(mine, "row", 1)
    grad_q, shift_q, grad_k, shift_k = call(
        finish_kernel,
        "finish",
        [
            sds((rows, chans), BF),
            sds((3, rows), F32),
            sds((keys, chans), BF),
            sds((3, keys), F32),
        ],
        [place],
        [],
        [qpart, moved, mine, other],
        [pltpu.VMEM((8, keys), F32)],
    )
    return pair_grad, grad_q, shift_q, grad_k, shift_k


def solution(mesh):
    placed = (
        P("row", "col", None),
        P("row", None),
        P("col", None),
        P(),
        P(),
        P(),
        P(),
        P(),
        P(),
        P(),
        P(),
        P(),
        P(),
        P(None, "row"),
        P(None, "row"),
        P(None, "col"),
        P(None, "col"),
        P("row"),
        P("col"),
        P("col"),
        P("row", None),
    )
    return jax.shard_map(
        body,
        mesh=mesh,
        in_specs=placed,
        out_specs=(
            P("row", "col", None),
            P("row", None),
            P(None, "row"),
            P("col", None),
            P(None, "col"),
        ),
        check_vma=False,
    )
```

```python
import functools
import math

import jax
import jax.numpy as jnp
from jax import lax
from jax.experimental import pallas as pl
from jax.experimental.pallas import tpu as pltpu
from jax.sharding import PartitionSpec as P

HIGH = lax.Precision.HIGHEST
F32 = jnp.float32
BF = jnp.bfloat16
HP = 16
LANE = 128
NEG = -1e30
LIMIT = 24 * 1024 * 1024
ALONE = 56 * 1024 * 1024


VMEM = pl.BlockSpec(memory_space=pltpu.VMEM)
SMEM = pl.BlockSpec(memory_space=pltpu.SMEM)
ANY = pl.BlockSpec(memory_space=pl.ANY)


def call(kernel, name, outs, smem, hbm, vmem, scratch=(), cost=None, limit=LIMIT):
    return pl.pallas_call(
        kernel,
        out_shape=outs,
        in_specs=[SMEM] * len(smem) + [ANY] * len(hbm) + [VMEM] * len(vmem),
        out_specs=[VMEM] * len(outs),
        scratch_shapes=list(scratch),
        compiler_params=pltpu.CompilerParams(vmem_limit_bytes=limit),
        name=name,
        cost_estimate=cost,
    )(*smem, *hbm, *vmem)


def nn(a, b, precision=None):
    return lax.dot_general(
        a, b, (((1,), (0,)), ((), ())), preferred_element_type=F32, precision=precision
    )


def nt(a, b, precision=None):
    return lax.dot_general(
        a, b, (((1,), (1,)), ((), ())), preferred_element_type=F32, precision=precision
    )


def tn(a, b, precision=None):
    return lax.dot_general(
        a, b, (((0,), (0,)), ((), ())), preferred_element_type=F32, precision=precision
    )


def split(x):
    hi = x.astype(BF)
    return hi, (x - hi.astype(F32)).astype(BF)


def iota(shape, axis):
    return lax.broadcasted_iota(jnp.int32, shape, axis)


def head_mask(heads, npoint, width):
    lane = iota((HP, width), 1) % LANE
    row = iota((HP, width), 0)
    return (lane // npoint == row) & (lane < heads * npoint)


def channel_mask(heads, channels):
    lane = iota((HP, heads * channels), 1)
    return lane // channels == iota((HP, heads * channels), 0)


def spread(x, mask):
    n, w = x.shape
    wide = jnp.broadcast_to(x[:, None, :], (n, HP, w))
    return jnp.where(mask[None], wide, jnp.zeros((), x.dtype)).reshape(n * HP, w)


def gather_heads(x, mask):
    w = x.shape[1]
    full = jnp.where(mask[None], x.reshape(-1, HP, w), 0.0)
    return jnp.sum(full, axis=1)


def to_lanes(col, offset=0):
    n = col.shape[0] // HP
    mask = iota((HP, LANE), 1) == iota((HP, LANE), 0) + offset
    wide = jnp.broadcast_to(col, (n * HP, LANE)).reshape(n, HP, LANE)
    return jnp.sum(jnp.where(mask[None], wide, 0.0), axis=1)


def to_col(x, offset=0):
    n = x.shape[0]
    mask = iota((HP, LANE), 1) == iota((HP, LANE), 0) + offset
    wide = jnp.broadcast_to(x[:, None, :], (n, HP, LANE))
    return jnp.sum(jnp.where(mask[None], wide, 0.0), axis=2, keepdims=True).reshape(n * HP, 1)


def pad_lanes(x, width=LANE):
    n, w = x.shape
    return jnp.concatenate([x, jnp.zeros((n, width - w), x.dtype)], axis=1)


def rotate_points(local, cols, hp):
    parts = [local[:, b * hp : (b + 1) * hp] for b in range(3)]
    out = []
    for a in range(3):
        g = cols[:, 9 + a : 10 + a]
        g = g + sum(cols[:, 3 * a + b : 3 * a + b + 1] * parts[b] for b in range(3))
        out.append(pad_lanes(g))
    return jnp.concatenate(out, axis=1)


def back_rotate(x, cols):
    parts = [x[:, a * LANE : (a + 1) * LANE] for a in range(3)]
    return [sum(cols[:, 3 * a + b : 3 * a + b + 1] * parts[a] for a in range(3)) for b in range(3)]


def load_pair(pair_hbm, pair_ref, sems):
    nchunk = sems.shape[0]
    step = pair_hbm.shape[0] // nchunk
    copies = [
        pltpu.make_async_copy(
            pair_hbm.at[pl.ds(c * step, step)], pair_ref.at[pl.ds(c * step, step)], sems.at[c]
        )
        for c in range(nchunk)
    ]
    for copy in copies:
        copy.start()
    return copies, step


def padded_bias(wb_ref):
    heads, depth = wb_ref.shape
    return jnp.concatenate([wb_ref[...].astype(F32), jnp.zeros((HP - heads, depth), F32)], axis=0)


class packing:
    def __init__(self, rows, keys, hc):
        first = keys + rows
        second = first + LANE
        self.shape = (second + keys, 3 * LANE)
        self.gk = (slice(0, keys), slice(0, 3 * LANE))
        self.gq = (slice(keys, first), slice(0, 3 * LANE))
        self.qcol = (slice(first, second), slice(0, LANE))
        self.query = (slice(first, first + rows), slice(LANE, LANE + hc))
        self.key = (slice(second, second + keys), slice(0, hc))
        self.kcol = (slice(second, second + keys), slice(2 * LANE, 3 * LANE))


class value_packing:
    def __init__(self, rows, keys, hc):
        first = keys + rows
        self.shape = (first + rows, 3 * LANE)
        self.gv = (slice(0, keys), slice(0, 3 * LANE))
        self.dol = [(slice(keys, first), slice(b * LANE, (b + 1) * LANE)) for b in range(3)]
        self.don = (slice(first, first + rows), slice(0, LANE))
        self.dos = (slice(first, first + rows), slice(LANE, LANE + hc))


def logits_kernel(
    heads,
    channels,
    npoint,
    pair_hbm,
    sq_ref,
    sk_ref,
    wq_ref,
    wk_ref,
    wqp_ref,
    wkp_ref,
    wb_ref,
    gamma_ref,
    chainb_ref,
    rotq_ref,
    trq_ref,
    rotk_ref,
    trk_ref,
    cq_ref,
    ck_ref,
    km_ref,
    masked_ref,
    stats_ref,
    pack_ref,
    pair_ref,
    tq_ref,
    tk_ref,
    sems,
):
    rows, keys, depth = pair_hbm.shape
    hp = heads * npoint
    copies, step = load_pair(pair_hbm, pair_ref, sems)
    place = packing(rows, keys, channels * heads)
    w_logit = math.sqrt(1.0 / 3.0)
    w_point = math.sqrt(2.0 / (9.0 * npoint))
    tq_ref[...] = jnp.zeros_like(tq_ref)
    tq_ref[0:9, 0:rows] = rotq_ref[...]
    tq_ref[9:12, 0:rows] = trq_ref[...]
    tq_ref[12:13, 0:rows] = cq_ref[...].astype(F32)
    tq_ref[13:14, 0:heads] = gamma_ref[...]
    tq_ref[14:15, 0:heads] = chainb_ref[...]
    qcols_all = tq_ref[...].T
    qcols = qcols_all[:rows]
    head_cols = qcols_all[:HP]
    pack_ref[place.qcol] = qcols_all
    tk_ref[...] = jnp.zeros_like(tk_ref)
    tk_ref[0:9, :] = rotk_ref[...]
    tk_ref[9:12, :] = trk_ref[...]
    kcols = tk_ref[...].T
    pack_ref[place.kcol] = kcols

    sq = sq_ref[...]
    sk = sk_ref[...]
    query = nt(sq, wq_ref[...]).astype(BF)
    key = nt(sk, wk_ref[...]).astype(BF)
    pack_ref[place.query] = query.astype(F32)
    pack_ref[place.key] = key.astype(F32)
    gq = rotate_points(nt(sq, wqp_ref[...]), qcols, hp)
    gk = rotate_points(nt(sk, wkp_ref[...]), kcols, hp)
    pack_ref[place.gq] = gq
    pack_ref[place.gk] = gk

    pmask = head_mask(heads, npoint, 3 * LANE)
    cmask = channel_mask(heads, channels)
    gqm = spread(gq, pmask)
    cross = nt(gqm, gk, HIGH)
    sqq = jnp.sum(gqm * gqm, axis=1, keepdims=True)
    sqk = nt(pmask.astype(F32), gk * gk, HIGH)
    qk = nt(spread(query.astype(F32), cmask).astype(BF), key)
    coef = (w_logit * w_point) * head_cols[:, 13:14]
    same = (qcols[:, 12:13] == ck_ref[...].astype(F32)).astype(F32)
    shape = (rows, HP, keys)
    dist = (sqq.reshape(rows, HP, 1) + sqk[None]) - 2.0 * cross.reshape(shape)
    inner = qk.reshape(shape) * (1.0 / math.sqrt(channels)) + head_cols[:, 14:15][
        None
    ] * jnp.broadcast_to(same[:, None, :], shape)
    logit = w_logit * inner - (0.5 * coef)[None] * dist
    masked_ref[...] = logit.reshape(rows * HP, keys)

    wbt = padded_bias(wb_ref).astype(BF)
    for c, copy in enumerate(copies):
        copy.wait()

        def one(i, carry):
            r = pl.multiple_of(i * HP, HP)
            masked_ref[pl.ds(r, HP), :] += w_logit * nt(wbt, pair_ref[i])
            return carry

        lax.fori_loop(c * step, (c + 1) * step, one, 0, unroll=16)

    valid = (km_ref[...] == 1)[None]
    masked = jnp.where(valid, masked_ref[...].reshape(shape), NEG)
    top = jnp.max(masked, axis=2, keepdims=True)
    total = jnp.sum(jnp.where(valid, jnp.exp(masked - top), 0.0), axis=2, keepdims=True)
    masked_ref[...] = masked.reshape(rows * HP, keys)
    packed = to_lanes(top.reshape(rows * HP, 1)) + to_lanes(total.reshape(rows * HP, 1), HP)
    stats_ref[...] = packed.T[: 2 * HP]


def base_kernel(
    heads,
    channels,
    npoint,
    pair_ref,
    pack_ref,
    sk_ref,
    cot_ref,
    wv_ref,
    wvp_ref,
    wout_ref,
    base_ref,
    vals_ref,
    doz_ref,
    lhs_ref,
):
    rows, keys, depth = pair_ref.shape
    hp = heads * npoint
    sk = sk_ref[...]
    cot = cot_ref[...]
    value = nt(sk, wv_ref[...]).astype(BF)
    nos = heads * channels
    place = value_packing(rows, keys, nos)
    kcols = pack_ref[packing(rows, keys, nos).kcol]
    vals_ref[place.gv] = rotate_points(nt(sk, wvp_ref[...]), kcols, hp)
    first = nos + heads * depth
    dos = nt(cot, wout_ref[0:nos, :]).astype(BF)
    vals_ref[place.dos] = dos.astype(F32)
    for b in range(4):
        d = nt(cot, wout_ref[first + b * hp : first + (b + 1) * hp, :]).astype(BF).astype(F32)
        vals_ref[(place.dol + [place.don])[b]] = pad_lanes(d)
    doz = nt(cot, wout_ref[nos:first, :]).astype(BF).astype(F32)
    lhs_ref[...] = jnp.zeros_like(lhs_ref)
    for h in range(heads):
        lhs_ref[pl.ds(h, rows, stride=HP), :] = doz[:, h * depth : (h + 1) * depth]
    doz_ref[...] = lhs_ref[...].astype(BF)
    dosm = spread(dos.astype(F32), channel_mask(heads, channels)).astype(BF)
    base_ref[...] = nt(dosm, value)

    def one(i, carry):
        r = pl.multiple_of(i * HP, HP)
        base_ref[pl.ds(r, HP), :] += nt(doz_ref[pl.ds(r, HP), :], pair_ref[i])
        return carry

    lax.fori_loop(0, rows, one, 0, unroll=16)


def softmax_rows(masked_ref, km_ref, stats_ref):
    rows = stats_ref.shape[1]
    stats = jnp.concatenate(
        [stats_ref[...], jnp.zeros((LANE - stats_ref.shape[0], rows), F32)], axis=0
    ).T
    top = to_col(stats)
    total = to_col(stats, HP)
    valid = km_ref[...] == 1
    return jnp.where(valid, jnp.exp(masked_ref[...] - top), 0.0) / total


def attend_kernel(heads, npoint, masked_ref, base_ref, vals_ref, km_ref, stats_ref, out_ref):
    attn_b = softmax_rows(masked_ref, km_ref, stats_ref).astype(BF)
    ghi, glo = split(vals_ref[0 : masked_ref.shape[1], :])
    opt = nn(attn_b, ghi) + nn(attn_b, glo)
    pmask = head_mask(heads, npoint, 3 * LANE)
    delta = jnp.sum(attn_b.astype(F32) * base_ref[...], axis=1, keepdims=True)
    out_ref[...] = gather_heads(opt, pmask)
    out_ref[:, 0:LANE] += to_lanes(delta, heads * npoint)


def frames_of(heads, npoint, qall, rows):
    pmask = head_mask(heads, npoint, 3 * LANE)
    w_logit = math.sqrt(1.0 / 3.0)
    w_point = math.sqrt(2.0 / (9.0 * npoint))
    coef = (w_logit * w_point) * qall[:HP, 13:14]
    coef_lane = jnp.sum(jnp.where(pmask, coef, 0.0), axis=0, keepdims=True)
    return pmask, qall[:rows], coef_lane


def project(parts, width):
    single = jnp.zeros((parts[0][0].shape[0], width), F32)
    for part, weight in parts:
        phi, plo = split(part)
        single = single + (nn(phi, weight) + nn(plo, weight))
    return single


def component_sums(x):
    n = x.shape[0]
    cols = [jnp.sum(x[:, a * LANE : (a + 1) * LANE], axis=1, keepdims=True) for a in range(3)]
    return jnp.concatenate(cols + [jnp.zeros((n, LANE - 3), F32)], axis=1).T


def query_kernel(
    heads,
    channels,
    npoint,
    place_ref,
    masked_ref,
    km_ref,
    stats_ref,
    base_ref,
    pack_ref,
    vals_ref,
    psum_ref,
    wq_ref,
    wqp_ref,
    qout_ref,
    both_ref,
    dlo_ref,
    alo_ref,
    dglob_ref,
):
    rows, keys = psum_ref.shape[0], base_ref.shape[1]
    place = packing(rows, keys, heads * channels)
    vplace = value_packing(rows, keys, heads * channels)
    hp = heads * npoint
    scale = math.sqrt(1.0 / 3.0) / math.sqrt(channels)
    cmask = channel_mask(heads, channels)
    pmask, qcols, coef_lane = frames_of(heads, npoint, pack_ref[place.qcol], rows)
    inside = iota((1, LANE), 1) < hp

    psum = psum_ref[...]
    delta0 = to_col(psum[:, :LANE], hp)
    opt = [jnp.where(inside, psum[:, a * LANE : (a + 1) * LANE], 0.0) for a in range(3)]
    moved = [jnp.where(inside, opt[a] - qcols[:, 9 + a : 10 + a], 0.0) for a in range(3)]
    oloc = back_rotate(jnp.concatenate(moved, axis=1), qcols)
    onorm = jnp.sqrt(1.0 + (oloc[0] * oloc[0] + oloc[1] * oloc[1] + oloc[2] * oloc[2]))
    ratio = vals_ref[vplace.don] / onorm
    dloc = [vals_ref[vplace.dol[b]] + ratio * oloc[b] for b in range(3)]
    dglob = jnp.concatenate(
        [
            sum(qcols[:, 3 * a + b : 3 * a + b + 1] * dloc[b] for b in range(3))
            for a in range(3)
        ],
        axis=1,
    )
    dglob_ref[...] = dglob
    dghi, dglo = split(spread(dglob, pmask))
    opt_row = jnp.concatenate(opt, axis=1)
    delta = delta0 + jnp.sum(spread(opt_row * dglob, pmask), axis=1, keepdims=True)
    gvhi, gvlo = split(vals_ref[vplace.gv])
    dattn = base_ref[...] + nt(dghi, gvhi) + (nt(dghi, gvlo) + nt(dglo, gvhi))
    attn = softmax_rows(masked_ref, km_ref, stats_ref)
    dlogit = attn * (dattn - delta)
    dhi, dlo = split(dlogit)
    ahi, alo = split(attn)
    both_ref[:, 0:HP, :] = dhi.reshape(rows, HP, keys)
    both_ref[:, HP : 2 * HP, :] = ahi.reshape(rows, HP, keys)
    dlo_ref[...] = dlo
    alo_ref[...] = alo

    gkhi, gklo = split(pack_ref[place.gk])
    dq = scale * gather_heads(nn(dhi, pack_ref[place.key].astype(BF)), cmask)
    qpts = gather_heads(nn(dhi, gkhi) + (nn(dhi, gklo) + nn(dlo, gkhi)), pmask)
    qsum = jnp.sum(dlogit, axis=1, keepdims=True)
    qsum_lane = gather_heads(jnp.broadcast_to(qsum, (rows * HP, 3 * LANE)), pmask)
    dgq = coef_lane * (qpts - pack_ref[place.gq] * qsum_lane)
    mq = back_rotate(dgq, qcols)
    width = qout_ref.shape[1]
    qout_ref[0:rows, :] = project(
        [(dq, wq_ref[...])]
        + [(mq[b][:, :hp], wqp_ref[b * hp : (b + 1) * hp, :]) for b in range(3)],
        width,
    )
    shift = jnp.where(place_ref[0] == 0, dgq - dglob, dgq)
    qout_ref[rows:, :] = jnp.zeros((qout_ref.shape[0] - rows, width), F32)
    qout_ref[rows : rows + 8, 0:rows] = component_sums(shift)[:8, :rows]


def key_kernel(
    heads,
    channels,
    npoint,
    place_ref,
    both_ref,
    dlo_ref,
    alo_ref,
    dglob_ref,
    pack_ref,
    vals_ref,
    wk_ref,
    wv_ref,
    wkp_ref,
    wvp_ref,
    mine_ref,
    other_ref,
):
    rows, keys = dglob_ref.shape[0], dlo_ref.shape[1]
    place = packing(rows, keys, heads * channels)
    vplace = value_packing(rows, keys, heads * channels)
    hp = heads * npoint
    scale = math.sqrt(1.0 / 3.0) / math.sqrt(channels)
    cmask = channel_mask(heads, channels)
    pmask, qcols, coef_lane = frames_of(heads, npoint, pack_ref[place.qcol], rows)
    kcols = pack_ref[place.kcol]
    dhi = both_ref[:, 0:HP, :].reshape(rows * HP, keys)
    ahi = both_ref[:, HP : 2 * HP, :].reshape(rows * HP, keys)
    dlo, alo = dlo_ref[...], alo_ref[...]
    dghi, dglo = split(spread(dglob_ref[...], pmask))
    gqhi, gqlo = split(spread(pack_ref[place.gq], pmask))
    ones = jnp.broadcast_to(pmask[None], (rows, HP, 3 * LANE)).astype(F32).reshape(
        rows * HP, 3 * LANE
    )
    ones = ones.astype(BF)
    qm = spread(pack_ref[place.query], cmask).astype(BF)
    dosm = spread(vals_ref[vplace.dos], cmask).astype(BF)
    dk = scale * tn(dhi, qm)
    dv = tn(ahi, dosm)
    kpts = tn(dhi, gqhi) + (tn(dhi, gqlo) + tn(dlo, gqhi))
    ksum = tn(dhi, ones) + tn(dlo, ones)
    vpts = tn(ahi, dghi) + (tn(ahi, dglo) + tn(alo, dghi))
    dgk = coef_lane * (kpts - pack_ref[place.gk] * ksum)
    mk = back_rotate(dgk, kcols)
    mv = back_rotate(vpts, kcols)
    width = mine_ref.shape[1]
    single = project(
        [(dk, wk_ref[...]), (dv, wv_ref[...])]
        + [(mk[b][:, :hp], wkp_ref[b * hp : (b + 1) * hp, :]) for b in range(3)]
        + [(mv[b][:, :hp], wvp_ref[b * hp : (b + 1) * hp, :]) for b in range(3)],
        width,
    )
    cols = component_sums(dgk + vpts)
    piece = keys // 8
    core, quarter = place_ref[1], place_ref[2]

    def put(ref, half):
        for n in range(4):
            k = half * 4 + n
            r = pl.multiple_of((n ^ quarter) * (piece + 8), 8)
            ref[pl.ds(r, piece), :] = single[k * piece : (k + 1) * piece]
            r = pl.multiple_of((n ^ quarter) * (piece + 8) + piece, 8)
            ref[pl.ds(r, 8), :] = jnp.concatenate(
                [cols[:8, k * piece : (k + 1) * piece], jnp.zeros((8, width - piece), F32)], axis=1
            )

    @pl.when(core == 0)
    def _():
        put(mine_ref, 0)
        put(other_ref, 1)

    @pl.when(core != 0)
    def _():
        put(mine_ref, 1)
        put(other_ref, 0)


def finish_kernel(
    place_ref,
    q0_ref,
    q1_ref,
    mine_ref,
    other_ref,
    gradq_ref,
    shiftq_ref,
    gradk_ref,
    shiftk_ref,
    shift_ref,
):
    rows = gradq_ref.shape[0]
    keys = gradk_ref.shape[0]
    piece = keys // 8
    total = q0_ref[...] + q1_ref[...]
    gradq_ref[...] = total[:rows].astype(BF)
    shiftq_ref[...] = total[rows : rows + 3, :rows]
    core, quarter = place_ref[1], place_ref[2]

    def put(ref, half):
        parts = []
        for n in range(4):
            k = half * 4 + n
            r = pl.multiple_of((n ^ quarter) * (piece + 8), 8)
            gradk_ref[k * piece : (k + 1) * piece, :] = ref[pl.ds(r, piece), :].astype(BF)
            r = pl.multiple_of((n ^ quarter) * (piece + 8) + piece, 8)
            parts.append(ref[pl.ds(r, 8), 0:piece])
        shift_ref[:, half * 4 * piece : (half + 1) * 4 * piece] = jnp.concatenate(parts, axis=1)

    @pl.when(core == 0)
    def _():
        put(mine_ref, 0)
        put(other_ref, 1)

    @pl.when(core != 0)
    def _():
        put(mine_ref, 1)
        put(other_ref, 0)

    shiftk_ref[...] = shift_ref[0:3, :]


def pair_kernel(both_ref, doz_ref, wb_ref, *refs):
    out_ref = refs[-1]
    rows = both_ref.shape[0]
    whi, wlo = split(math.sqrt(1.0 / 3.0) * padded_bias(wb_ref))

    def one(i, carry):
        both = both_ref[i]
        left = jnp.concatenate([both[:HP], both], axis=0)
        doz = doz_ref[pl.ds(pl.multiple_of(i * HP, HP), HP), :]
        right = jnp.concatenate([wlo, whi, doz], axis=0)
        out_ref[i] = tn(left, right).astype(BF)
        return carry

    lax.fori_loop(0, rows, one, 0, unroll=True)


def pair_part(part, parts, both, doz, w_bias, before, params):
    rows, _, keys = both.shape
    depth = doz.shape[1]
    step = rows // parts
    specs = [
        pl.BlockSpec((step, 2 * HP, keys), lambda g: (part, 0, 0)),
        pl.BlockSpec((step * HP, depth), lambda g: (part, 0)),
        pl.BlockSpec(w_bias.shape, lambda g: (0, 0)),
    ]
    operands = [both, doz, w_bias]
    if before is not None:
        specs.append(pl.BlockSpec(memory_space=pl.ANY))
        operands.append(before)
    return pl.pallas_call(
        pair_kernel,
        grid=(1,),
        out_shape=jax.ShapeDtypeStruct((rows, keys, depth), BF),
        in_specs=specs,
        out_specs=pl.BlockSpec((step, keys, depth), lambda g: (part, 0, 0)),
        input_output_aliases={} if before is None else {3: 0},
        compiler_params=params,
        name="pair_grad",
        cost_estimate=pl.CostEstimate(
            flops=2 * step * keys * depth * 3 * HP,
            bytes_accessed=2 * step * keys * depth,
            transcendentals=0,
        ),
    )(*operands)


def permuted(x, axis, flip):
    size = lax.axis_size(axis)
    return lax.ppermute(x, axis, [(i, i ^ flip) for i in range(size)])


def around(x, hops):
    size = lax.axis_size("col")
    ring = size // 2
    moves = []
    for i in range(size):
        z, low = i // 2, i % 2
        source = (z + (hops if z % 2 else -hops)) % ring
        moves.append((source * 2 + low, i))
    return lax.ppermute(x, "col", moves)


def merged(parts):
    top = functools.reduce(jnp.maximum, [p[:HP] for p in parts])
    total = sum(p[HP:] * jnp.exp(p[:HP] - top) for p in parts)
    return jnp.concatenate([top, total], axis=0)


def body(
    pair,
    single_q,
    single_k,
    w_query,
    w_key,
    w_value,
    w_qpoint,
    w_kpoint,
    w_vpoint,
    w_bias,
    w_out,
    head_gamma,
    chain_bias,
    rot_q,
    trans_q,
    rot_k,
    trans_k,
    chain_q,
    chain_k,
    key_mask,
    cotangent,
):
    rows, keys, depth = pair.shape
    heads = w_bias.shape[1]
    channels = w_query.shape[1] // heads
    npoint = w_qpoint.shape[1] // (3 * heads)
    chans = single_q.shape[1]
    hc = heads * channels
    n = rows * HP
    sds = jax.ShapeDtypeStruct
    params = pltpu.CompilerParams(vmem_limit_bytes=LIMIT)
    wide = 3 * LANE
    km = key_mask.reshape(1, keys)
    w_query, w_key, w_value = w_query.T, w_key.T, w_value.T
    w_qpoint, w_kpoint, w_vpoint = w_qpoint.T, w_kpoint.T, w_vpoint.T
    w_bias = w_bias.T
    frames = [head_gamma.reshape(1, heads), chain_bias.reshape(1, heads)]
    frames += [rot_q, trans_q, rot_k, trans_k, chain_q.reshape(1, rows), chain_k.reshape(1, keys)]
    inputs = [single_q, single_k, w_query, w_key, w_qpoint, w_kpoint, w_bias, *frames, km]
    masked, stats, pack = call(
        functools.partial(logits_kernel, heads, channels, npoint),
        "logits",
        [
            sds((n, keys), F32),
            sds((2 * HP, rows), F32),
            sds(packing(rows, keys, hc).shape, F32),
        ],
        [],
        [pair],
        inputs,
        [
            pltpu.VMEM((rows, keys, depth), BF),
            pltpu.VMEM((LANE, LANE), F32),
            pltpu.VMEM((LANE, keys), F32),
            pltpu.SemaphoreType.DMA((1,)),
        ],
        limit=ALONE,
    )

    first = [stats] + [permuted(stats, "col", f) for f in (1, 2, 3)]
    base, vals, doz = call(
        functools.partial(base_kernel, heads, channels, npoint),
        "base",
        [
            sds((n, keys), F32),
            sds(value_packing(rows, keys, hc).shape, F32),
            sds((n, depth), BF),
        ],
        [],
        [],
        [pair, pack, single_k, cotangent, w_value, w_vpoint, w_out],
        [pltpu.VMEM((n, depth), F32)],
        pl.CostEstimate(
            flops=8 * n * keys * wide, bytes_accessed=4 * rows * keys * depth, transcendentals=0
        ),
    )
    stats = merged(first)
    stats = merged([stats] + [around(stats, f) for f in (3, -2, 1)])

    points = call(
        functools.partial(attend_kernel, heads, npoint),
        "attend",
        [sds((rows, wide), F32)],
        [],
        [],
        [masked, base, vals, km, stats],
    )[0]
    points = points + sum(permuted(points, "col", f) for f in (1, 2, 3))
    points = points + sum(around(points, f) for f in (1, -2, 3))

    me = lax.axis_index("row")
    place = jnp.stack([lax.axis_index("col"), me % 2, me // 4]).astype(jnp.int32)
    qpart, both, dlo, alo, dglob = call(
        functools.partial(query_kernel, heads, channels, npoint),
        "query_grads",
        [
            sds((rows + 8, chans), F32),
            sds((rows, 2 * HP, keys), BF),
            sds((n, keys), BF),
            sds((n, keys), BF),
            sds((rows, wide), F32),
        ],
        [place],
        [],
        [masked, km, stats, base, pack, vals, points, w_query, w_qpoint],
    )

    moved = permuted(qpart, "col", 1)
    half = sds((keys // 2 + 32, chans), F32)
    mine, other = call(
        functools.partial(key_kernel, heads, channels, npoint),
        "key_grads",
        [half, half],
        [place],
        [],
        [both, dlo, alo, dglob, pack, vals, w_key, w_value, w_kpoint, w_vpoint],
        [],
        pl.CostEstimate(
            flops=2 * n * keys * 12 * wide, bytes_accessed=4 * n * keys, transcendentals=0
        ),
    )
    moved, mine, other = lax.optimization_barrier((moved, mine, other))

    qpart = qpart + moved
    mine = mine + permuted(other, "row", 1)
    mine, both = lax.optimization_barrier((mine, both))
    mine = mine.reshape(4, -1, chans)
    held = mine[0] + sum(permuted(mine[f], "row", 4 * f) for f in (1, 2, 3))
    moved = permuted(qpart, "col", 2)
    pair_grad = pair_part(0, 2, both, doz, w_bias, None, params)
    held, both, pair_grad, moved = lax.optimization_barrier((held, both, pair_grad, moved))
    qpart = qpart + moved
    received = permuted(held, "row", 2)
    moved = around(qpart, 3)
    pair_grad = pair_part(1, 2, both, doz, w_bias, pair_grad, params)
    received, moved, pair_grad = lax.optimization_barrier((received, moved, pair_grad))
    held = held + received
    qpart = qpart + moved
    mine = jnp.concatenate([held] + [permuted(held, "row", 4 * f) for f in (1, 2, 3)], axis=0)
    moved = around(qpart, 1)
    mine, moved = lax.optimization_barrier((mine, moved))
    other = permuted(mine, "row", 1)
    grad_q, shift_q, grad_k, shift_k = call(
        finish_kernel,
        "finish",
        [
            sds((rows, chans), BF),
            sds((3, rows), F32),
            sds((keys, chans), BF),
            sds((3, keys), F32),
        ],
        [place],
        [],
        [qpart, moved, mine, other],
        [pltpu.VMEM((8, keys), F32)],
    )
    return pair_grad, grad_q, shift_q, grad_k, shift_k


def solution(mesh):
    placed = (
        P("row", "col", None),
        P("row", None),
        P("col", None),
        P(),
        P(),
        P(),
        P(),
        P(),
        P(),
        P(),
        P(),
        P(),
        P(),
        P(None, "row"),
        P(None, "row"),
        P(None, "col"),
        P(None, "col"),
        P("row"),
        P("col"),
        P("col"),
        P("row", None),
    )
    return jax.shard_map(
        body,
        mesh=mesh,
        in_specs=placed,
        out_specs=(
            P("row", "col", None),
            P("row", None),
            P(None, "row"),
            P("col", None),
            P(None, "col"),
        ),
        check_vma=False,
    )
```

```python
import functools
import math

import jax
import jax.numpy as jnp
from jax import lax
from jax.experimental import pallas as pl
from jax.experimental.pallas import tpu as pltpu
from jax.sharding import PartitionSpec as P

HIGH = lax.Precision.HIGHEST
F32 = jnp.float32
BF = jnp.bfloat16
HP = 16
LANE = 128
NEG = -1e30
LIMIT = 24 * 1024 * 1024
ALONE = 56 * 1024 * 1024


VMEM = pl.BlockSpec(memory_space=pltpu.VMEM)
SMEM = pl.BlockSpec(memory_space=pltpu.SMEM)
ANY = pl.BlockSpec(memory_space=pl.ANY)


def call(kernel, name, outs, smem, hbm, vmem, scratch=(), cost=None, limit=LIMIT):
    return pl.pallas_call(
        kernel,
        out_shape=outs,
        in_specs=[SMEM] * len(smem) + [ANY] * len(hbm) + [VMEM] * len(vmem),
        out_specs=[VMEM] * len(outs),
        scratch_shapes=list(scratch),
        compiler_params=pltpu.CompilerParams(vmem_limit_bytes=limit),
        name=name,
        cost_estimate=cost,
    )(*smem, *hbm, *vmem)


def nn(a, b, precision=None):
    return lax.dot_general(
        a, b, (((1,), (0,)), ((), ())), preferred_element_type=F32, precision=precision
    )


def nt(a, b, precision=None):
    return lax.dot_general(
        a, b, (((1,), (1,)), ((), ())), preferred_element_type=F32, precision=precision
    )


def tn(a, b, precision=None):
    return lax.dot_general(
        a, b, (((0,), (0,)), ((), ())), preferred_element_type=F32, precision=precision
    )


def split(x):
    hi = x.astype(BF)
    return hi, (x - hi.astype(F32)).astype(BF)


def iota(shape, axis):
    return lax.broadcasted_iota(jnp.int32, shape, axis)


def head_mask(heads, npoint, width):
    lane = iota((HP, width), 1) % LANE
    row = iota((HP, width), 0)
    return (lane // npoint == row) & (lane < heads * npoint)


def channel_mask(heads, channels):
    lane = iota((HP, heads * channels), 1)
    return lane // channels == iota((HP, heads * channels), 0)


def spread(x, mask):
    n, w = x.shape
    wide = jnp.broadcast_to(x[:, None, :], (n, HP, w))
    return jnp.where(mask[None], wide, jnp.zeros((), x.dtype)).reshape(n * HP, w)


def gather_heads(x, mask):
    w = x.shape[1]
    full = jnp.where(mask[None], x.reshape(-1, HP, w), 0.0)
    return jnp.sum(full, axis=1)


def to_lanes(col, offset=0):
    n = col.shape[0] // HP
    mask = iota((HP, LANE), 1) == iota((HP, LANE), 0) + offset
    wide = jnp.broadcast_to(col, (n * HP, LANE)).reshape(n, HP, LANE)
    return jnp.sum(jnp.where(mask[None], wide, 0.0), axis=1)


def to_col(x, offset=0):
    n = x.shape[0]
    mask = iota((HP, LANE), 1) == iota((HP, LANE), 0) + offset
    wide = jnp.broadcast_to(x[:, None, :], (n, HP, LANE))
    return jnp.sum(jnp.where(mask[None], wide, 0.0), axis=2, keepdims=True).reshape(n * HP, 1)


def pad_lanes(x, width=LANE):
    n, w = x.shape
    if w == width:
        return x
    return jnp.concatenate([x, jnp.zeros((n, width - w), x.dtype)], axis=1)


def rotate_points(local, cols, hp):
    parts = [local[:, b * hp : (b + 1) * hp] for b in range(3)]
    out = []
    for a in range(3):
        g = cols[:, 9 + a : 10 + a]
        g = g + sum(cols[:, 3 * a + b : 3 * a + b + 1] * parts[b] for b in range(3))
        out.append(pad_lanes(g))
    return jnp.concatenate(out, axis=1)


def back_rotate(x, cols):
    parts = [x[:, a * LANE : (a + 1) * LANE] for a in range(3)]
    return [sum(cols[:, 3 * a + b : 3 * a + b + 1] * parts[a] for a in range(3)) for b in range(3)]


def load_pair(pair_hbm, pair_ref, sems):
    nchunk = sems.shape[0]
    step = pair_hbm.shape[0] // nchunk
    copies = [
        pltpu.make_async_copy(
            pair_hbm.at[pl.ds(c * step, step)], pair_ref.at[pl.ds(c * step, step)], sems.at[c]
        )
        for c in range(nchunk)
    ]
    for copy in copies:
        copy.start()
    return copies, step


def padded_bias(wb_ref):
    heads, depth = wb_ref.shape
    return jnp.concatenate([wb_ref[...].astype(F32), jnp.zeros((HP - heads, depth), F32)], axis=0)


class packing:
    def __init__(self, rows, keys, hc):
        first = keys + rows
        second = first + LANE
        self.shape = (second + keys, 3 * LANE)
        self.gk = (slice(0, keys), slice(0, 3 * LANE))
        self.gq = (slice(keys, first), slice(0, 3 * LANE))
        self.qcol = (slice(first, second), slice(0, LANE))
        self.query = (slice(first, first + rows), slice(LANE, LANE + hc))
        self.key = (slice(second, second + keys), slice(0, hc))
        self.kcol = (slice(second, second + keys), slice(2 * LANE, 3 * LANE))


class value_packing:
    def __init__(self, rows, keys, hc):
        first = keys + rows
        self.shape = (first + rows, 3 * LANE)
        self.gv = (slice(0, keys), slice(0, 3 * LANE))
        self.dol = [(slice(keys, first), slice(b * LANE, (b + 1) * LANE)) for b in range(3)]
        self.don = (slice(first, first + rows), slice(0, LANE))
        self.dos = (slice(first, first + rows), slice(LANE, LANE + hc))


def logits_kernel(
    heads,
    channels,
    npoint,
    pair_hbm,
    sq_ref,
    sk_ref,
    wq_ref,
    wk_ref,
    wqp_ref,
    wkp_ref,
    wb_ref,
    gamma_ref,
    chainb_ref,
    rotq_ref,
    trq_ref,
    rotk_ref,
    trk_ref,
    cq_ref,
    ck_ref,
    km_ref,
    masked_ref,
    stats_ref,
    pack_ref,
    pair_ref,
    tq_ref,
    tk_ref,
    sems,
):
    rows, keys, depth = pair_hbm.shape
    hp = heads * npoint
    copies, step = load_pair(pair_hbm, pair_ref, sems)
    place = packing(rows, keys, channels * heads)
    w_logit = math.sqrt(1.0 / 3.0)
    w_point = math.sqrt(2.0 / (9.0 * npoint))
    tq_ref[...] = jnp.zeros_like(tq_ref)
    tq_ref[0:9, 0:rows] = rotq_ref[...]
    tq_ref[9:12, 0:rows] = trq_ref[...]
    tq_ref[12:13, 0:rows] = cq_ref[...].astype(F32)
    tq_ref[13:14, 0:heads] = gamma_ref[...]
    tq_ref[14:15, 0:heads] = chainb_ref[...]
    qcols_all = tq_ref[...].T
    qcols = qcols_all[:rows]
    head_cols = qcols_all[:HP]
    pack_ref[place.qcol] = qcols_all
    tk_ref[...] = jnp.zeros_like(tk_ref)
    tk_ref[0:9, :] = rotk_ref[...]
    tk_ref[9:12, :] = trk_ref[...]
    kcols = tk_ref[...].T
    pack_ref[place.kcol] = kcols

    sq = sq_ref[...]
    sk = sk_ref[...]
    query = nt(sq, wq_ref[...]).astype(BF)
    key = nt(sk, wk_ref[...]).astype(BF)
    pack_ref[place.query] = query.astype(F32)
    pack_ref[place.key] = key.astype(F32)
    gq = rotate_points(nt(sq, wqp_ref[...]), qcols, hp)
    gk = rotate_points(nt(sk, wkp_ref[...]), kcols, hp)
    pack_ref[place.gq] = gq
    pack_ref[place.gk] = gk

    pmask = head_mask(heads, npoint, 3 * LANE)
    cmask = channel_mask(heads, channels)
    gqm = spread(gq, pmask)
    cross = nt(gqm, gk, HIGH)
    sqq = jnp.sum(gqm * gqm, axis=1, keepdims=True)
    sqk = nt(pmask.astype(F32), gk * gk, HIGH)
    qk = nt(spread(query.astype(F32), cmask).astype(BF), key)
    coef = (w_logit * w_point) * head_cols[:, 13:14]
    same = (qcols[:, 12:13] == ck_ref[...].astype(F32)).astype(F32)
    shape = (rows, HP, keys)
    dist = (sqq.reshape(rows, HP, 1) + sqk[None]) - 2.0 * cross.reshape(shape)
    inner = qk.reshape(shape) * (1.0 / math.sqrt(channels)) + head_cols[:, 14:15][
        None
    ] * jnp.broadcast_to(same[:, None, :], shape)
    logit = w_logit * inner - (0.5 * coef)[None] * dist
    masked_ref[...] = logit.reshape(rows * HP, keys)

    wbt = padded_bias(wb_ref).astype(BF)
    for c, copy in enumerate(copies):
        copy.wait()

        def one(i, carry):
            r = pl.multiple_of(i * HP, HP)
            masked_ref[pl.ds(r, HP), :] += w_logit * nt(wbt, pair_ref[i])
            return carry

        lax.fori_loop(c * step, (c + 1) * step, one, 0, unroll=16)

    valid = (km_ref[...] == 1)[None]
    masked = jnp.where(valid, masked_ref[...].reshape(shape), NEG)
    top = jnp.max(masked, axis=2, keepdims=True)
    total = jnp.sum(jnp.where(valid, jnp.exp(masked - top), 0.0), axis=2, keepdims=True)
    masked_ref[...] = masked.reshape(rows * HP, keys)
    packed = to_lanes(top.reshape(rows * HP, 1)) + to_lanes(total.reshape(rows * HP, 1), HP)
    stats_ref[...] = packed.T[: 2 * HP]


def base_kernel(
    heads,
    channels,
    npoint,
    pair_ref,
    pack_ref,
    sk_ref,
    cot_ref,
    wv_ref,
    wvp_ref,
    wout_ref,
    base_ref,
    vals_ref,
    doz_ref,
    lhs_ref,
):
    rows, keys, depth = pair_ref.shape
    hp = heads * npoint
    sk = sk_ref[...]
    cot = cot_ref[...]
    value = nt(sk, wv_ref[...]).astype(BF)
    nos = heads * channels
    place = value_packing(rows, keys, nos)
    kcols = pack_ref[packing(rows, keys, nos).kcol]
    vals_ref[place.gv] = rotate_points(nt(sk, wvp_ref[...]), kcols, hp)
    first = nos + heads * depth
    dos = nt(cot, wout_ref[0:nos, :]).astype(BF)
    vals_ref[place.dos] = dos.astype(F32)
    for b in range(4):
        d = nt(cot, wout_ref[first + b * hp : first + (b + 1) * hp, :]).astype(BF).astype(F32)
        vals_ref[(place.dol + [place.don])[b]] = pad_lanes(d)
    doz = nt(cot, wout_ref[nos:first, :]).astype(BF).astype(F32)
    lhs_ref[...] = jnp.zeros_like(lhs_ref)
    for h in range(heads):
        lhs_ref[pl.ds(h, rows, stride=HP), :] = doz[:, h * depth : (h + 1) * depth]
    doz_ref[...] = lhs_ref[...].astype(BF)
    dosm = spread(dos.astype(F32), channel_mask(heads, channels)).astype(BF)
    base_ref[...] = nt(dosm, value)

    def one(i, carry):
        r = pl.multiple_of(i * HP, HP)
        base_ref[pl.ds(r, HP), :] += nt(doz_ref[pl.ds(r, HP), :], pair_ref[i])
        return carry

    lax.fori_loop(0, rows, one, 0, unroll=16)


def folded(x, used):
    n, spare, half = x.shape[0], LANE - used, LANE // 2
    third = x[:, 2 * LANE :]
    second = jnp.concatenate([x[:, LANE : LANE + used], third[:, :spare]], axis=1)
    rest = pad_lanes(third[:, spare:used], half)
    quarter = n // 4
    rest = jnp.concatenate([rest[q * quarter : (q + 1) * quarter] for q in range(4)], axis=1)
    return jnp.concatenate([jnp.concatenate([x[:, :LANE], second], axis=1), rest], axis=0)


def unfolded(y, used):
    quarter = y.shape[0] // 5
    n, spare, half = 4 * quarter, LANE - used, LANE // 2
    rest = jnp.concatenate([y[n:, q * half : (q + 1) * half] for q in range(4)], axis=0)
    second = y[:n, LANE:]
    third = jnp.concatenate([second[:, used:], rest[:, : used - spare]], axis=1)
    return jnp.concatenate([y[:n, :LANE], pad_lanes(second[:, :used]), pad_lanes(third)], axis=1)


def attend_kernel(
    heads,
    npoint,
    masked_ref,
    base_ref,
    vals_ref,
    km_ref,
    stats_ref,
    attn_ref,
    out_ref,
):
    rows = stats_ref.shape[1]
    stats = jnp.concatenate(
        [stats_ref[...], jnp.zeros((LANE - stats_ref.shape[0], rows), F32)], axis=0
    ).T
    top = to_col(stats)
    total = to_col(stats, HP)
    valid = km_ref[...] == 1
    attn = jnp.where(valid, jnp.exp(masked_ref[...] - top), 0.0) / total
    attn_ref[...] = attn
    attn_b = attn.astype(BF)
    attn_f = attn_b.astype(F32)
    ghi, glo = split(vals_ref[0 : masked_ref.shape[1], :])
    opt = nn(attn_b, ghi) + nn(attn_b, glo)
    pmask = head_mask(heads, npoint, 3 * LANE)
    delta = jnp.sum(attn_f * base_ref[...], axis=1, keepdims=True)
    points = gather_heads(opt, pmask)
    stat = pad_lanes(to_lanes(delta, heads * npoint), 3 * LANE)
    out_ref[...] = folded(points + stat, heads * npoint)


def frames_of(heads, npoint, qall, rows):
    pmask = head_mask(heads, npoint, 3 * LANE)
    w_logit = math.sqrt(1.0 / 3.0)
    w_point = math.sqrt(2.0 / (9.0 * npoint))
    coef = (w_logit * w_point) * qall[:HP, 13:14]
    coef_lane = jnp.sum(jnp.where(pmask, coef, 0.0), axis=0, keepdims=True)
    return pmask, qall[:rows], coef_lane


def project(parts, width):
    single = jnp.zeros((parts[0][0].shape[0], width), F32)
    for part, weight in parts:
        phi, plo = split(part)
        single = single + (nn(phi, weight) + nn(plo, weight))
    return single


def component_sums(x):
    n = x.shape[0]
    cols = [jnp.sum(x[:, a * LANE : (a + 1) * LANE], axis=1, keepdims=True) for a in range(3)]
    return jnp.concatenate(cols + [jnp.zeros((n, LANE - 3), F32)], axis=1).T


def query_kernel(
    heads,
    channels,
    npoint,
    place_ref,
    attn_ref,
    base_ref,
    pack_ref,
    vals_ref,
    psum_ref,
    wq_ref,
    wqp_ref,
    qout_ref,
    both_ref,
    dlo_ref,
    alo_ref,
    dglob_ref,
):
    rows, keys = dglob_ref.shape[0], base_ref.shape[1]
    place = packing(rows, keys, heads * channels)
    vplace = value_packing(rows, keys, heads * channels)
    hp = heads * npoint
    scale = math.sqrt(1.0 / 3.0) / math.sqrt(channels)
    cmask = channel_mask(heads, channels)
    pmask, qcols, coef_lane = frames_of(heads, npoint, pack_ref[place.qcol], rows)
    inside = iota((1, LANE), 1) < hp

    psum = unfolded(psum_ref[...], hp)
    delta0 = to_col(psum[:, :LANE], hp)
    opt = [jnp.where(inside, psum[:, a * LANE : (a + 1) * LANE], 0.0) for a in range(3)]
    moved = [jnp.where(inside, opt[a] - qcols[:, 9 + a : 10 + a], 0.0) for a in range(3)]
    oloc = back_rotate(jnp.concatenate(moved, axis=1), qcols)
    onorm = jnp.sqrt(1.0 + (oloc[0] * oloc[0] + oloc[1] * oloc[1] + oloc[2] * oloc[2]))
    ratio = vals_ref[vplace.don] / onorm
    dloc = [vals_ref[vplace.dol[b]] + ratio * oloc[b] for b in range(3)]
    dglob = jnp.concatenate(
        [
            sum(qcols[:, 3 * a + b : 3 * a + b + 1] * dloc[b] for b in range(3))
            for a in range(3)
        ],
        axis=1,
    )
    dglob_ref[...] = dglob
    dghi, dglo = split(spread(dglob, pmask))
    opt_row = jnp.concatenate(opt, axis=1)
    delta = delta0 + jnp.sum(spread(opt_row * dglob, pmask), axis=1, keepdims=True)
    gvhi, gvlo = split(vals_ref[vplace.gv])
    dattn = base_ref[...] + nt(dghi, gvhi) + (nt(dghi, gvlo) + nt(dglo, gvhi))
    attn = attn_ref[...]
    dlogit = attn * (dattn - delta)
    dhi, dlo = split(dlogit)
    ahi, alo = split(attn)
    both_ref[:, 0:HP, :] = dhi.reshape(rows, HP, keys)
    both_ref[:, HP : 2 * HP, :] = ahi.reshape(rows, HP, keys)
    dlo_ref[...] = dlo
    alo_ref[...] = alo

    gkhi, gklo = split(pack_ref[place.gk])
    dq = scale * gather_heads(nn(dhi, pack_ref[place.key].astype(BF)), cmask)
    qpts = gather_heads(nn(dhi, gkhi) + (nn(dhi, gklo) + nn(dlo, gkhi)), pmask)
    qsum = jnp.sum(dlogit, axis=1, keepdims=True)
    qsum_lane = gather_heads(jnp.broadcast_to(qsum, (rows * HP, 3 * LANE)), pmask)
    dgq = coef_lane * (qpts - pack_ref[place.gq] * qsum_lane)
    mq = back_rotate(dgq, qcols)
    width = qout_ref.shape[1]
    qout_ref[0:rows, :] = project(
        [(dq, wq_ref[...])]
        + [(mq[b][:, :hp], wqp_ref[b * hp : (b + 1) * hp, :]) for b in range(3)],
        width,
    )
    shift = jnp.where(place_ref[0] == 0, dgq - dglob, dgq)
    qout_ref[rows:, :] = jnp.zeros((qout_ref.shape[0] - rows, width), F32)
    qout_ref[rows : rows + 8, 0:rows] = component_sums(shift)[:8, :rows]


def key_kernel(
    heads,
    channels,
    npoint,
    place_ref,
    both_ref,
    dlo_ref,
    alo_ref,
    dglob_ref,
    pack_ref,
    vals_ref,
    wk_ref,
    wv_ref,
    wkp_ref,
    wvp_ref,
    mine_ref,
    other_ref,
):
    rows, keys = dglob_ref.shape[0], dlo_ref.shape[1]
    place = packing(rows, keys, heads * channels)
    vplace = value_packing(rows, keys, heads * channels)
    hp = heads * npoint
    scale = math.sqrt(1.0 / 3.0) / math.sqrt(channels)
    cmask = channel_mask(heads, channels)
    pmask, qcols, coef_lane = frames_of(heads, npoint, pack_ref[place.qcol], rows)
    kcols = pack_ref[place.kcol]
    dhi = both_ref[:, 0:HP, :].reshape(rows * HP, keys)
    ahi = both_ref[:, HP : 2 * HP, :].reshape(rows * HP, keys)
    dlo, alo = dlo_ref[...], alo_ref[...]
    dghi, dglo = split(spread(dglob_ref[...], pmask))
    gqhi, gqlo = split(spread(pack_ref[place.gq], pmask))
    ones = jnp.broadcast_to(pmask[None], (rows, HP, 3 * LANE)).astype(F32).reshape(
        rows * HP, 3 * LANE
    )
    ones = ones.astype(BF)
    qm = spread(pack_ref[place.query], cmask).astype(BF)
    dosm = spread(vals_ref[vplace.dos], cmask).astype(BF)
    dk = scale * tn(dhi, qm)
    dv = tn(ahi, dosm)
    kpts = tn(dhi, gqhi) + (tn(dhi, gqlo) + tn(dlo, gqhi))
    ksum = tn(dhi, ones) + tn(dlo, ones)
    vpts = tn(ahi, dghi) + (tn(ahi, dglo) + tn(alo, dghi))
    dgk = coef_lane * (kpts - pack_ref[place.gk] * ksum)
    mk = back_rotate(dgk, kcols)
    mv = back_rotate(vpts, kcols)
    width = mine_ref.shape[1]
    single = project(
        [(dk, wk_ref[...]), (dv, wv_ref[...])]
        + [(mk[b][:, :hp], wkp_ref[b * hp : (b + 1) * hp, :]) for b in range(3)]
        + [(mv[b][:, :hp], wvp_ref[b * hp : (b + 1) * hp, :]) for b in range(3)],
        width,
    )
    cols = component_sums(dgk + vpts)
    piece = keys // 8
    core, quarter = place_ref[1], place_ref[2]

    def put(ref, half):
        for n in range(4):
            k = half * 4 + n
            r = pl.multiple_of((n ^ quarter) * (piece + 8), 8)
            ref[pl.ds(r, piece), :] = single[k * piece : (k + 1) * piece]
            r = pl.multiple_of((n ^ quarter) * (piece + 8) + piece, 8)
            ref[pl.ds(r, 8), :] = jnp.concatenate(
                [cols[:8, k * piece : (k + 1) * piece], jnp.zeros((8, width - piece), F32)], axis=1
            )

    @pl.when(core == 0)
    def _():
        put(mine_ref, 0)
        put(other_ref, 1)

    @pl.when(core != 0)
    def _():
        put(mine_ref, 1)
        put(other_ref, 0)


def finish_kernel(
    place_ref,
    q0_ref,
    q1_ref,
    mine_ref,
    other_ref,
    gradq_ref,
    shiftq_ref,
    gradk_ref,
    shiftk_ref,
    shift_ref,
):
    rows = gradq_ref.shape[0]
    keys = gradk_ref.shape[0]
    piece = keys // 8
    total = q0_ref[...] + q1_ref[...]
    gradq_ref[...] = total[:rows].astype(BF)
    shiftq_ref[...] = total[rows : rows + 3, :rows]
    core, quarter = place_ref[1], place_ref[2]

    def put(ref, half):
        parts = []
        for n in range(4):
            k = half * 4 + n
            r = pl.multiple_of((n ^ quarter) * (piece + 8), 8)
            gradk_ref[k * piece : (k + 1) * piece, :] = ref[pl.ds(r, piece), :].astype(BF)
            r = pl.multiple_of((n ^ quarter) * (piece + 8) + piece, 8)
            parts.append(ref[pl.ds(r, 8), 0:piece])
        shift_ref[:, half * 4 * piece : (half + 1) * 4 * piece] = jnp.concatenate(parts, axis=1)

    @pl.when(core == 0)
    def _():
        put(mine_ref, 0)
        put(other_ref, 1)

    @pl.when(core != 0)
    def _():
        put(mine_ref, 1)
        put(other_ref, 0)

    shiftk_ref[...] = shift_ref[0:3, :]


def pair_kernel(both_ref, doz_ref, wb_ref, *refs):
    out_ref = refs[-1]
    rows = both_ref.shape[0]
    whi, wlo = split(math.sqrt(1.0 / 3.0) * padded_bias(wb_ref))

    def one(i, carry):
        both = both_ref[i]
        left = jnp.concatenate([both[:HP], both], axis=0)
        doz = doz_ref[pl.ds(pl.multiple_of(i * HP, HP), HP), :]
        right = jnp.concatenate([wlo, whi, doz], axis=0)
        out_ref[i] = tn(left, right).astype(BF)
        return carry

    lax.fori_loop(0, rows, one, 0, unroll=True)


def pair_part(part, parts, both, doz, w_bias, before, params):
    rows, _, keys = both.shape
    depth = doz.shape[1]
    step = rows // parts
    specs = [
        pl.BlockSpec((step, 2 * HP, keys), lambda g: (part, 0, 0)),
        pl.BlockSpec((step * HP, depth), lambda g: (part, 0)),
        pl.BlockSpec(w_bias.shape, lambda g: (0, 0)),
    ]
    operands = [both, doz, w_bias]
    if before is not None:
        specs.append(pl.BlockSpec(memory_space=pl.ANY))
        operands.append(before)
    return pl.pallas_call(
        pair_kernel,
        grid=(1,),
        out_shape=jax.ShapeDtypeStruct((rows, keys, depth), BF),
        in_specs=specs,
        out_specs=pl.BlockSpec((step, keys, depth), lambda g: (part, 0, 0)),
        input_output_aliases={} if before is None else {3: 0},
        compiler_params=params,
        name="pair_grad",
        cost_estimate=pl.CostEstimate(
            flops=2 * step * keys * depth * 3 * HP,
            bytes_accessed=2 * step * keys * depth,
            transcendentals=0,
        ),
    )(*operands)


def permuted(x, axis, flip):
    size = lax.axis_size(axis)
    return lax.ppermute(x, axis, [(i, i ^ flip) for i in range(size)])


def around(x, hops):
    size = lax.axis_size("col")
    ring = size // 2
    moves = []
    for i in range(size):
        z, low = i // 2, i % 2
        source = (z + (hops if z % 2 else -hops)) % ring
        moves.append((source * 2 + low, i))
    return lax.ppermute(x, "col", moves)


def merged(parts):
    top = functools.reduce(jnp.maximum, [p[:HP] for p in parts])
    total = sum(p[HP:] * jnp.exp(p[:HP] - top) for p in parts)
    return jnp.concatenate([top, total], axis=0)


def body(
    pair,
    single_q,
    single_k,
    w_query,
    w_key,
    w_value,
    w_qpoint,
    w_kpoint,
    w_vpoint,
    w_bias,
    w_out,
    head_gamma,
    chain_bias,
    rot_q,
    trans_q,
    rot_k,
    trans_k,
    chain_q,
    chain_k,
    key_mask,
    cotangent,
):
    rows, keys, depth = pair.shape
    heads = w_bias.shape[1]
    channels = w_query.shape[1] // heads
    npoint = w_qpoint.shape[1] // (3 * heads)
    chans = single_q.shape[1]
    hc = heads * channels
    n = rows * HP
    sds = jax.ShapeDtypeStruct
    params = pltpu.CompilerParams(vmem_limit_bytes=LIMIT)
    wide = 3 * LANE
    km = key_mask.reshape(1, keys)
    w_query, w_key, w_value = w_query.T, w_key.T, w_value.T
    w_qpoint, w_kpoint, w_vpoint = w_qpoint.T, w_kpoint.T, w_vpoint.T
    w_bias = w_bias.T
    frames = [head_gamma.reshape(1, heads), chain_bias.reshape(1, heads)]
    frames += [rot_q, trans_q, rot_k, trans_k, chain_q.reshape(1, rows), chain_k.reshape(1, keys)]
    inputs = [single_q, single_k, w_query, w_key, w_qpoint, w_kpoint, w_bias, *frames, km]
    masked, stats, pack = call(
        functools.partial(logits_kernel, heads, channels, npoint),
        "logits",
        [
            sds((n, keys), F32),
            sds((2 * HP, rows), F32),
            sds(packing(rows, keys, hc).shape, F32),
        ],
        [],
        [pair],
        inputs,
        [
            pltpu.VMEM((rows, keys, depth), BF),
            pltpu.VMEM((LANE, LANE), F32),
            pltpu.VMEM((LANE, keys), F32),
            pltpu.SemaphoreType.DMA((1,)),
        ],
        limit=ALONE,
    )

    first = [stats] + [permuted(stats, "col", f) for f in (1, 2, 3)]
    base, vals, doz = call(
        functools.partial(base_kernel, heads, channels, npoint),
        "base",
        [
            sds((n, keys), F32),
            sds(value_packing(rows, keys, hc).shape, F32),
            sds((n, depth), BF),
        ],
        [],
        [],
        [pair, pack, single_k, cotangent, w_value, w_vpoint, w_out],
        [pltpu.VMEM((n, depth), F32)],
        pl.CostEstimate(
            flops=8 * n * keys * wide, bytes_accessed=4 * rows * keys * depth, transcendentals=0
        ),
    )
    stats = merged(first)
    stats = merged([stats] + [around(stats, f) for f in (3, -2, 1)])

    attn, points = call(
        functools.partial(attend_kernel, heads, npoint),
        "attend",
        [sds((n, keys), F32), sds((rows + rows // 4, 2 * LANE), F32)],
        [],
        [],
        [masked, base, vals, km, stats],
    )
    points = points + sum(permuted(points, "col", f) for f in (1, 2, 3))
    points = points + sum(around(points, f) for f in (1, -2, 3))

    me = lax.axis_index("row")
    place = jnp.stack([lax.axis_index("col"), me % 2, me // 4]).astype(jnp.int32)
    qpart, both, dlo, alo, dglob = call(
        functools.partial(query_kernel, heads, channels, npoint),
        "query_grads",
        [
            sds((rows + 8, chans), F32),
            sds((rows, 2 * HP, keys), BF),
            sds((n, keys), BF),
            sds((n, keys), BF),
            sds((rows, wide), F32),
        ],
        [place],
        [],
        [attn, base, pack, vals, points, w_query, w_qpoint],
    )

    moved = permuted(qpart, "col", 1)
    half = sds((keys // 2 + 32, chans), F32)
    mine, other = call(
        functools.partial(key_kernel, heads, channels, npoint),
        "key_grads",
        [half, half],
        [place],
        [],
        [both, dlo, alo, dglob, pack, vals, w_key, w_value, w_kpoint, w_vpoint],
        [],
        pl.CostEstimate(
            flops=2 * n * keys * 12 * wide, bytes_accessed=4 * n * keys, transcendentals=0
        ),
    )
    moved, mine, other = lax.optimization_barrier((moved, mine, other))

    qpart = qpart + moved
    mine = mine + permuted(other, "row", 1)
    mine, both = lax.optimization_barrier((mine, both))
    mine = mine.reshape(4, -1, chans)
    held = mine[0] + sum(permuted(mine[f], "row", 4 * f) for f in (1, 2, 3))
    moved = permuted(qpart, "col", 2)
    pair_grad = pair_part(0, 2, both, doz, w_bias, None, params)
    held, both, pair_grad, moved = lax.optimization_barrier((held, both, pair_grad, moved))
    qpart = qpart + moved
    received = permuted(held, "row", 2)
    moved = around(qpart, 1)
    pair_grad = pair_part(1, 2, both, doz, w_bias, pair_grad, params)
    received, moved, pair_grad = lax.optimization_barrier((received, moved, pair_grad))
    held = held + received
    qpart = qpart + moved
    mine = jnp.concatenate([held] + [permuted(held, "row", 4 * f) for f in (1, 2, 3)], axis=0)
    moved = around(qpart, -3)
    mine, moved = lax.optimization_barrier((mine, moved))
    other = permuted(mine, "row", 1)
    grad_q, shift_q, grad_k, shift_k = call(
        finish_kernel,
        "finish",
        [
            sds((rows, chans), BF),
            sds((3, rows), F32),
            sds((keys, chans), BF),
            sds((3, keys), F32),
        ],
        [place],
        [],
        [qpart, moved, mine, other],
        [pltpu.VMEM((8, keys), F32)],
    )
    return pair_grad, grad_q, shift_q, grad_k, shift_k


def solution(mesh):
    placed = (
        P("row", "col", None),
        P("row", None),
        P("col", None),
        P(),
        P(),
        P(),
        P(),
        P(),
        P(),
        P(),
        P(),
        P(),
        P(),
        P(None, "row"),
        P(None, "row"),
        P(None, "col"),
        P(None, "col"),
        P("row"),
        P("col"),
        P("col"),
        P("row", None),
    )
    return jax.shard_map(
        body,
        mesh=mesh,
        in_specs=placed,
        out_specs=(
            P("row", "col", None),
            P("row", None),
            P(None, "row"),
            P("col", None),
            P(None, "col"),
        ),
        check_vma=False,
    )
```
